32 devices in a mesh: section: 2 (over y), dp: 4 (over z), tensor: 4 (over x, core).
Axes of the slice: x: 2, y: 2, z: 4, core: 2. Of those that a mesh axis runs over, the one named last changes fastest.
Arguments:
- frames: bfloat16 [2, 1024, 1024], P(None, 'dp', 'tensor'), may hold values from -6 to 6
- cotangent: bfloat16 [2, 1024, 1024], P(None, 'dp', 'tensor'), may hold values from -6 to 6
- lengths: int32 [2, 4, 2], P(None, 'dp'), may hold values from 0 to 256, as said below
- norm1_gain: float32 [2, 1024], P('section'), may hold values from 0.5 to 1.5
- norm1_bias: float32 [2, 1024], P('section'), may hold values from -1.5 to 1.5
- norm2_gain: float32 [2, 1024], P('section'), may hold values from 0.5 to 1.5
- norm2_bias: float32 [2, 1024], P('section'), may hold values from -1.5 to 1.5
- w_qkv: bfloat16 [2, 1024, 3072], P('section', None, 'tensor'), may hold values from -0.1875 to 0.1875
- w_out: bfloat16 [2, 1024, 1024], P('section', 'tensor'), may hold values from -0.75 to 0.75
- w_up: bfloat16 [2, 1024, 4096], P('section', None, 'tensor'), may hold values from -0.1875 to 0.1875
- w_down: bfloat16 [2, 4096, 1024], P('section', 'tensor'), may hold values from -0.09375 to 0.09375
- w_skip: bfloat16 [2, 1024, 1024], P('section', None, 'tensor'), may hold values from -0.125 to 0.125
Outputs:
- boundary: bfloat16 [2, 2, 1024, 1024], P('section', None, 'dp', 'tensor')
- grad_norm1_gain: float32 [2, 1024], P('section')
- grad_norm1_bias: float32 [2, 1024], P('section')
- grad_norm2_gain: float32 [2, 1024], P('section')
- grad_norm2_bias: float32 [2, 1024], P('section')
- grad_qkv_weight: float32 [2, 1024, 3072], P('section', None, 'tensor')
- grad_out_weight: float32 [2, 1024, 1024], P('section', 'tensor')
- grad_up_weight: float32 [2, 1024, 4096], P('section', None, 'tensor')
- grad_down_weight: float32 [2, 4096, 1024], P('section', 'tensor')
- grad_skip_weight: float32 [2, 1024, 1024], P('section', None, 'tensor')
The draws below stay inside these ranges and needn't reach their ends.
Inputs may be any that keep to these rules, and one draw needn't show every extreme that they name: In each block the two lengths add up to at most 256; the first is at least 64; the second may be 0. In every micro-batch one index of dp has a first utterance of exactly 256 frames.
All inputs are finite; a program needn't handle non-finite values.
Results may differ from the reference program's by a relative error of at most 0.038.
Values may be sent and summed in bfloat16 or wider, within the bound.
No kernel may reach another device: no remote copies, remote signals or barrier semaphores. Data moves between devices by JAX's collectives and lax.ppermute only.
A program may use at most 128 MiB of HBM per device.

```python
import jax
import jax.numpy as jnp
from jax import lax

D = 1024
HEADS = 16
FF = 4096
HD = 64
ROWS = 256
MB = 2
UTT = 2
TOKENS = 1024
N_DP = 4


def draw_lengths(key, part):
    key = jax.random.fold_in(key, 7)
    key_first, key_second, key_pick = jax.random.split(key, 3)
    first_len = jax.random.randint(key_first, (MB, N_DP), ROWS // 4, ROWS + 1)
    portion = jax.random.randint(key_second, (MB, N_DP), 0, 1 << 20)
    second_len = portion % (ROWS - first_len + 1)
    chosen = jax.random.randint(key_pick, (MB, 1), 0, N_DP)
    column = jnp.arange(N_DP, dtype=jnp.int32)[None, :]
    first_len = jnp.where(column == chosen, ROWS, first_len)
    second_len = jnp.where(column == chosen, 0, second_len)
    return jnp.stack([first_len, second_len], -1).astype(jnp.int32)


def block_scale(key, dims, cuts, low, largest):
    loudness, own = 1.0, jax.random.fold_in(key, 6)
    for axis_at, shards_of in cuts:
        steps = jnp.exp(jax.random.uniform(jax.random.fold_in(own, axis_at), (shards_of,), jnp.float32, low / len(cuts), largest / len(cuts)))
        loudness = loudness * jnp.repeat(steps, dims[axis_at] // shards_of).reshape([-1 if axis == axis_at else 1 for axis in range(len(dims))])
    return loudness


def normal_values(own_key, extent, deviation, limit, cuts=(), kind=jnp.bfloat16):
    level = block_scale(own_key, extent, cuts, -0.22, 0.18) if cuts else 1.0
    values = jax.random.normal(own_key, extent, jnp.float32) * deviation * level
    return jnp.minimum(jnp.maximum(values, -limit), limit).astype(kind)


def setup_inputs(seed: int = 0) -> dict:
    key_of = jax.random.split(jax.random.key(seed), 13)
    frames = normal_values(key_of[0], (MB, TOKENS, D), 1.0, 6.0, ((1, 4), (2, 4)))
    cotangent = normal_values(key_of[1], (MB, TOKENS, D), 1.0, 6.0, ((1, 4), (2, 4)))
    lengths = draw_lengths(jax.random.fold_in(key_of[12], 71), 0)
    norm1_gain = jnp.clip(1.0 + 0.1 * jax.random.normal(key_of[3], (2, D), jnp.float32), 0.5, 1.5)
    norm1_bias = normal_values(key_of[4], (2, D), 0.3, 1.5, ((0, 2),), jnp.float32)
    norm2_gain = jnp.clip(1.0 + 0.1 * jax.random.normal(key_of[5], (2, D), jnp.float32), 0.5, 1.5)
    norm2_bias = normal_values(key_of[6], (2, D), 0.3, 1.5, ((0, 2),), jnp.float32)
    w_qkv = normal_values(key_of[7], (2, D, 3 * D), D ** -0.5, 0.1875, ((0, 2), (2, 4)))
    w_out = normal_values(key_of[8], (2, D, D), HD ** -0.5, 0.75, ((0, 2), (1, 4)))
    w_up = normal_values(key_of[9], (2, D, FF), D ** -0.5, 0.1875, ((0, 2), (2, 4)))
    w_down = normal_values(key_of[10], (2, FF, D), FF ** -0.5, 0.09375, ((0, 2), (1, 4)))
    w_skip = normal_values(key_of[11], (2, D, D), (2 * D) ** -0.5, 0.125, ((0, 2), (2, 4)))
    return dict(frames=frames, cotangent=cotangent, lengths=lengths, norm1_gain=norm1_gain, norm1_bias=norm1_bias, norm2_gain=norm2_gain, norm2_bias=norm2_bias, w_qkv=w_qkv, w_out=w_out, w_up=w_up, w_down=w_down, w_skip=w_skip)


highest = lax.Precision.HIGHEST
epsilon = 1e-05

@jax.custom_vjp
def low(v):
    return lax.optimization_barrier(v.astype(jnp.bfloat16)).astype(jnp.float32)

@jax.custom_vjp
def low_back(v):
    return v

def low_keep(v):
    return (low(v), None)

def low_pass(kept, grad):
    return (grad,)

def back_keep(v):
    return (v, None)

def back_low(kept, grad):
    return (low(grad),)
low.defvjp(low_keep, low_pass)
low_back.defvjp(back_keep, back_low)

def as_float(array):
    return array.astype(jnp.float32)

def product(left, right):
    return jnp.dot(left, right, precision=highest, preferred_element_type=jnp.float32)

def layer_norm(inputs, gain, bias):
    average = lax.optimization_barrier(jnp.mean(inputs, -1, keepdims=True))
    centred = inputs - average
    variance = lax.optimization_barrier(jnp.mean(centred * centred, -1, keepdims=True))
    return centred * lax.rsqrt(variance + epsilon) * gain + bias

def segments_of(slot_lengths):
    utt_ends = jnp.cumsum(slot_lengths).astype(jnp.int32)
    positions = jnp.arange(ROWS, dtype=jnp.int32)
    return lax.optimization_barrier(jnp.sum((positions[:, None] >= utt_ends[None, :]).astype(jnp.int32), -1)).astype(jnp.int32)

def attention(normed, w_qkv, w_out, segment):
    packed = low_back(low(product(normed, w_qkv))).reshape(ROWS, HEADS, 3, HD)
    queries = packed[:, :, 0]
    keys_all = packed[:, :, 1]
    values = packed[:, :, 2]
    positions = jnp.arange(ROWS, dtype=jnp.int32)
    distance = jnp.abs(positions[:, None] - positions[None, :]).astype(jnp.float32)
    slopes = 2.0 ** (-8.0 * (jnp.arange(HEADS, dtype=jnp.int32) + 1).astype(jnp.float32) / HEADS)
    scores = jnp.einsum('qhd,khd->hqk', queries, keys_all, precision=highest) * HD ** (-0.5)
    scores = low_back(scores - slopes[:, None, None] * distance[None])
    allowed = segment[:, None] == segment[None, :]
    scores = jnp.where(allowed[None], scores, -1e+30)
    top_score = lax.optimization_barrier(jnp.max(scores, -1, keepdims=True))
    exp_scores = jnp.exp(scores - top_score)
    attn_probs = exp_scores / lax.optimization_barrier(jnp.sum(exp_scores, -1, keepdims=True))
    head_mix = jnp.einsum('hqk,khd->qhd', low(attn_probs), values, precision=highest)
    head_mix = low_back(low(head_mix)).reshape(ROWS, HEADS * HD)
    return low_back(product(head_mix, w_out))

def feed_forward(normed, w_up, w_down):
    hidden = low_back(product(normed, w_up))
    activated = low(jax.nn.gelu(hidden, approximate=False))
    return low_back(product(activated, w_down))

def layer_block(inputs, layer_weights, segment):
    gain_one, bias_one, gain_two, bias_two, w_qkv, w_out, w_up, w_down = layer_weights
    attn_in = low(layer_norm(inputs, gain_one, bias_one))
    middle = inputs + attention(attn_in, w_qkv, w_out, segment)
    ffn_in = low(layer_norm(middle, gain_two, bias_two))
    return middle + feed_forward(ffn_in, w_up, w_down)

def layer_pair(inputs, segment, first_weights, second_weights, w_skip):
    encoded = layer_block(inputs, first_weights, segment)
    joined = low_back(product(low(encoded), w_skip[1]) + product(inputs, w_skip[0]))
    return layer_block(joined, second_weights, segment)

def reference(frames, cotangent, lengths, norm1_gain, norm1_bias, norm2_gain, norm2_bias, w_qkv, w_out, w_up, w_down, w_skip):
    params = (as_float(norm1_gain), as_float(norm1_bias), as_float(norm2_gain), as_float(norm2_bias), as_float(w_qkv), as_float(w_out), as_float(w_up), as_float(w_down), as_float(w_skip))
    slots = as_float(frames).reshape(MB * N_DP, ROWS, D)
    slot_segments = jax.vmap(segments_of)(lengths.reshape(MB * N_DP, UTT))

    def forward(slot_frames, weights):
        first_weights = tuple((item[0] for item in weights[:8]))
        second_weights = tuple((item[1] for item in weights[:8]))

        def one_slot(slot_item):
            return layer_pair(slot_item[0], slot_item[1], first_weights, second_weights, weights[8])
        return lax.map(jax.checkpoint(one_slot), (slot_frames, slot_segments))
    outputs, pull_back = jax.vjp(forward, slots, params)
    valid = (slot_segments < UTT).astype(jnp.float32)[..., None]
    seed_grad = as_float(cotangent).reshape(MB * N_DP, ROWS, D) * valid
    grad_frames, grad_params = pull_back(seed_grad)
    boundary = jnp.stack([grad_frames.reshape(MB, N_DP * ROWS, D), outputs.reshape(MB, N_DP * ROWS, D)], 0)
    return (boundary.astype(jnp.bfloat16), grad_params[0], grad_params[1], grad_params[2], grad_params[3], grad_params[4], grad_params[5], grad_params[6], grad_params[7], grad_params[8])
```

```python
import functools

import jax
import jax.numpy as jnp
from jax import lax
from jax.experimental import pallas as pl
from jax.experimental.pallas import tpu as pltpu
from jax.sharding import PartitionSpec as P

HEADS = 16
HD = 64
UTT = 2

epsilon = 1e-05
inv_root_two = 0.7071067811865476
inv_root_two_pi = 0.3989422804014327
MIB = 1 << 20
GROUP = 4


def core_swap(value):
    count = lax.axis_size("tensor")
    return lax.ppermute(value, "tensor", [(at, at ^ 1) for at in range(count)])


def x_swap(value):
    count = lax.axis_size("tensor")
    return lax.ppermute(value, "tensor", [(at, at ^ 2) for at in range(count)])


def section_swap(value):
    return lax.ppermute(value, "section", [(0, 1), (1, 0)])


def dp_swap(value, bit):
    count = lax.axis_size("dp")
    return lax.ppermute(value, "dp", [(at, at ^ bit) for at in range(count)])


def dp_shift(value, steps):
    count = lax.axis_size("dp")
    return lax.ppermute(value, "dp", [(at, (at + steps) % count) for at in range(count)])


def sum_half(theirs, mine):
    near = (mine.astype(jnp.float32) + core_swap(theirs).astype(jnp.float32)).astype(jnp.bfloat16)
    return near, x_swap(near)


def sum_whole(theirs, mine):
    near, far = sum_half(theirs, mine)
    half = (near.astype(jnp.float32) + far.astype(jnp.float32)).astype(jnp.bfloat16)
    return half, core_swap(half)


def dot(left, right):
    return jnp.dot(left, right, preferred_element_type=jnp.float32)


def dot_nt(left, right):
    return lax.dot_general(
        left, right, (((1,), (1,)), ((), ())), preferred_element_type=jnp.float32
    )


def dot_tn(left, right):
    return lax.dot_general(
        left, right, (((0,), (0,)), ((), ())), preferred_element_type=jnp.float32
    )


def f32(ref):
    return ref[...].astype(jnp.float32)


def both(mine, other):
    return jnp.concatenate([f32(mine), f32(other)], 0)


def norm_stats(inputs):
    average = jnp.mean(inputs, -1, keepdims=True)
    centred = inputs - average
    inverse = lax.rsqrt(jnp.mean(centred * centred, -1, keepdims=True) + epsilon)
    return centred * inverse, inverse


def norm_back(grad_norm, normed, inverse, gain):
    scaled = grad_norm * gain
    return inverse * (
        scaled
        - jnp.mean(scaled, -1, keepdims=True)
        - normed * jnp.mean(scaled * normed, -1, keepdims=True)
    )


def erf(value):
    value = jnp.clip(value, -3.832506856900711, 3.832506856900711)
    square = value * value
    top = 0.00022905065861350646
    for term in (
        0.0034082910107109506,
        0.050955695062380861,
        0.18520832239976145,
        1.128379143519084,
    ):
        top = top * square + term
    below = -1.1791602954361697e-7
    for term in (
        0.000023547966471313185,
        0.0010179625278914885,
        0.014070470171167667,
        0.11098505178285362,
        0.49746925110067538,
        1.0,
    ):
        below = below * square + term
    return value * top / below


def gelu_and_slope(hidden):
    normal_cdf = 0.5 * (1.0 + erf(hidden * inv_root_two))
    normal_pdf = jnp.exp(-0.5 * hidden * hidden) * inv_root_two_pi
    return hidden * normal_cdf, normal_cdf + hidden * normal_pdf


def pair_masks(turn, first_len, second_len, rows):
    def place(axis):
        at = lax.broadcasted_iota(jnp.int32, (rows, rows), axis) + turn
        return jnp.where(at >= rows, at - rows, at)

    def segment(at):
        return (at >= first_len).astype(jnp.int32) + (at >= first_len + second_len).astype(
            jnp.int32
        )

    queries, keys_all = place(0), place(1)
    return (
        segment(queries) == segment(keys_all),
        jnp.abs(queries - keys_all).astype(jnp.float32),
    )


def head_columns(rows, heads, head):
    lane = lax.broadcasted_iota(jnp.int32, (rows, heads * HD), 1)
    return (lane >= head * HD) & (lane < (head + 1) * HD)


def keep(mask, value):
    return jnp.where(mask, value, jnp.zeros_like(value))


def attention_probs(packed, slopes, allowed, distance, head, heads):
    rows, wide = packed.shape[0], heads * HD
    mask = head_columns(rows, heads, head)
    scores = dot_nt(keep(mask, packed[:, :wide]), packed[:, wide : 2 * wide]) * HD ** (-0.5)
    scores = jnp.where(allowed, scores - slopes[head] * distance, -1e30)
    exp_scores = jnp.exp(scores - jnp.max(scores, -1, keepdims=True))
    return (exp_scores / jnp.sum(exp_scores, -1, keepdims=True)).astype(jnp.bfloat16)


def attention_back(packed, grad_mix, probs_of, heads):
    rows, wide = packed.shape[0], heads * HD
    queries, keys_all, values = packed[:, :wide], packed[:, wide : 2 * wide], packed[:, 2 * wide :]
    grads = [jnp.zeros((rows, wide), jnp.float32) for _ in range(3)]
    for head in range(heads):
        mask = head_columns(rows, heads, head)
        probs = probs_of(head)
        grad_here = keep(mask, grad_mix)
        grad_probs = dot_nt(grad_here, values)
        wide_probs = probs.astype(jnp.float32)
        row_delta = jnp.sum(wide_probs * grad_probs, -1, keepdims=True)
        grad_scores = (wide_probs * (grad_probs - row_delta)).astype(jnp.bfloat16)
        grads[0] += dot(grad_scores, keep(mask, keys_all))
        grads[1] += dot_tn(grad_scores, keep(mask, queries))
        grads[2] += dot_tn(probs, grad_here)
    scale = HD ** (-0.5)
    return jnp.concatenate([grads[0] * scale, grads[1] * scale, grads[2]], 1).astype(jnp.bfloat16)


def store_halves(partial_sum, theirs, mine):
    half = mine.shape[0]
    mine[...] = partial_sum[:half].astype(mine.dtype)
    theirs[...] = partial_sum[half:].astype(theirs.dtype)


def attn_fwd_kernel(
    meta, slopes, v_mine, v_other, gain, bias, w_qkv, w_out, a_mine, packed_out, probs_out, theirs, mine
):
    heads, rows, _ = probs_out.shape
    normed, _ = norm_stats(both(v_mine, v_other))
    attn_in = (normed * gain[...] + bias[...]).astype(jnp.bfloat16)
    a_mine[...] = attn_in[: a_mine.shape[0]]
    packed = dot(attn_in, w_qkv[...]).astype(jnp.bfloat16)
    packed_out[...] = packed
    allowed, distance = pair_masks(meta[0] * a_mine.shape[0], meta[1], meta[2], rows)
    head_mix = jnp.zeros((rows, heads * HD), jnp.float32)
    for head in range(heads):
        probs = attention_probs(packed, slopes, allowed, distance, head, heads)
        probs_out[head] = probs
        values = keep(head_columns(rows, heads, head), packed[:, 2 * heads * HD :])
        head_mix += dot(probs, values)
    store_halves(dot(head_mix.astype(jnp.bfloat16), w_out[...]), theirs, mine)


def ffn_fwd_kernel(
    v_mine, v_other, s_mine, s_other, gain, bias, w_up, w_down,
    c_mine, x1_mine, slope_out, theirs, mine, ffn_in, total,
):
    step = pl.program_id(0)

    @pl.when(step == 0)
    def _():
        middle = both(v_mine, v_other) + both(s_mine, s_other)
        x1_mine[...] = middle[: x1_mine.shape[0]]
        normed, _ = norm_stats(middle)
        rounded = (normed * gain[...] + bias[...]).astype(jnp.bfloat16)
        ffn_in[...] = rounded
        c_mine[...] = rounded[: c_mine.shape[0]]
        total[...] = jnp.zeros_like(total)

    activated, act_slope = gelu_and_slope(dot(ffn_in[...], w_up[...]))
    slope_out[...] = act_slope
    total[...] += dot(activated.astype(jnp.bfloat16), w_down[...])

    @pl.when(step == pl.num_programs(0) - 1)
    def _():
        store_halves(total[...], theirs, mine)


def ffn_back_kernel(g_mine, g_other, slope_in, w_down, w_up, theirs, mine, total):
    step = pl.program_id(0)

    @pl.when(step == 0)
    def _():
        total[...] = jnp.zeros_like(total)

    grad = jnp.concatenate([g_mine[...], g_other[...]], 0)
    grad_pre = (dot_nt(grad, w_down[...]) * slope_in[...]).astype(jnp.bfloat16)
    total[...] += dot_nt(grad_pre, w_up[...])

    @pl.when(step == pl.num_programs(0) - 1)
    def _():
        store_halves(total[...], theirs, mine)


def attn_back_kernel(
    g_mine, g_other, v_mine, v_other, s_mine, s_other, t_mine, t_other, gain, w_out, w_qkv, packed, probs,
    ga_mine, x1_grad_mine, norm_grads, theirs, mine,
):
    heads = probs.shape[0]
    half = ga_mine.shape[0]
    normed, inverse = norm_stats(both(v_mine, v_other) + both(s_mine, s_other))
    grad_norm = both(t_mine, t_other)
    grad_mid = both(g_mine, g_other) + norm_back(grad_norm, normed, inverse, gain[...])
    x1_grad_mine[...] = grad_mid[:half]
    norm_grads[0:1] = jnp.sum(grad_norm[:half] * normed[:half], 0, keepdims=True)
    norm_grads[1:2] = jnp.sum(grad_norm[:half], 0, keepdims=True)
    grad_attn = grad_mid.astype(jnp.bfloat16)
    ga_mine[...] = grad_attn[:half]
    grad_mix = dot_nt(grad_attn, w_out[...]).astype(jnp.bfloat16)
    grad_packed = attention_back(packed[...], grad_mix, lambda head: probs[head], heads)
    store_halves(dot_nt(grad_packed, w_qkv[...]), theirs, mine)


def input_back(near, far, v_mine, x1_grad_mine, gain, norm_grads):
    normed, inverse = norm_stats(f32(v_mine))
    grad_norm = f32(near) + f32(far)
    norm_grads[0:1] = jnp.sum(grad_norm * normed, 0, keepdims=True)
    norm_grads[1:2] = jnp.sum(grad_norm, 0, keepdims=True)
    return x1_grad_mine[...] + norm_back(grad_norm, normed, inverse, gain[...])


def skip_back(rows, w_all):
    parts, _, wide = w_all.shape
    out = dot_nt(rows[:, :wide], w_all[0])
    for at in range(1, parts):
        out += dot_nt(rows[:, at * wide : (at + 1) * wide], w_all[at])
    return out


def hop_back_kernel(near, far, v_mine, x1_grad_mine, gain, w_all, joined_grad, h_grad, norm_grads):
    rounded = input_back(near, far, v_mine, x1_grad_mine, gain, norm_grads).astype(jnp.bfloat16)
    joined_grad[...] = rounded
    h_grad[...] = skip_back(rounded, w_all).astype(h_grad.dtype)


def frames_back_kernel(near, far, v_mine, x1_grad_mine, gain, w_all, joined_grad, out, norm_grads):
    grad_in = input_back(near, far, v_mine, x1_grad_mine, gain, norm_grads)
    out[...] = (grad_in + skip_back(joined_grad[...], w_all)).astype(out.dtype)


def skip_kernel(rows, w_all, out):
    wide = w_all.shape[2]
    for at in range(w_all.shape[0]):
        out[:, at * wide : (at + 1) * wide] = dot(rows[...], w_all[at]).astype(out.dtype)


def join_kernel(rows, w_all, skip_part, out):
    wide = w_all.shape[2]
    for at in range(w_all.shape[0]):
        columns = slice(at * wide, (at + 1) * wide)
        product = dot(rows[...], w_all[at]) + skip_part[:, columns].astype(jnp.float32)
        out[:, columns] = product.astype(out.dtype)


def ffn_weights_kernel(ffn_in, grad_out, w_up, w_down, grad_up, grad_down):
    @pl.when(pl.program_id(0) == 0)
    def _():
        grad_up[...] = jnp.zeros_like(grad_up)
        grad_down[...] = jnp.zeros_like(grad_down)

    wide = 256
    for at in range(0, w_up.shape[1], wide):
        units = slice(at, at + wide)
        activated, act_slope = gelu_and_slope(dot(ffn_in[...], w_up[:, units]))
        grad_pre = (dot_nt(grad_out[...], w_down[units]) * act_slope).astype(jnp.bfloat16)
        grad_down[units] += dot_tn(activated.astype(jnp.bfloat16), grad_out[...])
        grad_up[:, units] += dot_tn(ffn_in[...], grad_pre)


def attn_weights_kernel(
    here, lens, slopes, attn_in, grad_attn, w_qkv, w_out, order, grad_qkv, grad_out
):
    block = pl.program_id(0)

    @pl.when(block == 0)
    def _():
        grad_qkv[...] = jnp.zeros_like(grad_qkv)
        grad_out[...] = jnp.zeros_like(grad_out)

    heads = w_out.shape[0] // HD
    rows = attn_in.shape[0]
    per_index = here[1]
    group = here[2]
    away = lax.rem(here[0] - block // per_index + group, group)
    at = (away * per_index + lax.rem(block, per_index)) * UTT
    allowed, distance = pair_masks(0, lens[at], lens[at + 1], rows)
    packed = dot(attn_in[...], w_qkv[...]).astype(jnp.bfloat16)
    grad_mix = dot_nt(grad_attn[...], w_out[...]).astype(jnp.bfloat16)
    kept, head_mix = [], jnp.zeros((rows, heads * HD), jnp.float32)
    for head in range(heads):
        probs = attention_probs(packed, slopes, allowed, distance, head, heads)
        values = keep(head_columns(rows, heads, head), packed[:, 2 * heads * HD :])
        head_mix += dot(probs, values)
        kept.append(probs)
    grad_packed = attention_back(packed, grad_mix, lambda head: kept[head], heads)
    grad_packed = dot(grad_packed, order[...]).astype(jnp.bfloat16)
    grad_qkv[...] += dot_tn(attn_in[...], grad_packed)
    grad_out[...] += dot_tn(head_mix.astype(jnp.bfloat16), grad_attn[...])


def shape(dims, kind=jnp.bfloat16):
    return jax.ShapeDtypeStruct(dims, kind)


WHOLE = pl.BlockSpec(memory_space=pltpu.VMEM)
SCALARS = pl.BlockSpec(memory_space=pltpu.SMEM)


def call(kernel, outs, scalars, arrays, flops):
    moved = sum(item.size * item.dtype.itemsize for item in list(arrays) + list(outs))
    return pl.pallas_call(
        kernel,
        out_shape=list(outs),
        in_specs=[SCALARS] * len(scalars) + [WHOLE] * len(arrays),
        out_specs=[WHOLE] * len(outs),
        compiler_params=pltpu.CompilerParams(vmem_limit_bytes=32 * MIB),
        cost_estimate=pl.CostEstimate(flops=int(flops), bytes_accessed=int(moved), transcendentals=0),
    )(*scalars, *arrays)


def attn_forward(meta, slopes, v_mine, v_other, gain, bias, w_qkv, w_out):
    half, width = v_mine.shape
    rows, wide = 2 * half, w_out.shape[0]
    heads = wide // HD
    return call(
        attn_fwd_kernel,
        [
            shape((half, width)),
            shape((rows, 3 * wide)),
            shape((heads, rows, rows)),
            shape((half, width)),
            shape((half, width)),
        ],
        [meta, slopes],
        [v_mine, v_other, gain, bias, w_qkv, w_out],
        2 * rows * wide * (4 * width + 8 * rows),
    )


def constant(dims):
    return pl.BlockSpec(dims, lambda step: (0,) * len(dims))


def ffn_forward(v_mine, v_other, s_mine, s_other, gain, bias, w_up, w_down):
    half, width = v_mine.shape
    rows, units = 2 * half, w_up.shape[1]
    wide = min(256, units)
    part = constant((half, width))
    row = constant((1, width))
    return pl.pallas_call(
        ffn_fwd_kernel,
        grid=(units // wide,),
        in_specs=[
            part, part, part, part, row, row,
            pl.BlockSpec((width, wide), lambda step: (0, step)),
            pl.BlockSpec((wide, width), lambda step: (step, 0)),
        ],
        out_specs=[part, part, pl.BlockSpec((rows, wide), lambda step: (0, step)), part, part],
        out_shape=[
            shape((half, width)),
            shape((half, width), jnp.float32),
            shape((rows, units), jnp.float32),
            shape((half, width)),
            shape((half, width)),
        ],
        scratch_shapes=[pltpu.VMEM((rows, width), jnp.bfloat16), pltpu.VMEM((rows, width), jnp.float32)],
        compiler_params=pltpu.CompilerParams(vmem_limit_bytes=32 * MIB),
        cost_estimate=pl.CostEstimate(
            flops=4 * rows * width * units, bytes_accessed=4 * width * units + 4 * rows * units, transcendentals=0
        ),
    )(v_mine, v_other, s_mine, s_other, gain, bias, w_up, w_down)


def ffn_backward(g_mine, g_other, slope, w_down, w_up):
    half, width = g_mine.shape
    rows, units = 2 * half, w_up.shape[1]
    wide = min(256, units)
    part = constant((half, width))
    return pl.pallas_call(
        ffn_back_kernel,
        grid=(units // wide,),
        in_specs=[
            part, part,
            pl.BlockSpec((rows, wide), lambda step: (0, step)),
            pl.BlockSpec((wide, width), lambda step: (step, 0)),
            pl.BlockSpec((width, wide), lambda step: (0, step)),
        ],
        out_specs=[part, part],
        out_shape=[shape((half, width)), shape((half, width))],
        scratch_shapes=[pltpu.VMEM((rows, width), jnp.float32)],
        compiler_params=pltpu.CompilerParams(vmem_limit_bytes=32 * MIB),
        cost_estimate=pl.CostEstimate(
            flops=4 * rows * width * units, bytes_accessed=4 * width * units + 4 * rows * units, transcendentals=0
        ),
    )(g_mine, g_other, slope, w_down, w_up)


def attn_backward(g, v, s, t, gain, w_out, w_qkv, packed, probs):
    half, width = g[0].shape
    rows, wide = 2 * half, w_out.shape[0]
    return call(
        attn_back_kernel,
        [
            shape((half, width)),
            shape((half, width), jnp.float32),
            shape((2, width), jnp.float32),
            shape((half, width)),
            shape((half, width)),
        ],
        [],
        [*g, *v, *s, *t, gain, w_out, w_qkv, packed, probs],
        2 * rows * wide * (4 * width + 16 * rows),
    )


def ffn_weights(ffn_in, grad_out, w_up, w_down, block):
    width, units = w_up.shape
    rows = ffn_in.shape[0]
    piece = pl.BlockSpec((block, width), lambda step: (step, 0))
    return pl.pallas_call(
        ffn_weights_kernel,
        grid=(rows // block,),
        in_specs=[piece, piece, constant((width, units)), constant((units, width))],
        out_specs=[constant((width, units)), constant((units, width))],
        out_shape=[shape((width, units), jnp.float32), shape((units, width), jnp.float32)],
        compiler_params=pltpu.CompilerParams(vmem_limit_bytes=52 * MIB),
        cost_estimate=pl.CostEstimate(
            flops=8 * rows * width * units, bytes_accessed=16 * width * units, transcendentals=0
        ),
    )(ffn_in, grad_out, w_up, w_down)


def attn_weights(here, lens, slopes, attn_in, grad_attn, w_qkv, w_out, order, block):
    wide, width = w_out.shape
    rows = attn_in.shape[0]
    piece = pl.BlockSpec((block, width), lambda step: (step, 0))
    return pl.pallas_call(
        attn_weights_kernel,
        grid=(rows // block,),
        in_specs=[
            SCALARS, SCALARS, SCALARS, piece, piece,
            constant((width, 3 * wide)), constant((wide, width)), constant((3 * wide, 3 * wide)),
        ],
        out_specs=[constant((width, 3 * wide)), constant((wide, width))],
        out_shape=[shape((width, 3 * wide), jnp.float32), shape((wide, width), jnp.float32)],
        compiler_params=pltpu.CompilerParams(vmem_limit_bytes=48 * MIB),
        cost_estimate=pl.CostEstimate(
            flops=2 * rows * wide * (8 * width + 24 * block), bytes_accessed=24 * width * wide, transcendentals=0
        ),
    )(here, lens, slopes, attn_in, grad_attn, w_qkv, w_out, order)


def shards(
    frames,
    cotangent,
    lengths,
    norm1_gain,
    norm1_bias,
    norm2_gain,
    norm2_bias,
    w_qkv,
    w_out,
    w_up,
    w_down,
    w_skip,
):
    first = lax.axis_index("section") == 0
    dp_at = lax.axis_index("dp")
    tensor_at = lax.axis_index("tensor")
    core, chip = tensor_at % 2, tensor_at // 2
    dp_count = lax.axis_size("dp")
    micro, rows, quarter = frames.shape
    half = rows // 2
    w_qkv, w_out, w_up, w_down = w_qkv[0], w_out[0], w_up[0], w_down[0]
    heads = w_qkv.shape[1] // (3 * HD)
    wide = heads * HD

    def halves(whole):
        return (
            lax.dynamic_slice_in_dim(whole, core * half, half, 0),
            lax.dynamic_slice_in_dim(whole, (1 - core) * half, half, 0),
        )

    at = jnp.arange(3 * wide, dtype=jnp.int32)
    source = (at % wide) // HD * (3 * HD) + at // wide * HD + at % HD
    order = (source[:, None] == at[None, :]).astype(jnp.bfloat16)
    w_packed = dot_nt(w_qkv, order).astype(jnp.bfloat16)

    head_ids = tensor_at * heads + jnp.arange(heads, dtype=jnp.int32)
    slopes = 2.0 ** (-8.0 * (head_ids + 1).astype(jnp.float32) / HEADS)
    metas = [
        jnp.concatenate([core[None].astype(jnp.int32), lengths[m, 0]]) for m in range(micro)
    ]

    xs = [halves(lax.all_gather(frames[m], "tensor", axis=1, tiled=True)) for m in range(micro)]
    w_all = lax.all_gather(w_skip[0], "tensor", axis=0, tiled=False)
    whole_cot = lax.all_gather(cotangent, "tensor", axis=2, tiled=True)

    gather_dp = dp_count <= GROUP
    group = dp_count if gather_dp else 1
    lens = [lengths.reshape(-1)]
    for steps in range(1, group):
        lens.append(dp_shift(lens[0], steps))
    lens = jnp.concatenate(lens)
    here = jnp.stack([dp_at % group, jnp.int32(micro), jnp.int32(group)]).astype(jnp.int32)

    def forward(v):
        attn = [
            attn_forward(metas[m], slopes, *v[m], norm1_gain, norm1_bias, w_packed, w_out)
            for m in range(micro)
        ]
        sums = [sum_whole(item[3], item[4]) for item in attn]
        ffn = [
            ffn_forward(*v[m], *sums[m], norm2_gain, norm2_bias, w_up, w_down)
            for m in range(micro)
        ]
        outs = []
        for item in ffn:
            near, far = sum_half(item[3], item[4])
            outs.append((item[1] + near.astype(jnp.float32) + far.astype(jnp.float32)).astype(jnp.bfloat16))
        kept = dict(
            v=v,
            sums=sums,
            packed=[item[1] for item in attn],
            probs=[item[2] for item in attn],
            slope=[item[2] for item in ffn],
            attn_in=[item[0] for item in attn],
            ffn_in=[item[0] for item in ffn],
        )
        return outs, kept

    def backward(g, kept):
        ffn = [ffn_backward(*g[m], kept["slope"][m], w_down, w_up) for m in range(micro)]
        sums = [sum_whole(*item) for item in ffn]
        attn = [
            attn_backward(
                g[m], kept["v"][m], kept["sums"][m], sums[m], norm2_gain, w_out, w_packed,
                kept["packed"][m], kept["probs"][m],
            )
            for m in range(micro)
        ]
        halves_in = [sum_half(item[3], item[4]) for item in attn]
        return attn, halves_in

    skip_parts = [
        section_swap(call(skip_kernel, [shape(v[0].shape)], [], [v[0], w_all], 2 * v[0].size * v[0].shape[1])[0])
        for v in xs
    ]
    outs_a, kept_a = forward(xs)
    h_recv = [section_swap(item) for item in outs_a]
    joined = []
    for m in range(micro):
        mine = call(
            join_kernel, [shape(h_recv[m].shape)], [], [h_recv[m], w_all, skip_parts[m]], 2 * h_recv[m].size * h_recv[m].shape[1]
        )[0]
        joined.append((mine, core_swap(mine)))
    outs_b, kept_b = forward(joined)

    positions = jnp.arange(rows, dtype=jnp.int32)
    g_c = []
    for m in range(micro):
        valid = (positions < jnp.sum(lengths[m, 0]))[:, None]
        g_c.append(halves(jnp.where(valid, whole_cot[m], jnp.zeros_like(whole_cot[m]))))
    attn_c, sums_c = backward(g_c, kept_b)
    half_dims = shape((half, norm1_gain.shape[1]))
    vector = shape((2, norm1_gain.shape[1]), jnp.float32)
    square = 2 * half * norm1_gain.shape[1] ** 2
    hop = [
        call(
            hop_back_kernel, [half_dims, half_dims, vector], [],
            [*sums_c[m], kept_b["v"][m][0], attn_c[m][1], norm1_gain, w_all], square,
        )
        for m in range(micro)
    ]
    g_d = []
    for m in range(micro):
        mine = section_swap(hop[m][1])
        g_d.append((mine, core_swap(mine)))
    joined_recv = [section_swap(item[0]) for item in hop]
    attn_d, sums_d = backward(g_d, kept_a)
    last = [
        call(
            frames_back_kernel, [half_dims, vector], [],
            [*sums_d[m], kept_a["v"][m][0], attn_d[m][1], norm1_gain, w_all, joined_recv[m]], square,
        )
        for m in range(micro)
    ]

    def choose(early, late):
        return jnp.where(first, early, late)

    def all_rows(early, late):
        mine = jnp.where(
            chip == 0, choose(early[0], late[0]), choose(early[1], late[1])
        )
        if gather_dp:
            return lax.all_gather(mine, ("dp", "tensor"), axis=0, tiled=True)
        return lax.all_gather(mine, "tensor", axis=0, tiled=True)

    attn_in = all_rows(kept_a["attn_in"], kept_b["attn_in"])
    ffn_in = all_rows(kept_a["ffn_in"], kept_b["ffn_in"])
    grad_out = all_rows([item[0] for item in g_d], [item[0] for item in g_c])
    grad_attn = all_rows([item[0] for item in attn_d], [item[0] for item in attn_c])
    up_total, down_total = ffn_weights(ffn_in, grad_out, w_up, w_down, micro * rows)
    qkv_total, out_total = attn_weights(
        here, lens, slopes, attn_in, grad_attn, w_packed, w_out, order, rows
    )

    def over_dp(total):
        return lax.psum(total.astype(jnp.bfloat16), "dp").astype(jnp.float32)

    if not gather_dp:
        up_total, down_total, qkv_total, out_total = (
            over_dp(item) for item in (up_total, down_total, qkv_total, out_total)
        )

    def own_columns(item):
        return lax.dynamic_slice_in_dim(item, tensor_at * quarter, quarter, 1)

    def other_columns(item):
        return lax.dynamic_slice_in_dim(item, (tensor_at ^ 1) * quarter, quarter, 1)

    inputs, grads = [], []
    for m in range(micro):
        mine = choose(xs[m][0], h_recv[m])
        inputs += [mine, core_swap(mine)]
        grad = choose(joined_recv[m], hop[m][0])
        grads += [own_columns(grad), core_swap(other_columns(grad))]
    skip_total = over_dp(dot_tn(jnp.concatenate(inputs, 0), jnp.concatenate(grads, 0)))

    norm_grads = choose(
        jnp.concatenate([sum(item[1] for item in last), sum(item[2] for item in attn_d)], 0),
        jnp.concatenate([sum(item[2] for item in hop), sum(item[2] for item in attn_c)], 0),
    )
    norm_grads += core_swap(norm_grads)
    bit = 1
    while bit < dp_count:
        norm_grads += dp_swap(norm_grads, bit)
        bit *= 2

    pieces = []
    for m in range(micro):
        mine = choose(last[m][0], outs_b[m])
        own, other = own_columns(mine), core_swap(other_columns(mine))
        pieces.append(
            jnp.where(core == 0, jnp.concatenate([own, other], 0), jnp.concatenate([other, own], 0))
        )
    return (
        jnp.stack(pieces, 0)[None],
        norm_grads[0:1],
        norm_grads[1:2],
        norm_grads[2:3],
        norm_grads[3:4],
        qkv_total[None],
        out_total[None],
        up_total[None],
        down_total[None],
        skip_total[None],
    )


def solution(mesh):
    in_specs = (
        P(None, "dp", "tensor"),
        P(None, "dp", "tensor"),
        P(None, "dp", None),
        P("section", None),
        P("section", None),
        P("section", None),
        P("section", None),
        P("section", None, "tensor"),
        P("section", "tensor", None),
        P("section", None, "tensor"),
        P("section", "tensor", None),
        P("section", None, "tensor"),
    )
    out_specs = (
        P("section", None, "dp", "tensor"),
        P("section", None),
        P("section", None),
        P("section", None),
        P("section", None),
        P("section", None, "tensor"),
        P("section", "tensor", None),
        P("section", None, "tensor"),
        P("section", "tensor", None),
        P("section", None, "tensor"),
    )
    return jax.shard_map(shards, mesh=mesh, in_specs=in_specs, out_specs=out_specs, check_vma=False)
```

```python
import functools

import jax
import jax.numpy as jnp
from jax import lax
from jax.experimental import pallas as pl
from jax.experimental.pallas import tpu as pltpu
from jax.sharding import PartitionSpec as P

HEADS = 16
HD = 64
UTT = 2

epsilon = 1e-05
inv_root_two = 0.7071067811865476
inv_root_two_pi = 0.3989422804014327
MIB = 1 << 20
UNITS = 256
GROUP = 4


def core_swap(value):
    count = lax.axis_size("tensor")
    return lax.ppermute(value, "tensor", [(at, at ^ 1) for at in range(count)])


def x_swap(value):
    count = lax.axis_size("tensor")
    return lax.ppermute(value, "tensor", [(at, at ^ 2) for at in range(count)])


def section_swap(value):
    return lax.ppermute(value, "section", [(0, 1), (1, 0)])


def dp_swap(value, bit):
    count = lax.axis_size("dp")
    return lax.ppermute(value, "dp", [(at, at ^ bit) for at in range(count)])


def dp_shift(value, steps):
    count = lax.axis_size("dp")
    return lax.ppermute(value, "dp", [(at, (at + steps) % count) for at in range(count)])


def add_rounded(left, right):
    return (left.astype(jnp.float32) + right.astype(jnp.float32)).astype(jnp.bfloat16)


def near_sum(theirs, mine):
    return add_rounded(mine, core_swap(theirs))


def whole_sum(near):
    half = add_rounded(near, x_swap(near))
    return half, core_swap(half)


def dot(left, right):
    return jnp.dot(left, right, preferred_element_type=jnp.float32)


def dot_nt(left, right):
    return lax.dot_general(
        left, right, (((1,), (1,)), ((), ())), preferred_element_type=jnp.float32
    )


def dot_tn(left, right):
    return lax.dot_general(
        left, right, (((0,), (0,)), ((), ())), preferred_element_type=jnp.float32
    )


def f32(ref):
    return ref[...].astype(jnp.float32)


def both(mine, other):
    return jnp.concatenate([f32(mine), f32(other)], 0)


def norm_stats(inputs):
    average = jnp.mean(inputs, -1, keepdims=True)
    centred = inputs - average
    inverse = lax.rsqrt(jnp.mean(centred * centred, -1, keepdims=True) + epsilon)
    return centred * inverse, inverse


def norm_back(grad_norm, normed, inverse, gain):
    scaled = grad_norm * gain
    return inverse * (
        scaled
        - jnp.mean(scaled, -1, keepdims=True)
        - normed * jnp.mean(scaled * normed, -1, keepdims=True)
    )


def erf(value):
    value = jnp.clip(value, -3.832506856900711, 3.832506856900711)
    square = value * value
    top = 0.00022905065861350646
    for term in (
        0.0034082910107109506,
        0.050955695062380861,
        0.18520832239976145,
        1.128379143519084,
    ):
        top = top * square + term
    below = -1.1791602954361697e-7
    for term in (
        0.000023547966471313185,
        0.0010179625278914885,
        0.014070470171167667,
        0.11098505178285362,
        0.49746925110067538,
        1.0,
    ):
        below = below * square + term
    return value * top / below


def gelu_and_slope(hidden):
    normal_cdf = 0.5 * (1.0 + erf(hidden * inv_root_two))
    normal_pdf = jnp.exp(-0.5 * hidden * hidden) * inv_root_two_pi
    return hidden * normal_cdf, normal_cdf + hidden * normal_pdf


def pair_masks(turn, first_len, second_len, rows):
    def place(axis):
        at = lax.broadcasted_iota(jnp.int32, (rows, rows), axis) + turn
        return jnp.where(at >= rows, at - rows, at)

    def segment(at):
        return (at >= first_len).astype(jnp.int32) + (at >= first_len + second_len).astype(
            jnp.int32
        )

    queries, keys_all = place(0), place(1)
    return (
        segment(queries) == segment(keys_all),
        jnp.abs(queries - keys_all).astype(jnp.float32),
    )


def head_columns(rows, heads, head):
    lane = lax.broadcasted_iota(jnp.int32, (rows, heads * HD), 1)
    return (lane >= head * HD) & (lane < (head + 1) * HD)


def keep(mask, value):
    return jnp.where(mask, value, jnp.zeros_like(value))


def attention_probs(packed, slopes, allowed, distance, head, heads):
    rows, wide = packed.shape[0], heads * HD
    mask = head_columns(rows, heads, head)
    scores = dot_nt(keep(mask, packed[:, :wide]), packed[:, wide : 2 * wide]) * HD ** (-0.5)
    scores = jnp.where(allowed, scores - slopes[head] * distance, -1e30)
    exp_scores = jnp.exp(scores - jnp.max(scores, -1, keepdims=True))
    return (exp_scores / jnp.sum(exp_scores, -1, keepdims=True)).astype(jnp.bfloat16)


def attention_back(packed, grad_mix, probs_of, heads):
    rows, wide = packed.shape[0], heads * HD
    queries, keys_all, values = packed[:, :wide], packed[:, wide : 2 * wide], packed[:, 2 * wide :]
    grads = [jnp.zeros((rows, wide), jnp.float32) for _ in range(3)]
    for head in range(heads):
        mask = head_columns(rows, heads, head)
        probs = probs_of(head)
        grad_here = keep(mask, grad_mix)
        grad_probs = dot_nt(grad_here, values)
        wide_probs = probs.astype(jnp.float32)
        row_delta = jnp.sum(wide_probs * grad_probs, -1, keepdims=True)
        grad_scores = (wide_probs * (grad_probs - row_delta)).astype(jnp.bfloat16)
        grads[0] += dot(grad_scores, keep(mask, keys_all))
        grads[1] += dot_tn(grad_scores, keep(mask, queries))
        grads[2] += dot_tn(probs, grad_here)
    scale = HD ** (-0.5)
    return jnp.concatenate([grads[0] * scale, grads[1] * scale, grads[2]], 1).astype(jnp.bfloat16)


def store_halves(partial_sum, theirs, mine):
    half = mine.shape[0]
    mine[...] = partial_sum[:half].astype(mine.dtype)
    theirs[...] = partial_sum[half:].astype(theirs.dtype)


def flush(copies):
    for copy in copies:
        copy.wait()


def send_out(source, target, sems, at):
    copy = pltpu.make_async_copy(source, target, sems.at[at])
    copy.start()
    return copy


def fetch_columns(source, target, wide, sems, at):
    parts = []
    for start in range(0, target.shape[1], wide):
        columns = slice(start, start + wide)
        parts.append((columns, send_out(source.at[:, columns], target.at[:, columns], sems, at)))
        at += 1
    return parts, at


def fetch_hidden(up_in, down_in, w_up, w_down, sems, at):
    parts = []
    for start in range(0, w_up.shape[1], UNITS):
        units = slice(start, start + UNITS)
        up = send_out(up_in.at[:, units], w_up.at[:, units], sems, at)
        parts.append((units, up, send_out(down_in.at[units], w_down.at[units], sems, at + 1)))
        at += 2
    return parts


def attn_fwd_kernel(
    meta, slopes, v_mine, v_other, gain, bias, w_qkv_in, w_out_in,
    a_out, packed_out, probs_out, v_out, theirs, mine,
    a_mine, packed_here, probs_here, w_qkv, w_out, sems,
):
    heads, rows, _ = probs_here.shape
    parts, first = fetch_columns(w_qkv_in, w_qkv, heads * HD, sems, 3 + heads)
    last = send_out(w_out_in, w_out, sems, first)
    half = a_mine.shape[0]
    copies = [send_out(v_mine, v_out, sems, 2)]
    normed, _ = norm_stats(both(v_mine, v_other))
    attn_in = (normed * gain[...] + bias[...]).astype(jnp.bfloat16)
    a_mine[...] = attn_in[:half]
    copies.append(send_out(a_mine, a_out, sems, 0))
    packed = []
    for columns, part in parts:
        part.wait()
        packed.append(dot(attn_in, w_qkv[:, columns]).astype(jnp.bfloat16))
    packed = jnp.concatenate(packed, 1)
    packed_here[...] = packed
    copies.append(send_out(packed_here, packed_out, sems, 1))
    allowed, distance = pair_masks(meta[0] * half, meta[1], meta[2], rows)
    head_mix = jnp.zeros((rows, heads * HD), jnp.float32)
    for head in range(heads):
        probs = attention_probs(packed, slopes, allowed, distance, head, heads)
        probs_here[head] = probs
        copies.append(send_out(probs_here.at[head], probs_out.at[head], sems, 3 + head))
        values = keep(head_columns(rows, heads, head), packed[:, 2 * heads * HD :])
        head_mix += dot(probs, values)
    last.wait()
    store_halves(dot(head_mix.astype(jnp.bfloat16), w_out[...]), theirs, mine)
    flush(copies)


def ffn_fwd_kernel(
    v_mine, v_other, s_mine, s_other, gain, bias, up_in, down_in,
    c_out, x1_out, slope_out, theirs, mine,
    c_mine, x1_here, slope_here, w_up, w_down, sems,
):
    half, width = c_mine.shape
    blocks = slope_here.shape[0]
    parts = fetch_hidden(up_in, down_in, w_up, w_down, sems, 2 + blocks)
    middle = both(v_mine, v_other) + both(s_mine, s_other)
    x1_here[...] = middle
    copies = [send_out(x1_here, x1_out, sems, 0)]
    normed, _ = norm_stats(middle)
    ffn_in = (normed * gain[...] + bias[...]).astype(jnp.bfloat16)
    c_mine[...] = ffn_in[:half]
    copies.append(send_out(c_mine, c_out, sems, 1))
    total = jnp.zeros((2 * half, width), jnp.float32)
    for at, (units, up, down) in enumerate(parts):
        up.wait()
        activated, act_slope = gelu_and_slope(dot(ffn_in, w_up[:, units]))
        slope_here[at] = act_slope
        copies.append(send_out(slope_here.at[at], slope_out.at[at], sems, 2 + at))
        down.wait()
        total += dot(activated.astype(jnp.bfloat16), w_down[units])
    store_halves(total, theirs, mine)
    flush(copies)


def ffn_back_kernel(
    g_mine, g_other, up_in, down_in, slope_in, g_out, theirs, mine, w_up, w_down, slope, sems
):
    blocks = slope.shape[0]
    parts = fetch_hidden(up_in, down_in, w_up, w_down, sems, 1 + blocks)
    fetches = [send_out(slope_in.at[at], slope.at[at], sems, at) for at in range(blocks)]
    copy = send_out(g_mine, g_out, sems, blocks)
    grad = jnp.concatenate([g_mine[...], g_other[...]], 0)
    total = jnp.zeros(grad.shape, jnp.float32)
    for at, (units, up, down) in enumerate(parts):
        down.wait()
        grad_act = dot_nt(grad, w_down[units])
        fetches[at].wait()
        grad_pre = (grad_act * slope[at]).astype(jnp.bfloat16)
        up.wait()
        total += dot_nt(grad_pre, w_up[:, units])
    store_halves(total, theirs, mine)
    copy.wait()


def attn_back_kernel(
    g_mine, g_other, t_mine, t_other, gain, x1_in, w_out_in, packed_in, probs_in, w_qkv_in,
    ga_out, x1_grad_out, norm_grads, theirs, mine,
    x1, w_out, packed, probs, w_qkv, ga_mine, x1_grad_mine, sems,
):
    needs = ((x1_in, x1), (w_out_in, w_out), (packed_in, packed), (probs_in, probs), (w_qkv_in, w_qkv))
    fetches = [send_out(*pair, sems, at) for at, pair in enumerate(needs)]
    heads = probs.shape[0]
    half = ga_mine.shape[0]
    fetches[0].wait()
    normed, inverse = norm_stats(x1[...])
    grad_norm = both(t_mine, t_other)
    grad_mid = both(g_mine, g_other) + norm_back(grad_norm, normed, inverse, gain[...])
    x1_grad_mine[...] = grad_mid[:half]
    copies = [send_out(x1_grad_mine, x1_grad_out, sems, 5)]
    grad_attn = grad_mid.astype(jnp.bfloat16)
    ga_mine[...] = grad_attn[:half]
    copies.append(send_out(ga_mine, ga_out, sems, 6))
    norm_grads[0:1] = jnp.sum(grad_norm[:half] * normed[:half], 0, keepdims=True)
    norm_grads[1:2] = jnp.sum(grad_norm[:half], 0, keepdims=True)
    fetches[1].wait()
    grad_mix = dot_nt(grad_attn, w_out[...]).astype(jnp.bfloat16)
    fetches[2].wait()
    fetches[3].wait()
    grad_packed = attention_back(packed[...], grad_mix, lambda head: probs[head], heads)
    fetches[4].wait()
    store_halves(dot_nt(grad_packed, w_qkv[...]), theirs, mine)
    flush(copies)


def input_back(near, far, gain, norm_grads, v_mine, x1_grad_mine):
    normed, inverse = norm_stats(f32(v_mine))
    grad_norm = f32(near) + f32(far)
    norm_grads[0:1] = jnp.sum(grad_norm * normed, 0, keepdims=True)
    norm_grads[1:2] = jnp.sum(grad_norm, 0, keepdims=True)
    return x1_grad_mine[...] + norm_back(grad_norm, normed, inverse, gain[...])


def fetch_skip(w_in, w_all, sems):
    return [send_out(w_in.at[at], w_all.at[at], sems, at) for at in range(w_all.shape[0])]


def skip_back(rows, w_all, fetches):
    wide = w_all.shape[2]
    out = 0.0
    for at, fetch in enumerate(fetches):
        fetch.wait()
        out = out + dot_nt(rows[:, at * wide : (at + 1) * wide], w_all[at])
    return out


def hop_back_kernel(
    near, far, gain, v_in, x1_grad_in, w_in, joined_out, h_grad, norm_grads,
    v_mine, x1_grad_mine, w_all, joined_mine, sems,
):
    parts = w_all.shape[0]
    needs = [send_out(v_in, v_mine, sems, parts), send_out(x1_grad_in, x1_grad_mine, sems, parts + 1)]
    fetches = fetch_skip(w_in, w_all, sems)
    flush(needs)
    rounded = input_back(near, far, gain, norm_grads, v_mine, x1_grad_mine).astype(jnp.bfloat16)
    joined_mine[...] = rounded
    copy = send_out(joined_mine, joined_out, sems, parts + 2)
    h_grad[...] = skip_back(rounded, w_all, fetches).astype(h_grad.dtype)
    copy.wait()


def frames_back_kernel(
    near, far, gain, joined_grad, v_in, x1_grad_in, w_in, out, norm_grads,
    v_mine, x1_grad_mine, w_all, sems,
):
    parts = w_all.shape[0]
    needs = [send_out(v_in, v_mine, sems, parts), send_out(x1_grad_in, x1_grad_mine, sems, parts + 1)]
    fetches = fetch_skip(w_in, w_all, sems)
    flush(needs)
    grad_in = input_back(near, far, gain, norm_grads, v_mine, x1_grad_mine)
    out[...] = (grad_in + skip_back(joined_grad[...], w_all, fetches)).astype(out.dtype)


def skip_kernel(*refs):
    *parts, w_in, out, w_all, sems = refs
    wide = w_all.shape[2]
    for at, fetch in enumerate(fetch_skip(w_in, w_all, sems)):
        fetch.wait()
        for m, rows in enumerate(parts):
            out[m, :, at * wide : (at + 1) * wide] = dot(rows[...], w_all[at]).astype(out.dtype)


def join_kernel(m, rows, skip_part, w_in, rows_out, out, w_all, sems):
    wide = w_all.shape[2]
    fetches = fetch_skip(w_in, w_all, sems)
    copy = send_out(rows, rows_out, sems, len(fetches))
    for at, fetch in enumerate(fetches):
        fetch.wait()
        columns = slice(at * wide, (at + 1) * wide)
        product = dot(rows[...], w_all[at]) + skip_part[m, :, columns].astype(jnp.float32)
        out[:, columns] = product.astype(out.dtype)
    copy.wait()


def place_kernel(meta, *refs):
    core, here = meta[0], meta[1]
    micro = refs[0].shape[0]
    blocks, outs = refs[: -2 * micro], refs[-2 * micro :]
    for at in range(micro):
        mine, other = outs[2 * at : 2 * at + 2]
        half, wide = mine.shape[0], blocks[0].shape[2]
        valid = meta[2 + at]
        for flip, block in enumerate(blocks):
            owner = here ^ flip
            columns = pl.ds(pl.multiple_of(owner * wide, wide), wide)
            for start, out in ((core * half, mine), ((1 - core) * half, other)):
                start = pl.multiple_of(start, half)
                row = lax.broadcasted_iota(jnp.int32, (half, wide), 0) + start
                value = block[at, pl.ds(start, half)]
                out[:, columns] = jnp.where(row < valid, value, jnp.zeros_like(value))


def copy_kernel(source, out):
    out[...] = source[...]


def collect_kernel(here, *refs):
    *blocks, out, sems = refs
    flush([send_out(block, out.at[here[0] ^ flip], sems, flip) for flip, block in enumerate(blocks)])


def stack_kernel(*refs):
    *parts, out = refs
    for at, part in enumerate(parts):
        out[at] = part[...]


def ffn_weights_kernel(ffn_in, grad_out, w_up, w_down, grad_up, grad_down):
    @pl.when(pl.program_id(0) == 0)
    def _():
        grad_up[...] = jnp.zeros_like(grad_up)
        grad_down[...] = jnp.zeros_like(grad_down)

    wide = 256
    for at in range(0, w_up.shape[1], wide):
        units = slice(at, at + wide)
        activated, act_slope = gelu_and_slope(dot(ffn_in[...], w_up[:, units]))
        grad_pre = (dot_nt(grad_out[...], w_down[units]) * act_slope).astype(jnp.bfloat16)
        grad_down[units] += dot_tn(activated.astype(jnp.bfloat16), grad_out[...])
        grad_up[:, units] += dot_tn(ffn_in[...], grad_pre)


def attn_weights_kernel(
    here, lens, slopes, attn_in, grad_attn, w_qkv, w_out, order, grad_qkv, grad_out
):
    block = pl.program_id(0)

    @pl.when(block == 0)
    def _():
        grad_qkv[...] = jnp.zeros_like(grad_qkv)
        grad_out[...] = jnp.zeros_like(grad_out)

    heads = w_out.shape[0] // HD
    rows = attn_in.shape[0]
    per_index = here[1]
    group = here[2]
    away = lax.rem(here[0] - block // per_index + group, group)
    at = (away * per_index + lax.rem(block, per_index)) * UTT
    allowed, distance = pair_masks(0, lens[at], lens[at + 1], rows)
    packed = dot(attn_in[...], w_qkv[...]).astype(jnp.bfloat16)
    grad_mix = dot_nt(grad_attn[...], w_out[...]).astype(jnp.bfloat16)
    kept, head_mix = [], jnp.zeros((rows, heads * HD), jnp.float32)
    for head in range(heads):
        probs = attention_probs(packed, slopes, allowed, distance, head, heads)
        values = keep(head_columns(rows, heads, head), packed[:, 2 * heads * HD :])
        head_mix += dot(probs, values)
        kept.append(probs)
    grad_packed = attention_back(packed, grad_mix, lambda head: kept[head], heads)
    grad_packed = dot(grad_packed, order[...]).astype(jnp.bfloat16)
    grad_qkv[...] += dot_tn(attn_in[...], grad_packed)
    grad_out[...] += dot_tn(head_mix.astype(jnp.bfloat16), grad_attn[...])


def shape(dims, kind=jnp.bfloat16):
    return jax.ShapeDtypeStruct(dims, kind)


WHOLE = pl.BlockSpec(memory_space=pltpu.VMEM)
SCALARS = pl.BlockSpec(memory_space=pltpu.SMEM)
FAR = pl.BlockSpec(memory_space=pltpu.HBM)
LATER = pl.BlockSpec(memory_space=pl.ANY)
SMALL = pl.CostEstimate(flops=1, bytes_accessed=1, transcendentals=0)
LARGE = pl.CostEstimate(flops=12_000_000_000, bytes_accessed=40_000_000, transcendentals=0)


def constant(dims):
    return pl.BlockSpec(dims, lambda step: (0,) * len(dims))


def in_hbm(value):
    return pltpu.with_memory_space_constraint(value, pltpu.HBM)


def call(kernel, outs, scalars, arrays, far_in=(), far_outs=(), scratch=(), hold=(), cost=SMALL):
    skip = len(scalars) + len(arrays) + len(far_in)

    def body(*refs):
        kernel(*refs[:skip], *refs[skip + len(hold) :])

    return list(pl.pallas_call(
        body,
        name=getattr(kernel, "func", kernel).__name__,
        out_shape=[*(pltpu.HBM(item.shape, item.dtype) for item in far_outs), *outs],
        in_specs=[SCALARS] * len(scalars) + [WHOLE] * len(arrays) + [FAR] * len(far_in) + [LATER] * len(hold),
        out_specs=[FAR] * len(far_outs) + [WHOLE] * len(outs),
        scratch_shapes=list(scratch),
        compiler_params=pltpu.CompilerParams(vmem_limit_bytes=20 * MIB),
        cost_estimate=cost,
    )(*scalars, *arrays, *map(in_hbm, far_in), *hold))


def vmem(item):
    return pltpu.VMEM(item.shape, item.dtype)


def attn_forward(meta, slopes, v_mine, v_other, gain, bias, w_qkv, w_out, hold):
    half, width = v_mine.shape
    rows, wide = 2 * half, w_out.shape[0]
    heads = wide // HD
    far = [shape((half, width)), shape((rows, 3 * wide)), shape((heads, rows, rows))]
    return call(
        attn_fwd_kernel,
        [shape((half, width)), shape((half, width))],
        [meta, slopes],
        [v_mine, v_other, gain, bias],
        far_in=[w_qkv, w_out],
        far_outs=[*far, shape((half, width))],
        scratch=[*map(vmem, far), vmem(w_qkv), vmem(w_out), pltpu.SemaphoreType.DMA((7 + heads,))],
        hold=hold,
        cost=LARGE,
    )


def ffn_forward(v_mine, v_other, s_mine, s_other, gain, bias, w_up, w_down, hold):
    half, width = v_mine.shape
    rows, units = 2 * half, w_up.shape[1]
    far = [
        shape((half, width)),
        shape((rows, width), jnp.float32),
        shape((units // UNITS, rows, UNITS), jnp.float32),
    ]
    return call(
        ffn_fwd_kernel,
        [shape((half, width)), shape((half, width))],
        [],
        [v_mine, v_other, s_mine, s_other, gain, bias],
        far_in=[w_up, w_down],
        far_outs=far,
        scratch=[
            *map(vmem, far), vmem(w_up), vmem(w_down), pltpu.SemaphoreType.DMA((2 + 3 * (units // UNITS),))
        ],
        hold=hold,
        cost=LARGE,
    )


def ffn_backward(g_mine, g_other, slope, w_down, w_up, hold):
    half, width = g_mine.shape
    return call(
        ffn_back_kernel,
        [shape((half, width)), shape((half, width))],
        [],
        [g_mine, g_other],
        far_in=[w_up, w_down, slope],
        far_outs=[shape((half, width))],
        scratch=[
            vmem(w_up), vmem(w_down), vmem(slope), pltpu.SemaphoreType.DMA((3 * slope.shape[0] + 1,))
        ],
        hold=hold,
        cost=LARGE,
    )


def attn_backward(g, t, gain, w_out, w_qkv, x1, packed, probs, hold):
    half, width = g[0].shape
    rows, wide = 2 * half, w_out.shape[0]
    far = [shape((half, width)), shape((half, width), jnp.float32)]
    return call(
        attn_back_kernel,
        [
            shape((2, width), jnp.float32),
            shape((half, width)),
            shape((half, width)),
        ],
        [],
        [*g, *t, gain],
        far_in=[x1, w_out, packed, probs, w_qkv],
        far_outs=far,
        scratch=[
            *map(vmem, (x1, w_out, packed, probs, w_qkv)), *map(vmem, far), pltpu.SemaphoreType.DMA((7,))
        ],
        hold=hold,
        cost=LARGE,
    )


def ffn_weights(ffn_in, grad_out, w_up, w_down, block):
    width, units = w_up.shape
    rows = ffn_in.shape[0]
    piece = pl.BlockSpec((block, width), lambda step: (step, 0))
    return pl.pallas_call(
        ffn_weights_kernel,
        grid=(rows // block,),
        in_specs=[piece, piece, constant((width, units)), constant((units, width))],
        out_specs=[constant((width, units)), constant((units, width))],
        out_shape=[shape((width, units), jnp.float32), shape((units, width), jnp.float32)],
        compiler_params=pltpu.CompilerParams(vmem_limit_bytes=52 * MIB),
        cost_estimate=SMALL,
    )(*map(in_hbm, (ffn_in, grad_out, w_up, w_down)))


def attn_weights(here, lens, slopes, attn_in, grad_attn, w_qkv, w_out, order, block):
    wide, width = w_out.shape
    rows = attn_in.shape[0]
    piece = pl.BlockSpec((block, width), lambda step: (step, 0))
    return pl.pallas_call(
        attn_weights_kernel,
        grid=(rows // block,),
        in_specs=[
            SCALARS, SCALARS, SCALARS, piece, piece,
            constant((width, 3 * wide)), constant((wide, width)), constant((3 * wide, 3 * wide)),
        ],
        out_specs=[constant((width, 3 * wide)), constant((wide, width))],
        out_shape=[shape((width, 3 * wide), jnp.float32), shape((wide, width), jnp.float32)],
        compiler_params=pltpu.CompilerParams(vmem_limit_bytes=48 * MIB),
        cost_estimate=SMALL,
    )(here, lens, slopes, *map(in_hbm, (attn_in, grad_attn, w_qkv, w_out, order)))


def shards(
    frames,
    cotangent,
    lengths,
    norm1_gain,
    norm1_bias,
    norm2_gain,
    norm2_bias,
    w_qkv,
    w_out,
    w_up,
    w_down,
    w_skip,
):
    first = lax.axis_index("section") == 0
    dp_at = lax.axis_index("dp")
    tensor_at = lax.axis_index("tensor")
    core, chip = tensor_at % 2, tensor_at // 2
    dp_count = lax.axis_size("dp")
    micro, rows, quarter = frames.shape
    half = rows // 2
    w_qkv, w_out, w_up, w_down = w_qkv[0], w_out[0], w_up[0], w_down[0]
    heads = w_qkv.shape[1] // (3 * HD)
    wide = heads * HD

    at = jnp.arange(3 * wide, dtype=jnp.int32)
    source = (at % wide) // HD * (3 * HD) + at // wide * HD + at % HD
    order = (source[:, None] == at[None, :]).astype(jnp.bfloat16)
    w_packed = dot_nt(w_qkv, order).astype(jnp.bfloat16)

    head_ids = tensor_at * heads + jnp.arange(heads, dtype=jnp.int32)
    slopes = 2.0 ** (-8.0 * (head_ids + 1).astype(jnp.float32) / HEADS)
    metas = [
        jnp.concatenate([core[None].astype(jnp.int32), lengths[m, 0]]) for m in range(micro)
    ]

    def place(blocks, own, valid):
        meta = jnp.stack([jnp.int32(item) for item in (core, own, *valid)])
        dims = shape((half, quarter * len(blocks)))
        outs = call(place_kernel, [dims] * (2 * micro), [meta], blocks)
        return [(outs[2 * m], outs[2 * m + 1]) for m in range(micro)]

    over = x_swap(frames)
    w_near = call(copy_kernel, [shape(w_skip.shape[1:])], [], [w_skip[0]], hold=[over])[0]
    w_over = x_swap(w_near)
    w_blocks = [w_near, core_swap(w_near), w_over, core_swap(w_over)]
    w_all = call(
        collect_kernel, [], [tensor_at[None]], w_blocks,
        far_outs=[shape((len(w_blocks), *w_near.shape))],
        scratch=[pltpu.SemaphoreType.DMA((len(w_blocks),))],
    )[0]
    xs = place([frames, core_swap(frames), over, core_swap(over)], tensor_at, [rows] * micro)
    cot_blocks = lax.all_gather(cotangent, "tensor", axis=0, tiled=False)

    gather_dp = dp_count <= GROUP
    group = dp_count if gather_dp else 1
    lens = [lengths.reshape(-1)]
    for steps in range(1, group):
        lens.append(dp_shift(lens[0], steps))
    lens = jnp.concatenate(lens)
    here = jnp.stack([dp_at % group, jnp.int32(micro), jnp.int32(group)]).astype(jnp.int32)

    def choose(early, late):
        return jnp.where(first, early, late)

    def all_rows(early, late):
        mine = jnp.where(chip == 0, choose(early[0], late[0]), choose(early[1], late[1]))
        if gather_dp:
            return lax.all_gather(mine, ("dp", "tensor"), axis=0, tiled=True)
        return lax.all_gather(mine, "tensor", axis=0, tiled=True)

    def forward(v, holds_attn, holds_ffn):
        attn, ffn, near = [], [], []
        for m in range(micro):
            attn.append(
                attn_forward(metas[m], slopes, *v[m], norm1_gain, norm1_bias, w_packed, w_out, near[-1:] + (holds_attn if m else []))
            )
            near.append(near_sum(*attn[m][4:]))
        sums = [whole_sum(item) for item in near]
        near = []
        for m in range(micro):
            ffn.append(
                ffn_forward(
                    *v[m], *sums[m], norm2_gain, norm2_bias, w_up, w_down, near[-1:] + (holds_ffn if m else []) + attn[-1][4:5]
                )
            )
            near.append(near_sum(*ffn[m][3:]))
        kept = dict(
            v=[item[3] for item in attn],
            attn_in=[item[0] for item in attn],
            packed=[item[1] for item in attn],
            probs=[item[2] for item in attn],
            ffn_in=[item[0] for item in ffn],
            x1=[item[1] for item in ffn],
            slope=[item[2] for item in ffn],
        )
        return [(item[1], part) for item, part in zip(ffn, near)], kept

    def finish(x1, near):
        total = x1[:half] + near.astype(jnp.float32) + x_swap(near).astype(jnp.float32)
        return total.astype(jnp.bfloat16)

    def backward(g, kept, holds):
        near, attn, kept_g = [], [], []
        for m in range(micro):
            item = ffn_backward(*g[m], kept["slope"][m], w_down, w_up, near[-1:] + holds)
            kept_g.append(item[0])
            near.append(near_sum(*item[1:]))
        sums = [whole_sum(item) for item in near]
        near = []
        for m in range(micro):
            attn.append(
                attn_backward(
                    g[m], sums[m], norm2_gain, w_out, w_packed,
                    kept["x1"][m], kept["packed"][m], kept["probs"][m], near[-1:] + [item[1]],
                )
            )
            near.append(near_sum(*attn[m][3:]))
        return attn, near, kept_g

    half_dims = shape((half, norm1_gain.shape[1]))
    vector = shape((2, norm1_gain.shape[1]), jnp.float32)
    x1_dims = shape(half_dims.shape, jnp.float32)
    w_scratch = [vmem(w_all), pltpu.SemaphoreType.DMA((w_all.shape[0] + 3,))]

    pair_dims = shape((micro, *half_dims.shape))
    skip_recv = section_swap(
        call(skip_kernel, [pair_dims], [], [v[0] for v in xs], far_in=[w_all], scratch=w_scratch)[0]
    )
    outs_a, kept_a = forward(xs, [w_over], [skip_recv])
    h_recv = [section_swap(finish(*item)) for item in outs_a]
    joined, h_kept = [], []
    for m in range(micro):
        kept, mine = call(
            functools.partial(join_kernel, m), [half_dims], [], [h_recv[m], skip_recv],
            far_in=[w_all], far_outs=[half_dims], scratch=w_scratch,
        )
        h_kept.append(kept)
        joined.append((mine, core_swap(mine)))
    outs_b, kept_b = forward(joined, [], [])
    attn_in = all_rows(kept_a["attn_in"], kept_b["attn_in"])
    ffn_in = all_rows(kept_a["ffn_in"], kept_b["ffn_in"])

    g_c = place(
        [cot_blocks[at] for at in range(cot_blocks.shape[0])],
        0,
        [jnp.sum(lengths[m, 0]) for m in range(micro)],
    )
    attn_c, near_c, kept_g_c = backward(g_c, kept_b, [])
    hop = [
        call(
            hop_back_kernel, [half_dims, vector], [], [near_c[m], x_swap(near_c[m]), norm1_gain],
            far_in=[kept_b["v"][m], attn_c[m][1], w_all], far_outs=[half_dims],
            scratch=[vmem(half_dims), vmem(x1_dims), w_scratch[0], vmem(half_dims), w_scratch[1]],
        )
        for m in range(micro)
    ]
    g_d = []
    for m in range(micro):
        mine = section_swap(hop[m][1])
        g_d.append((mine, core_swap(mine)))
    attn_d, near_d, kept_g_d = backward(g_d, kept_a, [in_hbm(attn_in)])
    joined_own = call(
        stack_kernel, [pair_dims], [], [item[0] for item in hop], hold=[near_d[1]]
    )[0]
    joined_recv = section_swap(joined_own)
    last = [
        call(
            frames_back_kernel, [half_dims, vector], [],
            [near_d[m], x_swap(near_d[m]), norm1_gain, joined_recv[m]],
            far_in=[kept_a["v"][m], attn_d[m][1], w_all],
            scratch=[vmem(half_dims), vmem(x1_dims), *w_scratch], hold=[in_hbm(ffn_in)],
        )
        for m in range(micro)
    ]

    grad_out = all_rows(kept_g_d, kept_g_c)
    grad_attn = all_rows([item[0] for item in attn_d], [item[0] for item in attn_c])
    up_total, down_total = ffn_weights(ffn_in, grad_out, w_up, w_down, micro * rows)
    qkv_total, out_total = attn_weights(
        here, lens, slopes, attn_in, grad_attn, w_packed, w_out, order, rows
    )

    def over_dp(total):
        return lax.psum(total.astype(jnp.bfloat16), "dp").astype(jnp.float32)

    if not gather_dp:
        up_total, down_total, qkv_total, out_total = (
            over_dp(item) for item in (up_total, down_total, qkv_total, out_total)
        )

    def own_columns(item):
        return lax.dynamic_slice_in_dim(item, tensor_at * quarter, quarter, 1)

    def other_columns(item):
        return lax.dynamic_slice_in_dim(item, (tensor_at ^ 1) * quarter, quarter, 1)

    inputs, grads = [], []
    for m in range(micro):
        mine = choose(kept_a["v"][m], h_kept[m])
        inputs += [mine, core_swap(mine)]
        grad = choose(joined_recv[m], joined_own[m])
        grads += [own_columns(grad), core_swap(other_columns(grad))]
    skip_total = over_dp(dot_tn(jnp.concatenate(inputs, 0), jnp.concatenate(grads, 0)))

    norm_grads = choose(
        jnp.concatenate([sum(item[1] for item in last), sum(item[2] for item in attn_d)], 0),
        jnp.concatenate([sum(item[2] for item in hop), sum(item[2] for item in attn_c)], 0),
    )
    norm_grads += core_swap(norm_grads)
    bit = 1
    while bit < dp_count:
        norm_grads += dp_swap(norm_grads, bit)
        bit *= 2

    pieces = []
    for m in range(micro):
        mine = choose(last[m][0], finish(*outs_b[m]))
        own, other = own_columns(mine), core_swap(other_columns(mine))
        pieces.append(
            jnp.where(core == 0, jnp.concatenate([own, other], 0), jnp.concatenate([other, own], 0))
        )
    return (
        jnp.stack(pieces, 0)[None],
        norm_grads[0:1],
        norm_grads[1:2],
        norm_grads[2:3],
        norm_grads[3:4],
        qkv_total[None],
        out_total[None],
        up_total[None],
        down_total[None],
        skip_total[None],
    )


def solution(mesh):
    in_specs = (
        P(None, "dp", "tensor"),
        P(None, "dp", "tensor"),
        P(None, "dp", None),
        P("section", None),
        P("section", None),
        P("section", None),
        P("section", None),
        P("section", None, "tensor"),
        P("section", "tensor", None),
        P("section", None, "tensor"),
        P("section", "tensor", None),
        P("section", None, "tensor"),
    )
    out_specs = (
        P("section", None, "dp", "tensor"),
        P("section", None),
        P("section", None),
        P("section", None),
        P("section", None),
        P("section", None, "tensor"),
        P("section", "tensor", None),
        P("section", None, "tensor"),
        P("section", "tensor", None),
        P("section", None, "tensor"),
    )
    return jax.shard_map(shards, mesh=mesh, in_specs=in_specs, out_specs=out_specs, check_vma=False)
```

```python
import functools

import jax
import jax.numpy as jnp
from jax import lax
from jax.experimental import pallas as pl
from jax.experimental.pallas import tpu as pltpu
from jax.sharding import PartitionSpec as P

HEADS = 16
HD = 64
UTT = 2

epsilon = 1e-05
inv_root_two = 0.7071067811865476
inv_root_two_pi = 0.3989422804014327
MIB = 1 << 20
LANES = 128
LEN_ROWS = 16
GROUP = 4


def core_swap(value):
    count = lax.axis_size("tensor")
    return lax.ppermute(value, "tensor", [(at, at ^ 1) for at in range(count)])


def x_swap(value):
    count = lax.axis_size("tensor")
    return lax.ppermute(value, "tensor", [(at, at ^ 2) for at in range(count)])


def section_swap(value):
    return lax.ppermute(value, "section", [(0, 1), (1, 0)])


def dp_swap(value, bit):
    count = lax.axis_size("dp")
    return lax.ppermute(value, "dp", [(at, at ^ bit) for at in range(count)])


def dp_shift(value, steps):
    count = lax.axis_size("dp")
    return lax.ppermute(value, "dp", [(at, (at + steps) % count) for at in range(count)])


def add_rounded(left, right):
    return (left.astype(jnp.float32) + right.astype(jnp.float32)).astype(jnp.bfloat16)


def near_sum(theirs, mine):
    return add_rounded(mine, core_swap(theirs))


def whole_sum(near):
    half = add_rounded(near, x_swap(near))
    return half, core_swap(half)


def dot(left, right):
    return jnp.dot(left, right, preferred_element_type=jnp.float32)


def dot_nt(left, right):
    return lax.dot_general(
        left, right, (((1,), (1,)), ((), ())), preferred_element_type=jnp.float32
    )


def dot_tn(left, right):
    return lax.dot_general(
        left, right, (((0,), (0,)), ((), ())), preferred_element_type=jnp.float32
    )


def f32(ref):
    return ref[...].astype(jnp.float32)


def both(mine, other):
    return jnp.concatenate([f32(mine), f32(other)], 0)


def norm_stats(inputs):
    average = jnp.mean(inputs, -1, keepdims=True)
    centred = inputs - average
    inverse = lax.rsqrt(jnp.mean(centred * centred, -1, keepdims=True) + epsilon)
    return centred * inverse, inverse


def norm_back(grad_norm, normed, inverse, gain):
    scaled = grad_norm * gain
    return inverse * (
        scaled
        - jnp.mean(scaled, -1, keepdims=True)
        - normed * jnp.mean(scaled * normed, -1, keepdims=True)
    )


def gelu_and_slope(hidden):
    bell = jnp.exp(-0.5 * hidden * hidden)
    at = 1.0 / (1.0 + (0.3275911 * inv_root_two) * jnp.abs(hidden))
    tail = 1.061405429
    for term in (-1.453152027, 1.421413741, -0.284496736, 0.254829592):
        tail = tail * at + term
    tail = (0.5 * at) * tail * bell
    normal_cdf = jnp.where(hidden > 0, 1.0 - tail, tail)
    return hidden * normal_cdf, normal_cdf + hidden * (bell * inv_root_two_pi)


def pair_masks(turn, first_len, second_len, rows):
    def place(axis):
        at = lax.broadcasted_iota(jnp.int32, (rows, rows), axis) + turn
        return jnp.where(at >= rows, at - rows, at).astype(jnp.float32)

    def segment(at):
        return (at >= first_len).astype(jnp.int32) + (at >= first_len + second_len).astype(
            jnp.int32
        )

    queries, keys_all = place(0), place(1)
    return segment(queries) == segment(keys_all), jnp.abs(queries - keys_all)


def swap_sides(tile):
    return jnp.concatenate([tile[:, HD:], tile[:, :HD]], 1)


def side(tile, right):
    lane = lax.broadcasted_iota(jnp.int32, tile.shape, 1)
    return jnp.where((lane >= HD) == bool(right), tile, jnp.zeros_like(tile))


def pair_tiles(packed, pair):
    at = 6 * HD * pair
    return [packed[:, at + 2 * HD * i : at + 2 * HD * (i + 1)] for i in range(3)]


def attention_probs(queries, keys_all, slope, allowed, distance):
    scores = dot_nt(queries * HD ** (-0.5), keys_all)
    scores = jnp.where(allowed, scores - slope * distance, -1e30)
    exp_scores = jnp.exp(scores - jnp.max(scores, -1, keepdims=True))
    return (exp_scores / jnp.sum(exp_scores, -1, keepdims=True)).astype(jnp.bfloat16)


def pair_forward(tiles, slopes, pair, allowed, distance):
    left = attention_probs(
        side(tiles[0], 0), swap_sides(tiles[0]), slopes[2 * pair], allowed, distance
    )
    right = attention_probs(
        side(tiles[1], 1), swap_sides(tiles[2]), slopes[2 * pair + 1], allowed, distance
    )
    mixed = dot(left, side(tiles[1], 0)) + dot(right, side(tiles[2], 1))
    return left, right, mixed.astype(jnp.bfloat16)


def scores_back(probs, grad_mix, values):
    grad_probs = dot_nt(grad_mix, values)
    wide_probs = probs.astype(jnp.float32)
    delta = jnp.sum(wide_probs * grad_probs, -1, keepdims=True)
    return (wide_probs * (grad_probs - delta)).astype(jnp.bfloat16)


def pair_backward(tiles, left, right, grad_mix):
    scale = HD ** (-0.5)
    grad_left, grad_right = side(grad_mix, 0), side(grad_mix, 1)
    back_left = scores_back(left, grad_left, tiles[1])
    back_right = scores_back(right, grad_right, tiles[2])
    turned = [swap_sides(tile) * scale for tile in tiles]
    return [
        item.astype(jnp.bfloat16)
        for item in (
            dot(back_left, side(turned[0], 0)) + dot_tn(back_left, side(turned[0], 1)),
            dot_tn(left, grad_left) + dot(back_right, side(turned[2], 1)),
            dot_tn(back_right, side(turned[1], 0)) + dot_tn(right, grad_right),
        )
    ]


def attention_back(packed, grad_mix, probs_of, heads):
    grads = []
    for pair in range(heads // 2):
        columns = slice(2 * HD * pair, 2 * HD * (pair + 1))
        grads += pair_backward(
            pair_tiles(packed, pair), probs_of(2 * pair), probs_of(2 * pair + 1), grad_mix[:, columns]
        )
    return jnp.concatenate(grads, 1)


def store_halves(partial_sum, theirs, mine):
    half = mine.shape[0]
    mine[...] = partial_sum[:half].astype(mine.dtype)
    theirs[...] = partial_sum[half:].astype(theirs.dtype)


def flush(copies):
    for copy in copies:
        copy.wait()


def send_out(source, target, sems, at):
    copy = pltpu.make_async_copy(source, target, sems.at[at])
    copy.start()
    return copy


def attn_fwd_kernel(
    step, m, meta, lens, slopes, v_mine, v_other, gain, bias, w_qkv_in, w_out_in,
    packed_out, probs_out, v_out, a_out, theirs, mine,
    packed_here, probs_here, w_qkv, w_out, a_turned, sems,
):
    heads, rows, _ = probs_here.shape
    half = v_mine.shape[0]
    first_len, second_len = lens[m, 0, 0], lens[m, 0, 1]
    pairs = [slice(6 * HD * pair, 6 * HD * (pair + 1)) for pair in range(heads // 2)]
    parts = [
        send_out(w_qkv_in.at[:, here], w_qkv.at[:, here], sems, 4 + heads + pair)
        for pair, here in enumerate(pairs)
    ]
    last = send_out(w_out_in, w_out, sems, 3 + heads)
    copies = [send_out(v_mine, v_out.at[m], sems, 2)]
    normed, _ = norm_stats(both(v_mine, v_other))
    attn_in = (normed * gain[...] + bias[...]).astype(jnp.bfloat16)
    width = attn_in.shape[1]
    a_part = a_out.at[:, m * half : (m + 1) * half]
    chosen = meta[1] == step

    @pl.when(chosen)
    def _():
        a_turned[:width] = attn_in[:half].T
        row = lax.broadcasted_iota(jnp.int32, (LEN_ROWS, half), 0)
        own_lens = jnp.where(row == 0, first_len.astype(jnp.float32), second_len.astype(jnp.float32))
        a_turned[width:] = own_lens.astype(a_turned.dtype)
        send_out(a_turned, a_part, sems, 0)

    allowed, distance = pair_masks(
        meta[0] * half, first_len.astype(jnp.float32), second_len.astype(jnp.float32), rows
    )
    mixes = []
    for pair, here in enumerate(pairs):
        parts[pair].wait()
        packed = dot(attn_in, w_qkv[:, here]).astype(jnp.bfloat16)
        packed_here[:, here] = packed
        left, right, mixed = pair_forward(
            pair_tiles(packed, 0), slopes, pair, allowed, distance
        )
        for head, probs in ((2 * pair, left), (2 * pair + 1, right)):
            probs_here[head] = probs
            copies.append(send_out(probs_here.at[head], probs_out.at[head], sems, 3 + head))
        mixes.append(mixed)
    copies.append(send_out(packed_here, packed_out, sems, 1))
    last.wait()
    store_halves(dot(jnp.concatenate(mixes, 1), w_out[...]), theirs, mine)
    flush(copies)

    @pl.when(chosen)
    def _():
        pltpu.make_async_copy(a_turned, a_part, sems.at[0]).wait()


def ffn_fwd_kernel(
    step, m, meta, v_mine, v_other, s_mine, s_other, gain, bias, up_in, down_in,
    x1_out, normed_out, inverse_out, slope_out, c_out, theirs, mine,
    x1_mine, normed_here, inverse_here, slope_here, w_up, w_down, c_turned, sems,
):
    up, down = send_out(up_in, w_up, sems, 5), send_out(down_in, w_down, sems, 6)
    half = v_mine.shape[0]
    middle = both(v_mine, v_other) + both(s_mine, s_other)
    x1_mine[...] = middle[:half]
    normed, inverse = norm_stats(middle)
    normed_here[...] = normed.astype(jnp.bfloat16)
    inverse_here[...] = jnp.broadcast_to(inverse, inverse_here.shape)
    ffn_in = (normed * gain[...] + bias[...]).astype(jnp.bfloat16)
    c_part = c_out.at[:, m * half : (m + 1) * half]
    chosen = meta[1] == step

    @pl.when(chosen)
    def _():
        c_turned[...] = ffn_in[:half].T
        send_out(c_turned, c_part, sems, 3)

    pairs = ((x1_mine, x1_out), (normed_here, normed_out), (inverse_here, inverse_out))
    copies = [send_out(*pair, sems, at) for at, pair in enumerate(pairs)]
    up.wait()
    activated, act_slope = gelu_and_slope(dot(ffn_in, w_up[...]))
    slope_here[...] = act_slope.astype(jnp.bfloat16)
    copies.append(send_out(slope_here, slope_out, sems, 4))
    down.wait()
    store_halves(dot(activated.astype(jnp.bfloat16), w_down[...]), theirs, mine)
    flush(copies)

    @pl.when(chosen)
    def _():
        pltpu.make_async_copy(c_turned, c_part, sems.at[3]).wait()


def ffn_back_kernel(
    g_mine, g_other, down_in, slope_in, up_in, theirs, mine, w_down, slope, w_up, sems
):
    pairs = ((down_in, w_down), (slope_in, slope), (up_in, w_up))
    fetches = [send_out(*pair, sems, at) for at, pair in enumerate(pairs)]

    fetches[0].wait()
    grad_act = dot_nt(jnp.concatenate([g_mine[...], g_other[...]], 0), w_down[...])
    flush(fetches[1:])
    grad_pre = (grad_act * f32(slope)).astype(jnp.bfloat16)
    store_halves(dot_nt(grad_pre, w_up[...]), theirs, mine)


def attn_back_kernel(
    step, m, meta, g_mine, g_other, t_mine, t_other, gain,
    normed_in, inverse_in, w_out_in, packed_in, probs_in, w_qkv_in,
    x1_grad_out, ga_out, norm_grads, theirs, mine,
    normed_here, inverse_here, w_out, packed, probs, w_qkv, x1_grad_mine, ga_mine, sems,
):
    needs = (
        (inverse_in, inverse_here), (normed_in, normed_here), (w_out_in, w_out),
        (packed_in, packed), (probs_in, probs), (w_qkv_in, w_qkv),
    )
    fetches = [send_out(*pair, sems, at) for at, pair in enumerate(needs)]
    heads = probs.shape[0]
    half = ga_mine.shape[0]
    grad_norm = both(t_mine, t_other)
    grad_out = both(g_mine, g_other)
    flush(fetches[:2])
    normed = f32(normed_here)
    inverse = jnp.max(inverse_here[...], -1, keepdims=True)
    grad_mid = grad_out + norm_back(grad_norm, normed, inverse, gain[...])
    x1_grad_mine[...] = grad_mid[:half]
    grad_attn = grad_mid.astype(jnp.bfloat16)
    ga_mine[...] = grad_attn[:half]
    copies = [send_out(x1_grad_mine, x1_grad_out, sems, 6)]
    chosen = meta[1] == step

    @pl.when(chosen)
    def _():
        send_out(ga_mine, ga_out.at[m], sems, 7)

    norm_grads[0:1] = jnp.sum(grad_norm[:half] * normed[:half], 0, keepdims=True)
    norm_grads[1:2] = jnp.sum(grad_norm[:half], 0, keepdims=True)
    flush(fetches[2:5])
    grad_mix = dot_nt(grad_attn, w_out[...]).astype(jnp.bfloat16)
    grad_packed = attention_back(packed[...], grad_mix, lambda head: probs[head], heads)
    fetches[5].wait()
    store_halves(dot_nt(grad_packed, w_qkv[...]), theirs, mine)
    flush(copies)

    @pl.when(chosen)
    def _():
        pltpu.make_async_copy(ga_mine, ga_out.at[m], sems.at[7]).wait()


def input_back(near, far, gain, norm_grads, v_mine, x1_grad_mine):
    normed, inverse = norm_stats(f32(v_mine))
    grad_norm = f32(near) + f32(far)
    norm_grads[0:1] = jnp.sum(grad_norm * normed, 0, keepdims=True)
    norm_grads[1:2] = jnp.sum(grad_norm, 0, keepdims=True)
    return x1_grad_mine[...] + norm_back(grad_norm, normed, inverse, gain[...])


def fetch_skip(here, parts, w_all, sems):
    return [send_out(part, w_all.at[here ^ flip], sems, flip) for flip, part in enumerate(parts)]


def skip_back(rows, w_all, fetches):
    wide = w_all.shape[2]
    out = 0.0
    flush(fetches)
    for at in range(len(fetches)):
        out = out + dot_nt(rows[:, at * wide : (at + 1) * wide], w_all[at])
    return out


def hop_back_kernel(
    m, meta, near, far, gain, v_in, x1_grad_in, *refs
):
    *w_in, joined_out, h_grad, norm_grads, v_mine, x1_grad_mine, w_all, joined_mine, sems = refs
    parts = w_all.shape[0]
    needs = [send_out(v_in.at[m], v_mine, sems, parts), send_out(x1_grad_in, x1_grad_mine, sems, parts + 1)]
    fetches = fetch_skip(meta[3], w_in, w_all, sems)
    flush(needs)
    rounded = input_back(near, far, gain, norm_grads, v_mine, x1_grad_mine).astype(jnp.bfloat16)
    joined_mine[...] = rounded
    copy = send_out(joined_mine, joined_out.at[m], sems, parts + 2)
    h_grad[...] = skip_back(rounded, w_all, fetches).astype(h_grad.dtype)
    copy.wait()


def frames_back_kernel(
    m, meta, near, far, gain, joined_in, v_in, x1_grad_in, *refs
):
    *w_in, out, norm_grads, joined_grad, v_mine, x1_grad_mine, w_all, sems = refs
    parts = w_all.shape[0]
    pairs = ((v_in.at[m], v_mine), (x1_grad_in, x1_grad_mine), (joined_in.at[m], joined_grad))
    needs = [send_out(*pair, sems, parts + at) for at, pair in enumerate(pairs)]
    fetches = fetch_skip(meta[3], w_in, w_all, sems)
    flush(needs)
    grad_in = input_back(near, far, gain, norm_grads, v_mine, x1_grad_mine)
    out[...] = (grad_in + skip_back(joined_grad[...], w_all, fetches)).astype(out.dtype)


def skip_kernel(count, meta, *refs):
    parts, (*w_in, w_all, sems) = refs[:count], refs[count:]
    w_in, outs = w_in[:-count], w_in[-count:]
    wide = w_all.shape[2]
    flush(fetch_skip(meta[3], w_in, w_all, sems))
    for at in range(w_all.shape[0]):
        for rows, out in zip(parts, outs):
            out[:, at * wide : (at + 1) * wide] = dot(rows[...], w_all[at]).astype(out.dtype)


def join_kernel(m, meta, rows, skip_in, *refs):
    *w_in, rows_out, out, w_all, skip_part, sems = refs
    wide = w_all.shape[2]
    fetches = fetch_skip(meta[3], w_in, w_all, sems)
    fetches.append(send_out(skip_in, skip_part, sems, len(fetches) + 1))
    copy = send_out(rows, rows_out.at[m], sems, len(fetches) - 1)
    flush(fetches)
    for at in range(w_all.shape[0]):
        columns = slice(at * wide, (at + 1) * wide)
        product = dot(rows[...], w_all[at]) + skip_part[:, columns].astype(jnp.float32)
        out[:, columns] = product.astype(out.dtype)
    copy.wait()


def place_kernel(valid_of, meta, *refs):
    core, here = meta[0], meta[3]
    micro = refs[0].shape[0]
    blocks, outs = refs[: -2 * micro], refs[-2 * micro :]
    for at in range(micro):
        mine, other = outs[2 * at : 2 * at + 2]
        half, wide = mine.shape[0], blocks[0].shape[2]
        for flip, block in enumerate(blocks):
            columns = pl.ds(pl.multiple_of((here ^ flip) * wide, wide), wide)
            for start, out in ((core * half, mine), ((1 - core) * half, other)):
                start = pl.multiple_of(start, half)
                value = block[at, pl.ds(start, half)]
                if valid_of is not None:
                    row = lax.broadcasted_iota(jnp.int32, (half, wide), 0) + start
                    value = jnp.where(row < valid_of(at), value, jnp.zeros_like(value))
                out[:, columns] = value


def place_seed_kernel(meta, lens, blocks_in, *refs):
    *outs, blocks, sems = refs
    send_out(blocks_in, blocks, sems, 0).wait()
    place_kernel(
        lambda m: lens[m, 0, 0] + lens[m, 0, 1],
        meta,
        *[blocks.at[meta[3] ^ flip] for flip in range(blocks.shape[0])],
        *outs,
    )


def seed_block_kernel(meta, lens, blocks_in, out, blocks, turned, sems):
    @pl.when(meta[1] == 1)
    def _():
        send_out(blocks_in, blocks, sems, 0).wait()
        micro, wide = blocks.shape[1], blocks.shape[3]
        half = turned.shape[1] // micro
        start = pl.multiple_of(meta[0] * half, half)
        row = lax.broadcasted_iota(jnp.int32, (half, wide), 0) + start
        for m in range(micro):
            valid = row < lens[m, 0, 0] + lens[m, 0, 1]
            for at in range(blocks.shape[0]):
                value = blocks[at, m, pl.ds(start, half)]
                value = jnp.where(valid, value, jnp.zeros_like(value))
                turned[at * wide : (at + 1) * wide, m * half : (m + 1) * half] = value.T
        send_out(turned, out, sems, 1).wait()


def hop_block_kernel(meta, *refs):
    *sources, out, turned, sems = refs

    @pl.when(meta[1] == 0)
    def _():
        for m, source in enumerate(sources):
            half = source.shape[0]
            turned[:, m * half : (m + 1) * half] = source[...].T
        send_out(turned, out, sems, 0).wait()


def copy_kernel(source, out, here, sems):
    send_out(source, here, sems, 0).wait()
    send_out(here, out, sems, 0).wait()


def columns_of(pair, target, sems, at, start=True):
    copies = []
    half = pair[0].shape[2] // 2
    for index in range(pair[0].shape[0]):
        for m in range(2):
            for side_at, part in enumerate(pair):
                block = (index * 2 + m) * 2 + side_at
                source = part.at[index, : target.shape[0], m * half : (m + 1) * half]
                columns = slice(block * half, (block + 1) * half)
                copies.append(
                    pltpu.make_async_copy(source, target.at[:, columns], sems.at[at + len(copies)])
                )
                if start:
                    copies[-1].start()
    return copies


def ffn_weights_kernel(meta, early, early_other, late, late_other, up_turned, w_down, *refs):
    grad_up, grad_down, ffn_in, grad_out, sems = refs[-5:]

    @pl.when(pl.program_id(0) == 0)
    def _():
        first, second = (early, early_other), (late, late_other)
        for at, (norms, grads) in enumerate(((first, second), (second, first))):

            @pl.when(meta[1] == at)
            def _(norms=norms, grads=grads):
                copies = columns_of(norms, ffn_in, sems, 0)
                copies += columns_of(grads, grad_out, sems, len(copies))
                flush(copies)

    activated, act_slope = gelu_and_slope(dot(up_turned[...], ffn_in[...]))
    grad_pre = (dot(w_down[...], grad_out[...]) * act_slope).astype(jnp.bfloat16)
    grad_down[...] = dot_nt(activated.astype(jnp.bfloat16), grad_out[...])
    grad_up[...] = dot_nt(ffn_in[...], grad_pre)


def skip_pick_kernel(meta, *refs):
    *sources, inputs, own, other, inputs_here, grad_here, sems = refs
    for at in range(2):

        @pl.when(meta[1] == at)
        def _(at=at):
            pairs = ((sources[at], inputs_here), (sources[2 + at], grad_here))
            flush([send_out(*pair, sems, i) for i, pair in enumerate(pairs)])

    inputs[...] = inputs_here[...]
    wide = own.shape[2]
    for out, owner in ((own, meta[3]), (other, meta[3] ^ 1)):
        columns = pl.ds(pl.multiple_of(owner * wide, wide), wide)
        out[...] = grad_here[:, :, columns]


def pack_kernel(first, second, out):
    out[: first.shape[0]] = first[...]
    out[first.shape[0] :] = second[...]


def unpack_kernel(source, first, second):
    first[...] = f32(source)[: first.shape[0]]
    second[...] = f32(source)[first.shape[0] :]


def skip_weights_kernel(*refs):
    *parts, out = refs
    count = len(parts) // 2
    total = 0.0
    for rows, grads in zip(parts[:count], parts[count:]):
        for m in range(rows.shape[0]):
            total = total + dot_tn(rows[m], grads[m])
    out[...] = total.astype(out.dtype)


def attn_again_kernel(meta, slopes, mine, other, w_qkv, packed_out, probs_out, mix_out):
    heads, rows = probs_out.shape[1], probs_out.shape[2]
    width = w_qkv.shape[0]
    first_len, second_len = (
        mine[0, width + at : width + at + 1, :1].astype(jnp.float32) for at in range(2)
    )
    allowed, distance = pair_masks(meta[0] * (rows // 2), first_len, second_len, rows)
    frames = jnp.concatenate([mine[0, :width].T, other[0, :width].T], 0)
    packed = dot(frames, w_qkv[...]).astype(jnp.bfloat16)
    packed_out[...] = packed
    for pair in range(heads // 2):
        left, right, mixed = pair_forward(
            pair_tiles(packed, pair), slopes, pair, allowed, distance
        )
        probs_out[0, 2 * pair] = left
        probs_out[0, 2 * pair + 1] = right
        mix_out[2 * HD * pair : 2 * HD * (pair + 1)] = mixed.T


def attn_weights_kernel(
    mine, other, packed, probs, w_out, in_mine, in_other, grad_mine, grad_other, mix_in, grad_qkv, grad_out,
    grad_packed, attn_in, grad_all, mix, sems,
):
    step = pl.program_id(0)
    rows = probs.shape[2]
    half = rows // 2

    def fetches():
        made = columns_of((in_mine, in_other), attn_in, sems, 1, False)
        for index in range(grad_mine.shape[0]):
            for m in range(2):
                for side_at, part in enumerate((grad_mine, grad_other)):
                    block = (index * 2 + m) * 2 + side_at
                    target = grad_all.at[block * half : (block + 1) * half]
                    made.append(pltpu.make_async_copy(part.at[index, m], target, sems.at[1 + len(made)]))
        made.append(pltpu.make_async_copy(mix_in, mix, sems.at[0]))
        return made

    @pl.when(step == 0)
    def _():
        for copy in fetches():
            copy.start()

    heads = probs.shape[1]
    grad_attn = jnp.concatenate([mine[0, 0], other[0, 0]], 0)
    grad_mix = dot_nt(grad_attn, w_out[...]).astype(jnp.bfloat16)
    here = attention_back(packed[...], grad_mix, lambda head: probs[0, head], heads)
    grad_packed[pl.ds(pl.multiple_of(step * rows, rows), rows)] = here

    @pl.when(step == pl.num_programs(0) - 1)
    def _():
        flush(fetches())
        grad_qkv[...] = dot(attn_in[...], grad_packed[...])
        grad_out[...] = dot(mix[...], grad_all[...])


def shape(dims, kind=jnp.bfloat16):
    return jax.ShapeDtypeStruct(dims, kind)


WHOLE = pl.BlockSpec(memory_space=pltpu.VMEM)
SCALARS = pl.BlockSpec(memory_space=pltpu.SMEM)
FAR = pl.BlockSpec(memory_space=pltpu.HBM)
LATER = pl.BlockSpec(memory_space=pl.ANY)
SMALL = pl.CostEstimate(flops=1, bytes_accessed=1, transcendentals=0)
COSTS = [
    pl.CostEstimate(flops=int(part * 1.1e9), bytes_accessed=int(part * 3.6e6), transcendentals=0)
    for part in (11, 4, 4, 4)
]


def constant(dims):
    return pl.BlockSpec(dims, lambda step: (0,) * len(dims))


def in_hbm(value):
    return pltpu.with_memory_space_constraint(value, pltpu.HBM)


def call(
    kernel, outs, scalars, arrays, far_in=(), free_in=(), far_outs=(), scratch=(), hold=(), keep=(), cost=SMALL
):
    count = len(scalars) + len(arrays) + len(far_in) + len(free_in)
    later = count + len(hold)

    def body(*refs):
        kernel(*refs[:count], *refs[later + len(keep) :])

    return list(
        pl.pallas_call(
            body,
            name=getattr(kernel, "func", kernel).__name__,
            out_shape=[*(pltpu.HBM(item.shape, item.dtype) for item in far_outs), *outs],
            in_specs=[SCALARS] * len(scalars)
            + [WHOLE] * len(arrays)
            + [FAR] * len(far_in)
            + [LATER] * (len(free_in) + len(hold))
            + [FAR] * len(keep),
            out_specs=[FAR] * len(far_outs) + [WHOLE] * len(outs),
            scratch_shapes=list(scratch),
            input_output_aliases={later + at: at for at in range(len(keep))},
            compiler_params=pltpu.CompilerParams(vmem_limit_bytes=20 * MIB),
            cost_estimate=cost,
        )(*scalars, *arrays, *map(in_hbm, far_in), *free_in, *hold, *map(in_hbm, keep))
    )


def vmem(item):
    return pltpu.VMEM(item.shape, item.dtype)


def attn_forward(place, scalars, v, gain, bias, w_qkv, w_out, kept, hold, cost):
    half, width = v[0].shape
    rows, wide = 2 * half, w_out.shape[0]
    heads = wide // HD
    buffers = [shape((2, half, width)), shape((width + LEN_ROWS, 2 * half))]
    far = [shape((rows, 3 * wide)), shape((heads, rows, rows))]

    def kernel(*refs):
        count = len(refs) - 12
        v_out, a_out, packed_out, probs_out = refs[count : count + 4]
        attn_fwd_kernel(*place, *refs[:count], packed_out, probs_out, v_out, a_out, *refs[count + 4 :])

    kernel.__name__ = "attn_fwd_kernel"
    return call(
        kernel,
        [shape((half, width)), shape((half, width))],
        scalars,
        [*v, gain, bias],
        far_in=[w_qkv, w_out],
        far_outs=[*buffers, *far],
        scratch=[
            *map(vmem, far), vmem(w_qkv), vmem(w_out), pltpu.VMEM((width + LEN_ROWS, half), jnp.bfloat16),
            pltpu.SemaphoreType.DMA((4 + heads + heads // 2,)),
        ],
        hold=hold,
        keep=kept,
        cost=cost,
    )


def ffn_forward(place, scalars, v, s, gain, bias, w_up, w_down, kept, hold, cost):
    half, width = v[0].shape
    rows, units = 2 * half, w_up.shape[1]
    buffer = shape((width, 2 * half))
    far = [
        shape((half, width), jnp.float32),
        shape((rows, width)),
        shape((rows, LANES), jnp.float32),
        shape((rows, units)),
    ]

    def kernel(*refs):
        count = len(refs) - 15
        c_out, *others = refs[count : count + 5]
        ffn_fwd_kernel(*place, *refs[:count], *others, c_out, *refs[count + 5 :])

    kernel.__name__ = "ffn_fwd_kernel"
    return call(
        kernel,
        [shape((half, width)), shape((half, width))],
        scalars,
        [*v, *s, gain, bias],
        far_in=[w_up, w_down],
        far_outs=[buffer, *far],
        scratch=[
            *map(vmem, far), vmem(w_up), vmem(w_down), pltpu.VMEM((width, half), jnp.bfloat16),
            pltpu.SemaphoreType.DMA((7,)),
        ],
        hold=hold,
        keep=kept,
        cost=cost,
    )


def ffn_backward(g, slope, w_down, w_up, hold, cost):
    half, width = g[0].shape
    return call(
        ffn_back_kernel,
        [shape((half, width)), shape((half, width))],
        [],
        [*g],
        far_in=[w_down, slope, w_up],
        scratch=[vmem(w_down), vmem(slope), vmem(w_up), pltpu.SemaphoreType.DMA((3,))],
        hold=hold,
        cost=cost,
    )


def attn_backward(
    place, scalars, g, t, gain, w_out, w_qkv, normed, inverse, packed, probs, kept, hold, cost
):
    half, width = g[0].shape
    far = [shape((2, half, width)), shape((half, width), jnp.float32)]
    needs = [normed, inverse, w_out, packed, probs, w_qkv]

    def kernel(*refs):
        count = len(refs) - 14
        ga_out, x1_grad_out = refs[count : count + 2]
        attn_back_kernel(*place, *refs[:count], x1_grad_out, ga_out, *refs[count + 2 :])

    kernel.__name__ = "attn_back_kernel"
    return call(
        kernel,
        [shape((2, width), jnp.float32), shape((half, width)), shape((half, width))],
        scalars,
        [*g, *t, gain],
        far_in=needs,
        far_outs=far,
        scratch=[
            *map(vmem, needs), vmem(far[1]), pltpu.VMEM((half, width), jnp.bfloat16),
            pltpu.SemaphoreType.DMA((8,)),
        ],
        hold=hold,
        keep=kept,
        cost=cost,
    )


def ffn_weights(meta, early, late, up_turned, w_down, hold):
    units, width = w_down.shape
    group, _, part = early[0].shape
    rows = 2 * group * part
    wide = min(256, units)
    return pl.pallas_call(
        ffn_weights_kernel,
        name="ffn_weights_kernel",
        grid=(units // wide,),
        in_specs=[
            SCALARS, FAR, FAR, FAR, FAR,
            pl.BlockSpec((wide, width), lambda step: (step, 0)),
            pl.BlockSpec((wide, width), lambda step: (step, 0)),
            *[LATER] * len(hold),
        ],
        out_specs=[
            pl.BlockSpec((width, wide), lambda step: (0, step)),
            pl.BlockSpec((wide, width), lambda step: (step, 0)),
        ],
        out_shape=[shape((width, units), jnp.float32), shape((units, width), jnp.float32)],
        scratch_shapes=[
            pltpu.VMEM((width, rows), jnp.bfloat16),
            pltpu.VMEM((width, rows), jnp.bfloat16),
            pltpu.SemaphoreType.DMA((8 * group,)),
        ],
        compiler_params=pltpu.CompilerParams(vmem_limit_bytes=40 * MIB),
        cost_estimate=pl.CostEstimate(flops=30_000_000_000, bytes_accessed=100_000_000, transcendentals=0),
    )(meta, *map(in_hbm, (*early, *late, up_turned, w_down)), *hold)


def attn_again(meta, slopes, attn_in, w_qkv, per_call):
    group, tall, part = attn_in[0].shape
    half = part // 2
    rows = 2 * half
    count = 2 * group
    per_call = min(per_call, count)
    width = w_qkv.shape[0]
    wide = w_qkv.shape[1] // 3
    heads = wide // HD
    outs = [((rows * count, 3 * wide)), (count, heads, rows, rows), (wide, rows * count)]
    kept = []
    for start in range(0, count, per_call):
        piece = pl.BlockSpec(
            (1, tall, half), lambda step, start=start: ((start + step) // 2, 0, (start + step) % 2)
        )

        def kernel(*refs):
            attn_again_kernel(*refs[:5], *refs[-3:])

        kept = pl.pallas_call(
            kernel,
            name="attn_again_kernel",
            grid=(per_call,),
            in_specs=[SCALARS, SCALARS, piece, piece, constant((width, 3 * wide))] + [FAR] * len(kept),
            out_specs=[
                pl.BlockSpec((rows, 3 * wide), lambda step, start=start: (start + step, 0)),
                pl.BlockSpec((1, heads, rows, rows), lambda step, start=start: (start + step, 0, 0, 0)),
                pl.BlockSpec((wide, rows), lambda step, start=start: (0, start + step)),
            ],
            out_shape=[pltpu.HBM(dims, jnp.bfloat16) for dims in outs],
            input_output_aliases={5 + at: at for at in range(len(kept))},
            compiler_params=pltpu.CompilerParams(vmem_limit_bytes=20 * MIB),
            cost_estimate=pl.CostEstimate(
                flops=2_000_000_000 * per_call, bytes_accessed=6_000_000 * per_call, transcendentals=0
            ),
        )(meta, slopes, *map(in_hbm, (*attn_in, w_qkv, *kept)))
    return kept


def attn_weights(attn_in, grad_attn, packed, probs, mix, w_out):
    wide, width = w_out.shape
    count, heads, rows, _ = probs.shape
    half = rows // 2
    group = count // 2
    piece = pl.BlockSpec((1, 1, half, width), lambda step: (step // 2, step % 2, 0, 0))
    return pl.pallas_call(
        attn_weights_kernel,
        name="attn_weights_kernel",
        grid=(count,),
        in_specs=[
            piece, piece,
            pl.BlockSpec((rows, 3 * wide), lambda step: (step, 0)),
            pl.BlockSpec((1, heads, rows, rows), lambda step: (step, 0, 0, 0)),
            constant((wide, width)), FAR, FAR, FAR, FAR, FAR,
        ],
        out_specs=[constant((width, 3 * wide)), constant((wide, width))],
        out_shape=[shape((width, 3 * wide), jnp.float32), shape((wide, width), jnp.float32)],
        scratch_shapes=[
            pltpu.VMEM((rows * count, 3 * wide), jnp.bfloat16),
            pltpu.VMEM((width, rows * count), jnp.bfloat16),
            pltpu.VMEM((rows * count, width), jnp.bfloat16),
            pltpu.VMEM((wide, rows * count), jnp.bfloat16),
            pltpu.SemaphoreType.DMA((1 + 8 * group,)),
        ],
        compiler_params=pltpu.CompilerParams(vmem_limit_bytes=40 * MIB),
        cost_estimate=SMALL,
    )(*map(in_hbm, (*grad_attn, packed, probs, w_out, *attn_in, *grad_attn, mix)))


def shards(
    frames,
    cotangent,
    lengths,
    norm1_gain,
    norm1_bias,
    norm2_gain,
    norm2_bias,
    w_qkv,
    w_out,
    w_up,
    w_down,
    w_skip,
):
    first = lax.axis_index("section") == 0
    dp_at = lax.axis_index("dp")
    tensor_at = lax.axis_index("tensor")
    core, chip = tensor_at % 2, tensor_at // 2
    dp_count = lax.axis_size("dp")
    micro, rows, quarter = frames.shape
    half = rows // 2
    w_qkv, w_out, w_up, w_down = w_qkv[0], w_out[0], w_up[0], w_down[0]
    heads = w_qkv.shape[1] // (3 * HD)
    gather_dp = dp_count <= GROUP
    group = dp_count if gather_dp else 1
    section = lax.axis_index("section")
    meta = jnp.stack([core, section, chip, tensor_at, dp_at % group]).astype(jnp.int32)
    scalars = [meta, lengths]

    half_dims = shape((half, norm1_gain.shape[1]))
    pair_dims = shape((micro, *half_dims.shape))
    x1_dims = shape(half_dims.shape, jnp.float32)
    vector = shape((2, norm1_gain.shape[1]), jnp.float32)

    over = x_swap(frames)
    blocks = [frames, core_swap(frames), over, core_swap(over)]
    xs = call(functools.partial(place_kernel, None), [half_dims] * (2 * micro), [meta], blocks)
    xs = [xs[2 * m : 2 * m + 2] for m in range(micro)]
    head_ids = tensor_at * heads + jnp.arange(heads, dtype=jnp.int32)
    slopes = 2.0 ** (-8.0 * (head_ids + 1).astype(jnp.float32) / HEADS)
    up_turned = w_up.T

    w_near = call(
        copy_kernel, [], [], [], far_in=[w_skip[0]], far_outs=[shape(w_skip.shape[1:])],
        scratch=[vmem(w_skip[0]), pltpu.SemaphoreType.DMA((1,))], hold=[over],
    )[0]
    w_over = x_swap(w_near)
    w_blocks = [w_near, core_swap(w_near), w_over, core_swap(w_over)]
    w_scratch = [
        pltpu.VMEM((len(w_blocks), *w_near.shape), w_near.dtype),
        pltpu.SemaphoreType.DMA((len(w_blocks) + 3,)),
    ]
    cot_blocks = lax.all_gather(cotangent, "tensor", axis=0, tiled=False)

    def all_rows(mine):
        every = lax.all_gather(mine, "dp", axis=0, tiled=False) if gather_dp else mine[None]
        return every, core_swap(every)

    def forward(step, v, buffers, holds_attn, holds_ffn):
        attn, ffn, near = [], [], []
        keep_attn, keep_ffn = buffers
        for m in range(micro):
            item = attn_forward(
                (step, m), [*scalars, slopes], v[m], norm1_gain, norm1_bias, w_qkv, w_out, keep_attn,
                near[-1:] + holds_attn[m], COSTS[step],
            )
            keep_attn = item[:2]
            attn.append(item[2:])
            near.append(near_sum(*item[4:]))
        sums = [whole_sum(item) for item in near]
        near = []
        for m in range(micro):
            item = ffn_forward(
                (step, m), [meta], v[m], sums[m], norm2_gain, norm2_bias, w_up, w_down, keep_ffn,
                near[-1:] + holds_ffn[m] + attn[-1][2:3], COSTS[step],
            )
            keep_ffn = item[:1]
            ffn.append(item[1:])
            near.append(near_sum(*item[5:]))
        kept = dict(
            v=keep_attn[0],
            packed=[item[0] for item in attn],
            probs=[item[1] for item in attn],
            norm=[item[1:3] for item in ffn],
            slope=[item[3] for item in ffn],
        )
        return [(item[0], part) for item, part in zip(ffn, near)], kept, (keep_attn, keep_ffn)

    def finish(x1, near):
        total = x1 + near.astype(jnp.float32) + x_swap(near).astype(jnp.float32)
        return total.astype(jnp.bfloat16)

    def backward(step, g, kept, buffers, holds, holds_attn=((), ())):
        near, attn = [], []
        keep_attn = buffers
        for m in range(micro):
            item = ffn_backward(g[m], kept["slope"][m], w_down, w_up, near[-1:] + holds[m], COSTS[3 - step])
            near.append(near_sum(*item))
        last = item[0]
        sums = [whole_sum(item) for item in near]
        near = []
        for m in range(micro):
            item = attn_backward(
                (step, m), [meta], g[m], sums[m], norm2_gain, w_out, w_qkv,
                *kept["norm"][m], kept["packed"][m], kept["probs"][m], keep_attn, [*near[-1:], last, *holds_attn[m]],
                COSTS[3 - step],
            )
            keep_attn = item[:1]
            attn.append(item[1:])
            near.append(near_sum(*item[3:]))
        return attn, near, keep_attn

    skip_parts = call(
        functools.partial(skip_kernel, micro), [half_dims] * micro, [meta], [v[0] for v in xs],
        far_in=w_blocks, scratch=w_scratch,
    )
    skip_recv = [section_swap(item) for item in skip_parts]
    outs_a, kept_a, (keep_attn, keep_ffn) = forward(0, xs, ([], []), [[], [w_over]], [[*skip_parts[:1], in_hbm(cot_blocks)], [skip_recv[0]]])
    early = call(
        seed_block_kernel, [], scalars, [], far_in=[cot_blocks], far_outs=[shape(keep_ffn[0].shape)],
        scratch=[vmem(cot_blocks), vmem(keep_ffn[0]), pltpu.SemaphoreType.DMA((2,))], keep=keep_ffn,
    )[0]
    early = all_rows(early)
    h_recv = [section_swap(finish(*item)) for item in outs_a]
    joined, h_kept = [], []
    for m in range(micro):
        *h_kept, mine = call(
            functools.partial(join_kernel, m), [half_dims], [meta], [h_recv[m]],
            far_in=[skip_recv[m], *w_blocks], far_outs=[pair_dims], keep=h_kept,
            scratch=[w_scratch[0], vmem(half_dims), w_scratch[1]],
        )
        joined.append((mine, core_swap(mine)))
    outs_b, kept_b, (keep_attn, keep_ffn) = forward(1, joined, (keep_attn, []), [[], []], [[], []])
    g_c = call(
        place_seed_kernel, [half_dims] * (2 * micro), scalars, [], far_in=[cot_blocks],
        scratch=[vmem(cot_blocks), pltpu.SemaphoreType.DMA((1,))], hold=[keep_attn[0]],
    )
    g_c = [g_c[2 * m : 2 * m + 2] for m in range(micro)]
    attn_in = all_rows(keep_attn[1])

    attn_c, near_c, keep_back = backward(1, g_c, kept_b, [], [[], [in_hbm(early[0])]])
    hop, joined_own = [], []
    for m in range(micro):
        *joined_own, h_grad, norm_grads = call(
            functools.partial(hop_back_kernel, m), [half_dims, vector], [meta],
            [near_c[m], x_swap(near_c[m]), norm1_gain],
            far_in=[kept_b["v"], attn_c[m][0], *w_blocks], far_outs=[pair_dims], keep=joined_own,
            scratch=[vmem(half_dims), vmem(x1_dims), w_scratch[0], vmem(half_dims), w_scratch[1]],
        )
        hop.append((h_grad, norm_grads))
    g_d = []
    for m in range(micro):
        mine = section_swap(hop[m][0])
        g_d.append((mine, core_swap(mine)))
    def over_dp(total):
        return lax.psum(total.astype(jnp.bfloat16), "dp").astype(jnp.float32)

    late = call(
        hop_block_kernel, [], [meta], [item[0] for item in g_d], far_outs=[shape(keep_ffn[0].shape)],
        scratch=[vmem(keep_ffn[0]), pltpu.SemaphoreType.DMA((1,))], keep=keep_ffn,
    )[0]
    joined_recv = section_swap(joined_own[0])
    columns = shape((micro, half, quarter))
    inputs, own, other = call(
        skip_pick_kernel, [pair_dims, columns, columns], [meta], [],
        far_in=[kept_a["v"], h_kept[0], joined_recv, joined_own[0]],
        scratch=[vmem(pair_dims), vmem(pair_dims), pltpu.SemaphoreType.DMA((2,))],
    )
    skip_total = call(
        skip_weights_kernel, [shape(w_skip.shape[1:])], [], [inputs, core_swap(inputs), own, core_swap(other)]
    )[0]
    attn_d, near_d, keep_back = backward(
        0, g_d, kept_a, keep_back, [[in_hbm(attn_in[0])], [in_hbm(late)]], [[joined_recv], [skip_total]]
    )

    late = all_rows(late)
    grad_attn = all_rows(keep_back[0])
    again = attn_again(meta, slopes, attn_in, w_qkv, 2 * micro)
    last = [
        call(
            functools.partial(frames_back_kernel, m), [half_dims, vector], [meta],
            [near_d[m], x_swap(near_d[m]), norm1_gain],
            far_in=[joined_recv, kept_a["v"], attn_d[m][0], *w_blocks],
            scratch=[vmem(half_dims), vmem(half_dims), vmem(x1_dims), *w_scratch],
        )
        for m in range(micro)
    ]
    def choose(early, late):
        return jnp.where(first, early, late)

    norm_grads = choose(
        jnp.concatenate([sum(item[1] for item in last), sum(item[1] for item in attn_d)], 0),
        jnp.concatenate([sum(item[1] for item in hop), sum(item[1] for item in attn_c)], 0),
    )
    norm_grads += core_swap(norm_grads)
    tall = skip_total.shape[0]
    flat = norm_grads.astype(jnp.bfloat16).reshape(-1, quarter)
    packed_sums = call(
        pack_kernel, [shape((tall + flat.shape[0], quarter))], [], [skip_total, flat],
        hold=[in_hbm(grad_attn[0]), in_hbm(again[2])],
    )[0]
    summed = lax.psum(packed_sums, "dp")
    up_total, down_total = ffn_weights(meta, early, late, up_turned, w_down, [packed_sums])
    qkv_total, out_total = attn_weights(attn_in, grad_attn, *again, w_out)
    skip_total, norm_grads = call(
        unpack_kernel,
        [shape((tall, quarter), jnp.float32), shape((summed.shape[0] - tall, quarter), jnp.float32)],
        [], [summed], hold=[in_hbm(out_total)],
    )
    norm_grads = norm_grads.reshape(4, -1)
    if not gather_dp:
        up_total, down_total, qkv_total, out_total = (
            over_dp(item) for item in (up_total, down_total, qkv_total, out_total)
        )

    def own_columns(item):
        return lax.dynamic_slice_in_dim(item, tensor_at * quarter, quarter, 1)

    def other_columns(item):
        return lax.dynamic_slice_in_dim(item, (tensor_at ^ 1) * quarter, quarter, 1)

    pieces = []
    for m in range(micro):
        mine = choose(last[m][0], finish(*outs_b[m]))
        own, other = own_columns(mine), core_swap(other_columns(mine))
        pieces.append(
            jnp.where(core == 0, jnp.concatenate([own, other], 0), jnp.concatenate([other, own], 0))
        )
    return (
        jnp.stack(pieces, 0)[None],
        norm_grads[0:1],
        norm_grads[1:2],
        norm_grads[2:3],
        norm_grads[3:4],
        qkv_total[None],
        out_total[None],
        up_total[None],
        down_total[None],
        skip_total.astype(jnp.float32)[None],
    )


def solution(mesh):
    in_specs = (
        P(None, "dp", "tensor"),
        P(None, "dp", "tensor"),
        P(None, "dp", None),
        P("section", None),
        P("section", None),
        P("section", None),
        P("section", None),
        P("section", None, "tensor"),
        P("section", "tensor", None),
        P("section", None, "tensor"),
        P("section", "tensor", None),
        P("section", None, "tensor"),
    )
    out_specs = (
        P("section", None, "dp", "tensor"),
        P("section", None),
        P("section", None),
        P("section", None),
        P("section", None),
        P("section", None, "tensor"),
        P("section", "tensor", None),
        P("section", None, "tensor"),
        P("section", "tensor", None),
        P("section", None, "tensor"),
    )
    return jax.shard_map(shards, mesh=mesh, in_specs=in_specs, out_specs=out_specs, check_vma=False)
```

```python
import functools

import jax
import jax.numpy as jnp
from jax import lax
from jax.experimental import pallas as pl
from jax.experimental.pallas import tpu as pltpu
from jax.sharding import PartitionSpec as P

HEADS = 16
HD = 64
UTT = 2

epsilon = 1e-05
inv_root_two = 0.7071067811865476
inv_root_two_pi = 0.3989422804014327
MIB = 1 << 20
LANES = 128
LEN_ROWS = 16
GROUP = 4


def core_swap(value):
    count = lax.axis_size("tensor")
    return lax.ppermute(value, "tensor", [(at, at ^ 1) for at in range(count)])


def x_swap(value):
    count = lax.axis_size("tensor")
    return lax.ppermute(value, "tensor", [(at, at ^ 2) for at in range(count)])


def section_swap(value):
    return lax.ppermute(value, "section", [(0, 1), (1, 0)])


def dp_swap(value, bit):
    count = lax.axis_size("dp")
    return lax.ppermute(value, "dp", [(at, at ^ bit) for at in range(count)])


def dp_shift(value, steps):
    count = lax.axis_size("dp")
    return lax.ppermute(value, "dp", [(at, (at + steps) % count) for at in range(count)])


def add_rounded(left, right):
    return (left.astype(jnp.float32) + right.astype(jnp.float32)).astype(jnp.bfloat16)


def near_sum(theirs, mine):
    return add_rounded(mine, core_swap(theirs))


def whole_sum(near):
    half = add_rounded(near, x_swap(near))
    return half, core_swap(half)


def dot(left, right):
    return jnp.dot(left, right, preferred_element_type=jnp.float32)


def dot_nt(left, right):
    return lax.dot_general(
        left, right, (((1,), (1,)), ((), ())), preferred_element_type=jnp.float32
    )


def dot_tn(left, right):
    return lax.dot_general(
        left, right, (((0,), (0,)), ((), ())), preferred_element_type=jnp.float32
    )


def f32(ref):
    return ref[...].astype(jnp.float32)


def both(mine, other):
    return jnp.concatenate([f32(mine), f32(other)], 0)


def norm_stats(inputs):
    average = jnp.mean(inputs, -1, keepdims=True)
    centred = inputs - average
    inverse = lax.rsqrt(jnp.mean(centred * centred, -1, keepdims=True) + epsilon)
    return centred * inverse, inverse


def norm_back(grad_norm, normed, inverse, gain):
    scaled = grad_norm * gain
    return inverse * (
        scaled
        - jnp.mean(scaled, -1, keepdims=True)
        - normed * jnp.mean(scaled * normed, -1, keepdims=True)
    )


def gelu_and_slope(hidden):
    bell = jnp.exp(-0.5 * hidden * hidden)
    at = 1.0 / (1.0 + (0.3275911 * inv_root_two) * jnp.abs(hidden))
    tail = 1.061405429
    for term in (-1.453152027, 1.421413741, -0.284496736, 0.254829592):
        tail = tail * at + term
    tail = (0.5 * at) * tail * bell
    normal_cdf = jnp.where(hidden > 0, 1.0 - tail, tail)
    return hidden * normal_cdf, normal_cdf + hidden * (bell * inv_root_two_pi)


def pair_masks(turn, first_len, second_len, rows):
    def place(axis):
        at = lax.broadcasted_iota(jnp.int32, (rows, rows), axis) + turn
        return jnp.where(at >= rows, at - rows, at).astype(jnp.float32)

    def segment(at):
        return (at >= first_len).astype(jnp.int32) + (at >= first_len + second_len).astype(
            jnp.int32
        )

    queries, keys_all = place(0), place(1)
    return segment(queries) == segment(keys_all), jnp.abs(queries - keys_all)


def swap_sides(tile):
    return jnp.concatenate([tile[:, HD:], tile[:, :HD]], 1)


def side(tile, right):
    lane = lax.broadcasted_iota(jnp.int32, tile.shape, 1)
    return jnp.where((lane >= HD) == bool(right), tile, jnp.zeros_like(tile))


def pair_tiles(packed, pair):
    at = 6 * HD * pair
    return [packed[:, at + 2 * HD * i : at + 2 * HD * (i + 1)] for i in range(3)]


def attention_probs(queries, keys_all, slope, allowed, distance):
    scores = dot_nt(queries * HD ** (-0.5), keys_all)
    scores = jnp.where(allowed, scores - slope * distance, -1e30)
    exp_scores = jnp.exp(scores - jnp.max(scores, -1, keepdims=True))
    return (exp_scores / jnp.sum(exp_scores, -1, keepdims=True)).astype(jnp.bfloat16)


def pair_forward(tiles, slopes, pair, allowed, distance):
    left = attention_probs(
        side(tiles[0], 0), swap_sides(tiles[0]), slopes[2 * pair], allowed, distance
    )
    right = attention_probs(
        side(tiles[1], 1), swap_sides(tiles[2]), slopes[2 * pair + 1], allowed, distance
    )
    mixed = dot(left, side(tiles[1], 0)) + dot(right, side(tiles[2], 1))
    return left, right, mixed.astype(jnp.bfloat16)


def scores_back(probs, grad_mix, values):
    grad_probs = dot_nt(grad_mix, values)
    wide_probs = probs.astype(jnp.float32)
    delta = jnp.sum(wide_probs * grad_probs, -1, keepdims=True)
    return (wide_probs * (grad_probs - delta)).astype(jnp.bfloat16)


def pair_backward(tiles, left, right, grad_mix):
    scale = HD ** (-0.5)
    grad_left, grad_right = side(grad_mix, 0), side(grad_mix, 1)
    back_left = scores_back(left, grad_left, tiles[1])
    back_right = scores_back(right, grad_right, tiles[2])
    turned = [swap_sides(tile) * scale for tile in tiles]
    return [
        item.astype(jnp.bfloat16)
        for item in (
            dot(back_left, side(turned[0], 0)) + dot_tn(back_left, side(turned[0], 1)),
            dot_tn(left, grad_left) + dot(back_right, side(turned[2], 1)),
            dot_tn(back_right, side(turned[1], 0)) + dot_tn(right, grad_right),
        )
    ]


def attention_back(packed, grad_mix, probs_of, heads):
    grads = []
    for pair in range(heads // 2):
        columns = slice(2 * HD * pair, 2 * HD * (pair + 1))
        grads += pair_backward(
            pair_tiles(packed, pair), probs_of(2 * pair), probs_of(2 * pair + 1), grad_mix[:, columns]
        )
    return jnp.concatenate(grads, 1)


def store_halves(partial_sum, theirs, mine):
    half = mine.shape[0]
    mine[...] = partial_sum[:half].astype(mine.dtype)
    theirs[...] = partial_sum[half:].astype(theirs.dtype)


def flush(copies):
    for copy in copies:
        copy.wait()


def send_out(source, target, sems, at):
    copy = pltpu.make_async_copy(source, target, sems.at[at])
    copy.start()
    return copy


def attn_fwd_kernel(
    step, m, meta, lens, slopes, v_mine, v_other, gain, bias, w_qkv_in, w_out_in,
    packed_out, probs_out, v_out, a_out, theirs, mine,
    packed_here, probs_here, w_qkv, w_out, a_turned, sems,
):
    heads, rows, _ = probs_here.shape
    half = v_mine.shape[0]
    first_len, second_len = lens[m, 0, 0], lens[m, 0, 1]
    pairs = [slice(6 * HD * pair, 6 * HD * (pair + 1)) for pair in range(heads // 2)]
    parts = [
        send_out(w_qkv_in.at[:, here], w_qkv.at[:, here], sems, 4 + heads + pair)
        for pair, here in enumerate(pairs)
    ]
    last = send_out(w_out_in, w_out, sems, 3 + heads)
    copies = [send_out(v_mine, v_out.at[m], sems, 2)]
    normed, _ = norm_stats(both(v_mine, v_other))
    attn_in = (normed * gain[...] + bias[...]).astype(jnp.bfloat16)
    width = attn_in.shape[1]
    a_part = a_out.at[:, m * half : (m + 1) * half]
    chosen = meta[1] == step

    @pl.when(chosen)
    def _():
        a_turned[:width] = attn_in[:half].T
        row = lax.broadcasted_iota(jnp.int32, (LEN_ROWS, half), 0)
        own_lens = jnp.where(row == 0, first_len.astype(jnp.float32), second_len.astype(jnp.float32))
        a_turned[width:] = own_lens.astype(a_turned.dtype)
        send_out(a_turned, a_part, sems, 0)

    allowed, distance = pair_masks(
        meta[0] * half, first_len.astype(jnp.float32), second_len.astype(jnp.float32), rows
    )
    mixes = []
    for pair, here in enumerate(pairs):
        parts[pair].wait()
        packed = dot(attn_in, w_qkv[:, here]).astype(jnp.bfloat16)
        packed_here[:, here] = packed
        left, right, mixed = pair_forward(
            pair_tiles(packed, 0), slopes, pair, allowed, distance
        )
        for head, probs in ((2 * pair, left), (2 * pair + 1, right)):
            probs_here[head] = probs
            copies.append(send_out(probs_here.at[head], probs_out.at[head], sems, 3 + head))
        mixes.append(mixed)
    copies.append(send_out(packed_here, packed_out, sems, 1))
    last.wait()
    store_halves(dot(jnp.concatenate(mixes, 1), w_out[...]), theirs, mine)
    flush(copies)

    @pl.when(chosen)
    def _():
        pltpu.make_async_copy(a_turned, a_part, sems.at[0]).wait()


def ffn_fwd_kernel(
    step, m, meta, v_mine, v_other, s_mine, s_other, gain, bias, up_in, down_in,
    x1_out, normed_out, inverse_out, slope_out, c_out, theirs, mine,
    x1_mine, normed_here, inverse_here, slope_here, w_up, w_down, c_turned, sems,
):
    up, down = send_out(up_in, w_up, sems, 5), send_out(down_in, w_down, sems, 6)
    half = v_mine.shape[0]
    middle = both(v_mine, v_other) + both(s_mine, s_other)
    x1_mine[...] = middle[:half]
    normed, inverse = norm_stats(middle)
    normed_here[...] = normed.astype(jnp.bfloat16)
    inverse_here[...] = jnp.broadcast_to(inverse, inverse_here.shape)
    ffn_in = (normed * gain[...] + bias[...]).astype(jnp.bfloat16)
    c_part = c_out.at[:, m * half : (m + 1) * half]
    chosen = meta[1] == step

    @pl.when(chosen)
    def _():
        c_turned[...] = ffn_in[:half].T
        send_out(c_turned, c_part, sems, 3)

    pairs = ((x1_mine, x1_out), (normed_here, normed_out), (inverse_here, inverse_out))
    copies = [send_out(*pair, sems, at) for at, pair in enumerate(pairs)]
    up.wait()
    activated, act_slope = gelu_and_slope(dot(ffn_in, w_up[...]))
    slope_here[...] = act_slope.astype(jnp.bfloat16)
    copies.append(send_out(slope_here, slope_out, sems, 4))
    down.wait()
    store_halves(dot(activated.astype(jnp.bfloat16), w_down[...]), theirs, mine)
    flush(copies)

    @pl.when(chosen)
    def _():
        pltpu.make_async_copy(c_turned, c_part, sems.at[3]).wait()


def ffn_back_kernel(
    g_mine, g_other, down_in, slope_in, up_in, theirs, mine, w_down, slope, w_up, sems
):
    pairs = ((down_in, w_down), (slope_in, slope), (up_in, w_up))
    fetches = [send_out(*pair, sems, at) for at, pair in enumerate(pairs)]

    fetches[0].wait()
    grad_act = dot_nt(jnp.concatenate([g_mine[...], g_other[...]], 0), w_down[...])
    flush(fetches[1:])
    grad_pre = (grad_act * f32(slope)).astype(jnp.bfloat16)
    store_halves(dot_nt(grad_pre, w_up[...]), theirs, mine)


def attn_back_kernel(
    step, m, meta, g_mine, g_other, t_mine, t_other, gain,
    normed_in, inverse_in, w_out_in, packed_in, probs_in, w_qkv_in,
    x1_grad_out, ga_out, norm_grads, theirs, mine,
    normed_here, inverse_here, w_out, packed, probs, w_qkv, x1_grad_mine, ga_mine, sems,
):
    needs = (
        (inverse_in, inverse_here), (normed_in, normed_here), (w_out_in, w_out),
        (packed_in, packed), (probs_in, probs), (w_qkv_in, w_qkv),
    )
    fetches = [send_out(*pair, sems, at) for at, pair in enumerate(needs)]
    heads = probs.shape[0]
    half = ga_mine.shape[0]
    grad_norm = both(t_mine, t_other)
    grad_out = both(g_mine, g_other)
    flush(fetches[:2])
    normed = f32(normed_here)
    inverse = jnp.max(inverse_here[...], -1, keepdims=True)
    grad_mid = grad_out + norm_back(grad_norm, normed, inverse, gain[...])
    x1_grad_mine[...] = grad_mid[:half]
    grad_attn = grad_mid.astype(jnp.bfloat16)
    ga_mine[...] = grad_attn[:half]
    copies = [send_out(x1_grad_mine, x1_grad_out, sems, 6)]
    chosen = meta[1] == step

    @pl.when(chosen)
    def _():
        send_out(ga_mine, ga_out.at[m], sems, 7)

    norm_grads[0:1] = jnp.sum(grad_norm[:half] * normed[:half], 0, keepdims=True)
    norm_grads[1:2] = jnp.sum(grad_norm[:half], 0, keepdims=True)
    flush(fetches[2:5])
    grad_mix = dot_nt(grad_attn, w_out[...]).astype(jnp.bfloat16)
    grad_packed = attention_back(packed[...], grad_mix, lambda head: probs[head], heads)
    fetches[5].wait()
    store_halves(dot_nt(grad_packed, w_qkv[...]), theirs, mine)
    flush(copies)

    @pl.when(chosen)
    def _():
        pltpu.make_async_copy(ga_mine, ga_out.at[m], sems.at[7]).wait()


def input_back(near, far, gain, norm_grads, v_mine, x1_grad_mine):
    normed, inverse = norm_stats(f32(v_mine))
    grad_norm = f32(near) + f32(far)
    norm_grads[0:1] = jnp.sum(grad_norm * normed, 0, keepdims=True)
    norm_grads[1:2] = jnp.sum(grad_norm, 0, keepdims=True)
    return x1_grad_mine[...] + norm_back(grad_norm, normed, inverse, gain[...])


def fetch_skip(here, parts, w_all, sems):
    return [send_out(part, w_all.at[here ^ flip], sems, flip) for flip, part in enumerate(parts)]


def skip_back(rows, w_all, fetches):
    wide = w_all.shape[2]
    out = 0.0
    flush(fetches)
    for at in range(len(fetches)):
        out = out + dot_nt(rows[:, at * wide : (at + 1) * wide], w_all[at])
    return out


def hop_back_kernel(
    m, meta, near, far, gain, v_in, x1_grad_in, *refs
):
    *w_in, joined_out, h_grad, norm_grads, v_mine, x1_grad_mine, w_all, joined_mine, sems = refs
    parts = w_all.shape[0]
    needs = [send_out(v_in.at[m], v_mine, sems, parts), send_out(x1_grad_in, x1_grad_mine, sems, parts + 1)]
    fetches = fetch_skip(meta[3], w_in, w_all, sems)
    flush(needs)
    rounded = input_back(near, far, gain, norm_grads, v_mine, x1_grad_mine).astype(jnp.bfloat16)
    joined_mine[...] = rounded
    copy = send_out(joined_mine, joined_out.at[m], sems, parts + 2)
    h_grad[...] = skip_back(rounded, w_all, fetches).astype(h_grad.dtype)
    copy.wait()


def frames_back_kernel(
    m, meta, near, far, gain, joined_in, v_in, x1_grad_in, *refs
):
    *w_in, out, norm_grads, joined_grad, v_mine, x1_grad_mine, w_all, sems = refs
    parts = w_all.shape[0]
    pairs = ((v_in.at[m], v_mine), (x1_grad_in, x1_grad_mine), (joined_in.at[m], joined_grad))
    needs = [send_out(*pair, sems, parts + at) for at, pair in enumerate(pairs)]
    fetches = fetch_skip(meta[3], w_in, w_all, sems)
    flush(needs)
    grad_in = input_back(near, far, gain, norm_grads, v_mine, x1_grad_mine)
    out[...] = (grad_in + skip_back(joined_grad[...], w_all, fetches)).astype(out.dtype)


def skip_kernel(count, meta, *refs):
    parts, (*w_in, w_all, sems) = refs[:count], refs[count:]
    w_in, outs = w_in[:-count], w_in[-count:]
    wide = w_all.shape[2]
    flush(fetch_skip(meta[3], w_in, w_all, sems))
    for at in range(w_all.shape[0]):
        for rows, out in zip(parts, outs):
            out[:, at * wide : (at + 1) * wide] = dot(rows[...], w_all[at]).astype(out.dtype)


def join_kernel(m, meta, rows, skip_in, *refs):
    *w_in, rows_out, out, w_all, skip_part, sems = refs
    wide = w_all.shape[2]
    fetches = fetch_skip(meta[3], w_in, w_all, sems)
    fetches.append(send_out(skip_in, skip_part, sems, len(fetches) + 1))
    copy = send_out(rows, rows_out.at[m], sems, len(fetches) - 1)
    flush(fetches)
    for at in range(w_all.shape[0]):
        columns = slice(at * wide, (at + 1) * wide)
        product = dot(rows[...], w_all[at]) + skip_part[:, columns].astype(jnp.float32)
        out[:, columns] = product.astype(out.dtype)
    copy.wait()


def place_kernel(valid_of, meta, *refs):
    core, here = meta[0], meta[3]
    micro = refs[0].shape[0]
    blocks, outs = refs[: -2 * micro], refs[-2 * micro :]
    for at in range(micro):
        mine, other = outs[2 * at : 2 * at + 2]
        half, wide = mine.shape[0], blocks[0].shape[2]
        for flip, block in enumerate(blocks):
            columns = pl.ds(pl.multiple_of((here ^ flip) * wide, wide), wide)
            for start, out in ((core * half, mine), ((1 - core) * half, other)):
                start = pl.multiple_of(start, half)
                value = block[at, pl.ds(start, half)]
                if valid_of is not None:
                    row = lax.broadcasted_iota(jnp.int32, (half, wide), 0) + start
                    value = jnp.where(row < valid_of(at), value, jnp.zeros_like(value))
                out[:, columns] = value


def place_seed_kernel(meta, lens, blocks_in, *refs):
    *outs, blocks, sems = refs
    send_out(blocks_in, blocks, sems, 0).wait()
    place_kernel(
        lambda m: lens[m, 0, 0] + lens[m, 0, 1],
        meta,
        *[blocks.at[meta[3] ^ flip] for flip in range(blocks.shape[0])],
        *outs,
    )


def seed_block_kernel(meta, lens, blocks_in, out, blocks, turned, sems):
    @pl.when(meta[1] == 1)
    def _():
        send_out(blocks_in, blocks, sems, 0).wait()
        micro, wide = blocks.shape[1], blocks.shape[3]
        half = turned.shape[1] // micro
        start = pl.multiple_of(meta[0] * half, half)
        row = lax.broadcasted_iota(jnp.int32, (half, wide), 0) + start
        for m in range(micro):
            valid = row < lens[m, 0, 0] + lens[m, 0, 1]
            for at in range(blocks.shape[0]):
                value = blocks[at, m, pl.ds(start, half)]
                value = jnp.where(valid, value, jnp.zeros_like(value))
                turned[at * wide : (at + 1) * wide, m * half : (m + 1) * half] = value.T
        send_out(turned, out, sems, 1).wait()


def hop_block_kernel(meta, *refs):
    *sources, out, turned, sems = refs

    @pl.when(meta[1] == 0)
    def _():
        for m, source in enumerate(sources):
            half = source.shape[0]
            turned[:, m * half : (m + 1) * half] = source[...].T
        send_out(turned, out, sems, 0).wait()


def hand_on_kernel(*refs):
    pass


def copy_kernel(source, out, here, sems):
    send_out(source, here, sems, 0).wait()
    send_out(here, out, sems, 0).wait()


def columns_of(pair, target, sems, at, start=True):
    copies = []
    half = pair[0].shape[2] // 2
    for index in range(pair[0].shape[0]):
        for m in range(2):
            for side_at, part in enumerate(pair):
                block = (index * 2 + m) * 2 + side_at
                source = part.at[index, : target.shape[0], m * half : (m + 1) * half]
                columns = slice(block * half, (block + 1) * half)
                copies.append(
                    pltpu.make_async_copy(source, target.at[:, columns], sems.at[at + len(copies)])
                )
                if start:
                    copies[-1].start()
    return copies


def ffn_weights_kernel(meta, early, early_other, late, late_other, up_turned, w_down, *refs):
    grad_up, grad_down, ffn_in, grad_out, sems = refs[-5:]

    @pl.when(pl.program_id(0) == 0)
    def _():
        first, second = (early, early_other), (late, late_other)
        for at, (norms, grads) in enumerate(((first, second), (second, first))):

            @pl.when(meta[1] == at)
            def _(norms=norms, grads=grads):
                copies = columns_of(norms, ffn_in, sems, 0)
                copies += columns_of(grads, grad_out, sems, len(copies))
                flush(copies)

    activated, act_slope = gelu_and_slope(dot(up_turned[...], ffn_in[...]))
    grad_pre = (dot(w_down[...], grad_out[...]) * act_slope).astype(jnp.bfloat16)
    grad_down[...] = dot_nt(activated.astype(jnp.bfloat16), grad_out[...])
    grad_up[...] = dot_nt(ffn_in[...], grad_pre)


def skip_pick_kernel(meta, *refs):
    *sources, inputs, own, other, inputs_here, grad_here, sems = refs
    for at in range(2):

        @pl.when(meta[1] == at)
        def _(at=at):
            pairs = ((sources[at], inputs_here), (sources[2 + at], grad_here))
            flush([send_out(*pair, sems, i) for i, pair in enumerate(pairs)])

    inputs[...] = inputs_here[...]
    wide = own.shape[2]
    for out, owner in ((own, meta[3]), (other, meta[3] ^ 1)):
        columns = pl.ds(pl.multiple_of(owner * wide, wide), wide)
        out[...] = grad_here[:, :, columns]


def pack_kernel(first, second, out):
    out[: first.shape[0]] = first[...]
    out[first.shape[0] :] = second[...]


def unpack_kernel(source, first, *rows):
    tall, wide = first.shape
    first[...] = f32(source)[:tall]
    each = rows[0].shape[1] // wide
    for at, row in enumerate(rows):
        for part in range(each):
            here = tall + at * each + part
            row[:, part * wide : (part + 1) * wide] = source[here : here + 1].astype(jnp.float32)


def skip_weights_kernel(*refs):
    *parts, out = refs
    count = len(parts) // 2
    total = 0.0
    for rows, grads in zip(parts[:count], parts[count:]):
        for m in range(rows.shape[0]):
            total = total + dot_tn(rows[m], grads[m])
    out[...] = total.astype(out.dtype)


def attn_again_kernel(meta, slopes, mine, other, w_qkv, packed_out, probs_out, mix_out):
    heads, rows = probs_out.shape[1], probs_out.shape[2]
    width = w_qkv.shape[0]
    first_len, second_len = (
        mine[0, width + at : width + at + 1, :1].astype(jnp.float32) for at in range(2)
    )
    allowed, distance = pair_masks(meta[0] * (rows // 2), first_len, second_len, rows)
    frames = jnp.concatenate([mine[0, :width].T, other[0, :width].T], 0)
    packed = dot(frames, w_qkv[...]).astype(jnp.bfloat16)
    packed_out[...] = packed
    for pair in range(heads // 2):
        left, right, mixed = pair_forward(
            pair_tiles(packed, pair), slopes, pair, allowed, distance
        )
        probs_out[0, 2 * pair] = left
        probs_out[0, 2 * pair + 1] = right
        mix_out[2 * HD * pair : 2 * HD * (pair + 1)] = mixed.T


def attn_weights_kernel(
    mine, other, packed, probs, w_out, in_mine, in_other, grad_mine, grad_other, mix_in, *refs
):
    grad_qkv, grad_out, grad_packed, attn_in, grad_all, mix, sems = refs[-7:]
    step = pl.program_id(0)
    rows = probs.shape[2]
    half = rows // 2

    def fetches():
        made = columns_of((in_mine, in_other), attn_in, sems, 1, False)
        for index in range(grad_mine.shape[0]):
            for m in range(2):
                for side_at, part in enumerate((grad_mine, grad_other)):
                    block = (index * 2 + m) * 2 + side_at
                    target = grad_all.at[block * half : (block + 1) * half]
                    made.append(pltpu.make_async_copy(part.at[index, m], target, sems.at[1 + len(made)]))
        made.append(pltpu.make_async_copy(mix_in, mix, sems.at[0]))
        return made

    @pl.when(step == 0)
    def _():
        for copy in fetches():
            copy.start()

    heads = probs.shape[1]
    grad_attn = jnp.concatenate([mine[0, 0], other[0, 0]], 0)
    grad_mix = dot_nt(grad_attn, w_out[...]).astype(jnp.bfloat16)
    here = attention_back(packed[...], grad_mix, lambda head: probs[0, head], heads)
    grad_packed[pl.ds(pl.multiple_of(step * rows, rows), rows)] = here

    @pl.when(step == pl.num_programs(0) - 1)
    def _():
        flush(fetches())
        grad_qkv[...] = dot(attn_in[...], grad_packed[...])
        grad_out[...] = dot(mix[...], grad_all[...])


def shape(dims, kind=jnp.bfloat16):
    return jax.ShapeDtypeStruct(dims, kind)


WHOLE = pl.BlockSpec(memory_space=pltpu.VMEM)
SCALARS = pl.BlockSpec(memory_space=pltpu.SMEM)
FAR = pl.BlockSpec(memory_space=pltpu.HBM)
LATER = pl.BlockSpec(memory_space=pl.ANY)
SMALL = pl.CostEstimate(flops=1, bytes_accessed=1, transcendentals=0)
AGAIN = pl.CostEstimate(flops=8_000_000_000, bytes_accessed=24_000_000, transcendentals=0)
COSTS = [
    pl.CostEstimate(flops=int(part * 1.1e9), bytes_accessed=int(part * 3.6e6), transcendentals=0)
    for part in (11, 4, 4, 4)
]


def constant(dims):
    return pl.BlockSpec(dims, lambda step: (0,) * len(dims))


def in_hbm(value):
    return pltpu.with_memory_space_constraint(value, pltpu.HBM)


def call(
    kernel, outs, scalars, arrays, far_in=(), free_in=(), far_outs=(), scratch=(), hold=(), keep=(), cost=SMALL
):
    count = len(scalars) + len(arrays) + len(far_in) + len(free_in)
    later = count + len(hold)

    def body(*refs):
        kernel(*refs[:count], *refs[later + len(keep) :])

    return list(
        pl.pallas_call(
            body,
            name=getattr(kernel, "func", kernel).__name__,
            out_shape=[*(pltpu.HBM(item.shape, item.dtype) for item in far_outs), *outs],
            in_specs=[SCALARS] * len(scalars)
            + [WHOLE] * len(arrays)
            + [FAR] * len(far_in)
            + [LATER] * (len(free_in) + len(hold))
            + [FAR] * len(keep),
            out_specs=[FAR] * len(far_outs) + [WHOLE] * len(outs),
            scratch_shapes=list(scratch),
            input_output_aliases={later + at: at for at in range(len(keep))},
            compiler_params=pltpu.CompilerParams(vmem_limit_bytes=20 * MIB),
            cost_estimate=cost,
        )(*scalars, *arrays, *map(in_hbm, far_in), *free_in, *hold, *map(in_hbm, keep))
    )


def vmem(item):
    return pltpu.VMEM(item.shape, item.dtype)


def attn_forward(place, scalars, v, gain, bias, w_qkv, w_out, kept, hold, cost):
    half, width = v[0].shape
    rows, wide = 2 * half, w_out.shape[0]
    heads = wide // HD
    buffers = [shape((2, half, width)), shape((width + LEN_ROWS, 2 * half))]
    far = [shape((rows, 3 * wide)), shape((heads, rows, rows))]

    def kernel(*refs):
        count = len(refs) - 12
        v_out, a_out, packed_out, probs_out = refs[count : count + 4]
        attn_fwd_kernel(*place, *refs[:count], packed_out, probs_out, v_out, a_out, *refs[count + 4 :])

    kernel.__name__ = "attn_fwd_kernel"
    return call(
        kernel,
        [shape((half, width)), shape((half, width))],
        scalars,
        [*v, gain, bias],
        far_in=[w_qkv, w_out],
        far_outs=[*buffers, *far],
        scratch=[
            *map(vmem, far), vmem(w_qkv), vmem(w_out), pltpu.VMEM((width + LEN_ROWS, half), jnp.bfloat16),
            pltpu.SemaphoreType.DMA((4 + heads + heads // 2,)),
        ],
        hold=hold,
        keep=kept,
        cost=cost,
    )


def ffn_forward(place, scalars, v, s, gain, bias, w_up, w_down, kept, hold, cost):
    half, width = v[0].shape
    rows, units = 2 * half, w_up.shape[1]
    buffer = shape((width, 2 * half))
    far = [
        shape((half, width), jnp.float32),
        shape((rows, width)),
        shape((rows, LANES), jnp.float32),
        shape((rows, units)),
    ]

    def kernel(*refs):
        count = len(refs) - 15
        c_out, *others = refs[count : count + 5]
        ffn_fwd_kernel(*place, *refs[:count], *others, c_out, *refs[count + 5 :])

    kernel.__name__ = "ffn_fwd_kernel"
    return call(
        kernel,
        [shape((half, width)), shape((half, width))],
        scalars,
        [*v, *s, gain, bias],
        far_in=[w_up, w_down],
        far_outs=[buffer, *far],
        scratch=[
            *map(vmem, far), vmem(w_up), vmem(w_down), pltpu.VMEM((width, half), jnp.bfloat16),
            pltpu.SemaphoreType.DMA((7,)),
        ],
        hold=hold,
        keep=kept,
        cost=cost,
    )


def ffn_backward(g, slope, w_down, w_up, hold, cost):
    half, width = g[0].shape
    return call(
        ffn_back_kernel,
        [shape((half, width)), shape((half, width))],
        [],
        [*g],
        far_in=[w_down, slope, w_up],
        scratch=[vmem(w_down), vmem(slope), vmem(w_up), pltpu.SemaphoreType.DMA((3,))],
        hold=hold,
        cost=cost,
    )


def attn_backward(
    place, scalars, g, t, gain, w_out, w_qkv, normed, inverse, packed, probs, kept, hold, cost
):
    half, width = g[0].shape
    far = [shape((2, half, width)), shape((half, width), jnp.float32)]
    needs = [normed, inverse, w_out, packed, probs, w_qkv]

    def kernel(*refs):
        count = len(refs) - 14
        ga_out, x1_grad_out = refs[count : count + 2]
        attn_back_kernel(*place, *refs[:count], x1_grad_out, ga_out, *refs[count + 2 :])

    kernel.__name__ = "attn_back_kernel"
    return call(
        kernel,
        [shape((2, width), jnp.float32), shape((half, width)), shape((half, width))],
        scalars,
        [*g, *t, gain],
        far_in=needs,
        far_outs=far,
        scratch=[
            *map(vmem, needs), vmem(far[1]), pltpu.VMEM((half, width), jnp.bfloat16),
            pltpu.SemaphoreType.DMA((8,)),
        ],
        hold=hold,
        keep=kept,
        cost=cost,
    )


def ffn_weights(meta, early, late, up_turned, w_down, hold):
    units, width = w_down.shape
    group, _, part = early[0].shape
    rows = 2 * group * part
    wide = min(256, units)
    return pl.pallas_call(
        ffn_weights_kernel,
        name="ffn_weights_kernel",
        grid=(units // wide,),
        in_specs=[
            SCALARS, FAR, FAR, FAR, FAR,
            pl.BlockSpec((wide, width), lambda step: (step, 0)),
            pl.BlockSpec((wide, width), lambda step: (step, 0)),
            *[LATER] * len(hold),
        ],
        out_specs=[
            pl.BlockSpec((width, wide), lambda step: (0, step)),
            pl.BlockSpec((wide, width), lambda step: (step, 0)),
        ],
        out_shape=[shape((width, units), jnp.float32), shape((units, width), jnp.float32)],
        scratch_shapes=[
            pltpu.VMEM((width, rows), jnp.bfloat16),
            pltpu.VMEM((width, rows), jnp.bfloat16),
            pltpu.SemaphoreType.DMA((8 * group,)),
        ],
        compiler_params=pltpu.CompilerParams(vmem_limit_bytes=40 * MIB),
        cost_estimate=pl.CostEstimate(flops=30000000000, bytes_accessed=100000000, transcendentals=0),
    )(meta, *map(in_hbm, (*early, *late, up_turned, w_down)), *hold)


def attn_again(meta, slopes, attn_in, w_qkv, part_at, parts, kept, hold, cost):
    group, tall, part = attn_in[0].shape
    half = part // 2
    rows = 2 * half
    count = 2 * group
    per_call = count // parts
    start = part_at * per_call
    width = w_qkv.shape[0]
    wide = w_qkv.shape[1] // 3
    heads = wide // HD
    outs = [((rows * count, 3 * wide)), (count, heads, rows, rows), (wide, rows * count)]
    piece = pl.BlockSpec(
        (1, tall, half), lambda step: ((start + step) // 2, 0, (start + step) % 2)
    )

    def kernel(*refs):
        attn_again_kernel(*refs[:5], *refs[-3:])

    return pl.pallas_call(
        kernel,
        name="attn_again_kernel",
        grid=(per_call,),
        in_specs=[SCALARS, SCALARS, piece, piece, constant((width, 3 * wide))]
        + [LATER] * len(hold)
        + [FAR] * len(kept),
        out_specs=[
            pl.BlockSpec((rows, 3 * wide), lambda step: (start + step, 0)),
            pl.BlockSpec((1, heads, rows, rows), lambda step: (start + step, 0, 0, 0)),
            pl.BlockSpec((wide, rows), lambda step: (0, start + step)),
        ],
        out_shape=[pltpu.HBM(dims, jnp.bfloat16) for dims in outs],
        input_output_aliases={5 + len(hold) + at: at for at in range(len(kept))},
        compiler_params=pltpu.CompilerParams(vmem_limit_bytes=20 * MIB),
        cost_estimate=cost,
    )(meta, slopes, *map(in_hbm, (*attn_in, w_qkv)), *hold, *map(in_hbm, kept))


def attn_weights(attn_in, grad_attn, packed, probs, mix, w_out, hold):
    wide, width = w_out.shape
    count, heads, rows, _ = probs.shape
    half = rows // 2
    group = count // 2
    piece = pl.BlockSpec((1, 1, half, width), lambda step: (step // 2, step % 2, 0, 0))
    return pl.pallas_call(
        attn_weights_kernel,
        name="attn_weights_kernel",
        grid=(count,),
        in_specs=[
            piece, piece,
            pl.BlockSpec((rows, 3 * wide), lambda step: (step, 0)),
            pl.BlockSpec((1, heads, rows, rows), lambda step: (step, 0, 0, 0)),
            constant((wide, width)), FAR, FAR, FAR, FAR, FAR, *[LATER] * len(hold),
        ],
        out_specs=[constant((width, 3 * wide)), constant((wide, width))],
        out_shape=[shape((width, 3 * wide), jnp.float32), shape((wide, width), jnp.float32)],
        scratch_shapes=[
            pltpu.VMEM((rows * count, 3 * wide), jnp.bfloat16),
            pltpu.VMEM((width, rows * count), jnp.bfloat16),
            pltpu.VMEM((rows * count, width), jnp.bfloat16),
            pltpu.VMEM((wide, rows * count), jnp.bfloat16),
            pltpu.SemaphoreType.DMA((1 + 8 * group,)),
        ],
        compiler_params=pltpu.CompilerParams(vmem_limit_bytes=40 * MIB),
        cost_estimate=SMALL,
    )(*map(in_hbm, (*grad_attn, packed, probs, w_out, *attn_in, *grad_attn, mix)), *hold)


def shards(
    frames,
    cotangent,
    lengths,
    norm1_gain,
    norm1_bias,
    norm2_gain,
    norm2_bias,
    w_qkv,
    w_out,
    w_up,
    w_down,
    w_skip,
):
    first = lax.axis_index("section") == 0
    dp_at = lax.axis_index("dp")
    tensor_at = lax.axis_index("tensor")
    core, chip = tensor_at % 2, tensor_at // 2
    dp_count = lax.axis_size("dp")
    micro, rows, quarter = frames.shape
    half = rows // 2
    w_qkv, w_out, w_up, w_down = w_qkv[0], w_out[0], w_up[0], w_down[0]
    heads = w_qkv.shape[1] // (3 * HD)
    gather_dp = dp_count <= GROUP
    group = dp_count if gather_dp else 1
    section = lax.axis_index("section")
    meta = jnp.stack([core, section, chip, tensor_at, dp_at % group]).astype(jnp.int32)
    scalars = [meta, lengths]

    half_dims = shape((half, norm1_gain.shape[1]))
    pair_dims = shape((micro, *half_dims.shape))
    x1_dims = shape(half_dims.shape, jnp.float32)
    vector = shape((2, norm1_gain.shape[1]), jnp.float32)

    over = x_swap(frames)
    blocks = [frames, core_swap(frames), over, core_swap(over)]
    xs = call(functools.partial(place_kernel, None), [half_dims] * (2 * micro), [meta], blocks)
    xs = [xs[2 * m : 2 * m + 2] for m in range(micro)]
    head_ids = tensor_at * heads + jnp.arange(heads, dtype=jnp.int32)
    slopes = 2.0 ** (-8.0 * (head_ids + 1).astype(jnp.float32) / HEADS)
    up_turned = w_up.T

    w_near = call(
        copy_kernel, [], [], [], far_in=[w_skip[0]], far_outs=[shape(w_skip.shape[1:])],
        scratch=[vmem(w_skip[0]), pltpu.SemaphoreType.DMA((1,))], hold=[over],
    )[0]
    w_over = x_swap(w_near)
    w_blocks = [w_near, core_swap(w_near), w_over, core_swap(w_over)]
    w_scratch = [
        pltpu.VMEM((len(w_blocks), *w_near.shape), w_near.dtype),
        pltpu.SemaphoreType.DMA((len(w_blocks) + 3,)),
    ]
    cot_blocks = lax.all_gather(cotangent, "tensor", axis=0, tiled=False)

    def hand_on(value, after):
        return call(
            hand_on_kernel, [], [], [], far_outs=[shape(value.shape, value.dtype)], keep=[value],
            hold=after,
        )[0]

    def gather_rows(mine):
        return lax.all_gather(mine, "dp", axis=0, tiled=False) if gather_dp else mine[None]

    def all_rows(mine):
        every = gather_rows(mine)
        return every, core_swap(every)

    def forward(step, v, buffers, holds_attn, holds_ffn):
        attn, ffn, near = [], [], []
        keep_attn, keep_ffn = buffers
        for m in range(micro):
            item = attn_forward(
                (step, m), [*scalars, slopes], v[m], norm1_gain, norm1_bias, w_qkv, w_out, keep_attn,
                near[-1:] + holds_attn[m], COSTS[step],
            )
            keep_attn = item[:2]
            attn.append(item[2:])
            near.append(near_sum(*item[4:]))
        sums = [whole_sum(item) for item in near]
        near = []
        for m in range(micro):
            item = ffn_forward(
                (step, m), [meta], v[m], sums[m], norm2_gain, norm2_bias, w_up, w_down, keep_ffn,
                near[-1:] + holds_ffn[m] + attn[-1][2:3], COSTS[step],
            )
            keep_ffn = item[:1]
            ffn.append(item[1:])
            near.append(near_sum(*item[5:]))
        kept = dict(
            v=keep_attn[0],
            packed=[item[0] for item in attn],
            probs=[item[1] for item in attn],
            norm=[item[1:3] for item in ffn],
            slope=[item[3] for item in ffn],
        )
        return [(item[0], part) for item, part in zip(ffn, near)], kept, (keep_attn, keep_ffn)

    def finish(x1, near, far):
        total = x1 + near.astype(jnp.float32) + far.astype(jnp.float32)
        return total.astype(jnp.bfloat16)

    def backward(step, g, kept, buffers, holds, holds_attn=((), ())):
        near, attn = [], []
        keep_attn = buffers
        for m in range(micro):
            item = ffn_backward(g[m], kept["slope"][m], w_down, w_up, near[-1:] + holds[m], COSTS[3 - step])
            near.append(near_sum(*item))
        last = item[0]
        sums = [whole_sum(item) for item in near]
        near = []
        for m in range(micro):
            item = attn_backward(
                (step, m), [meta], g[m], sums[m], norm2_gain, w_out, w_qkv,
                *kept["norm"][m], kept["packed"][m], kept["probs"][m], keep_attn, [*near[-1:], last, *holds_attn[m]],
                COSTS[3 - step],
            )
            keep_attn = item[:1]
            attn.append(item[1:])
            near.append(near_sum(*item[3:]))
        return attn, near, keep_attn

    skip_parts = call(
        functools.partial(skip_kernel, micro), [half_dims] * micro, [meta], [v[0] for v in xs],
        far_in=w_blocks, scratch=w_scratch,
    )
    skip_recv = [section_swap(item) for item in skip_parts]
    outs_a, kept_a, (keep_attn, keep_ffn) = forward(0, xs, ([], []), [[], [w_over, in_hbm(up_turned)]], [[*skip_parts[:1], in_hbm(cot_blocks)], []])
    early = call(
        seed_block_kernel, [], scalars, [], far_in=[cot_blocks], far_outs=[shape(keep_ffn[0].shape)],
        scratch=[vmem(cot_blocks), vmem(keep_ffn[0]), pltpu.SemaphoreType.DMA((2,))], keep=keep_ffn,
    )[0]
    early = all_rows(early)
    h_recv = [section_swap(finish(*item, x_swap(item[1]))) for item in outs_a]
    joined, h_kept = [], []
    for m in range(micro):
        *h_kept, mine = call(
            functools.partial(join_kernel, m), [half_dims], [meta], [h_recv[m]],
            far_in=[skip_recv[m], *w_blocks], far_outs=[pair_dims], keep=h_kept,
            scratch=[w_scratch[0], vmem(half_dims), w_scratch[1]],
        )
        joined.append((mine, core_swap(mine)))
    outs_b, kept_b, (keep_attn, keep_ffn) = forward(1, joined, (keep_attn, []), [[], []], [[], []])
    g_c = call(
        place_seed_kernel, [half_dims] * (2 * micro), scalars, [], far_in=[cot_blocks],
        scratch=[vmem(cot_blocks), pltpu.SemaphoreType.DMA((1,))], hold=[keep_attn[0]],
    )
    g_c = [g_c[2 * m : 2 * m + 2] for m in range(micro)]
    attn_in = all_rows(keep_attn[1])

    attn_c, near_c, keep_back = backward(1, g_c, kept_b, [], [[], [in_hbm(early[0])]])
    hop, joined_own = [], []
    for m in range(micro):
        *joined_own, h_grad, norm_grads = call(
            functools.partial(hop_back_kernel, m), [half_dims, vector], [meta],
            [near_c[m], x_swap(near_c[m]), norm1_gain],
            far_in=[kept_b["v"], attn_c[m][0], *w_blocks], far_outs=[pair_dims], keep=joined_own,
            scratch=[vmem(half_dims), vmem(x1_dims), w_scratch[0], vmem(half_dims), w_scratch[1]],
        )
        hop.append((h_grad, norm_grads))
    g_d = []
    for m in range(micro):
        mine = section_swap(hop[m][0])
        g_d.append((mine, core_swap(mine)))
    def over_dp(total):
        return lax.psum(total.astype(jnp.bfloat16), "dp").astype(jnp.float32)

    late = call(
        hop_block_kernel, [], [meta], [item[0] for item in g_d], far_outs=[shape(keep_ffn[0].shape)],
        scratch=[vmem(keep_ffn[0]), pltpu.SemaphoreType.DMA((1,))], keep=keep_ffn,
    )[0]
    attn_d, near_d, keep_back = backward(
        0, g_d, kept_a, keep_back, [[in_hbm(attn_in[0])], [in_hbm(late)]]
    )

    late = gather_rows(late)
    far_d = [x_swap(item) for item in near_d]
    far_b = [x_swap(item[1]) for item in outs_b]
    joined_recv = section_swap(joined_own[0])
    again = attn_again(meta, slopes, attn_in, w_qkv, 0, 2, [], [attn_d[-1][1]], AGAIN)
    late = hand_on(late, [in_hbm(again[2])])
    late = late, core_swap(late)
    grad_every = gather_rows(hand_on(keep_back[0], [in_hbm(again[2])]))
    up_total, down_total = ffn_weights(meta, early, late, up_turned, w_down, [])
    again = attn_again(meta, slopes, attn_in, w_qkv, 1, 2, again, [in_hbm(up_total)], SMALL)
    columns = shape((micro, half, quarter))
    inputs, own, other = call(
        skip_pick_kernel, [pair_dims, columns, columns], [meta], [],
        far_in=[kept_a["v"], h_kept[0], joined_recv, joined_own[0]],
        scratch=[vmem(pair_dims), vmem(pair_dims), pltpu.SemaphoreType.DMA((2,))], hold=[in_hbm(again[2])],
    )
    skip_total = call(
        skip_weights_kernel, [shape(w_skip.shape[1:])], [], [inputs, core_swap(inputs), own, core_swap(other)]
    )[0]
    last = [
        call(
            functools.partial(frames_back_kernel, m), [half_dims, vector], [meta],
            [near_d[m], far_d[m], norm1_gain],
            far_in=[joined_recv, kept_a["v"], attn_d[m][0], *w_blocks],
            scratch=[vmem(half_dims), vmem(half_dims), vmem(x1_dims), *w_scratch],
            hold=[inputs, far_b[0], far_b[1]],
        )
        for m in range(micro)
    ]
    def choose(early, late):
        return jnp.where(first, early, late)

    norm_grads = choose(
        jnp.concatenate([sum(item[1] for item in last), sum(item[1] for item in attn_d)], 0),
        jnp.concatenate([sum(item[1] for item in hop), sum(item[1] for item in attn_c)], 0),
    )
    norm_grads += core_swap(norm_grads)
    tall = skip_total.shape[0]
    flat = norm_grads.astype(jnp.bfloat16).reshape(-1, quarter)
    packed_sums = call(
        pack_kernel, [shape((tall + flat.shape[0], quarter))], [], [skip_total, flat],
    )[0]
    summed = lax.psum(packed_sums, "dp")
    grad_every = hand_on(grad_every, [item[0] for item in last])
    grad_attn = grad_every, core_swap(grad_every)
    qkv_total, out_total = attn_weights(attn_in, grad_attn, *again, w_out, [in_hbm(up_total)])
    skip_total, *norm_grads = call(
        unpack_kernel,
        [shape((tall, quarter), jnp.float32)] + [shape((1, norm_grads.shape[1]), jnp.float32)] * 4,
        [], [summed], hold=[in_hbm(out_total)],
    )
    if not gather_dp:
        up_total, down_total, qkv_total, out_total = (
            over_dp(item) for item in (up_total, down_total, qkv_total, out_total)
        )

    def own_columns(item):
        return lax.dynamic_slice_in_dim(item, tensor_at * quarter, quarter, 1)

    def other_columns(item):
        return lax.dynamic_slice_in_dim(item, (tensor_at ^ 1) * quarter, quarter, 1)

    pieces = []
    for m in range(micro):
        mine = choose(last[m][0], finish(*outs_b[m], far_b[m]))
        own, other = own_columns(mine), core_swap(other_columns(mine))
        pieces.append(
            jnp.where(core == 0, jnp.concatenate([own, other], 0), jnp.concatenate([other, own], 0))
        )
    return (
        jnp.stack(pieces, 0)[None],
        *norm_grads,
        qkv_total[None],
        out_total[None],
        up_total[None],
        down_total[None],
        skip_total.astype(jnp.float32)[None],
    )


def solution(mesh):
    in_specs = (
        P(None, "dp", "tensor"),
        P(None, "dp", "tensor"),
        P(None, "dp", None),
        P("section", None),
        P("section", None),
        P("section", None),
        P("section", None),
        P("section", None, "tensor"),
        P("section", "tensor", None),
        P("section", None, "tensor"),
        P("section", "tensor", None),
        P("section", None, "tensor"),
    )
    out_specs = (
        P("section", None, "dp", "tensor"),
        P("section", None),
        P("section", None),
        P("section", None),
        P("section", None),
        P("section", None, "tensor"),
        P("section", "tensor", None),
        P("section", None, "tensor"),
        P("section", "tensor", None),
        P("section", None, "tensor"),
    )
    return jax.shard_map(shards, mesh=mesh, in_specs=in_specs, out_specs=out_specs, check_vma=False)
```

```python
import functools

import jax
import jax.numpy as jnp
from jax import lax
from jax.experimental import pallas as pl
from jax.experimental.pallas import tpu as pltpu
from jax.sharding import PartitionSpec as P

HEADS = 16
HD = 64
UTT = 2

epsilon = 1e-05
inv_root_two = 0.7071067811865476
inv_root_two_pi = 0.3989422804014327
MIB = 1 << 20
LANES = 128
LEN_ROWS = 16
GROUP = 4


def core_swap(value):
    count = lax.axis_size("tensor")
    return lax.ppermute(value, "tensor", [(at, at ^ 1) for at in range(count)])


def x_swap(value):
    count = lax.axis_size("tensor")
    return lax.ppermute(value, "tensor", [(at, at ^ 2) for at in range(count)])


def section_swap(value):
    return lax.ppermute(value, "section", [(0, 1), (1, 0)])


def dp_swap(value, bit):
    count = lax.axis_size("dp")
    return lax.ppermute(value, "dp", [(at, at ^ bit) for at in range(count)])


def dp_shift(value, steps):
    count = lax.axis_size("dp")
    return lax.ppermute(value, "dp", [(at, (at + steps) % count) for at in range(count)])


def add_rounded(left, right):
    return (left.astype(jnp.float32) + right.astype(jnp.float32)).astype(jnp.bfloat16)


def near_sum(theirs, mine):
    return add_rounded(mine, core_swap(theirs))


def whole_sum(near):
    half = add_rounded(near, x_swap(near))
    return half, core_swap(half)


def dot(left, right):
    return jnp.dot(left, right, preferred_element_type=jnp.float32)


def dot_nt(left, right):
    return lax.dot_general(
        left, right, (((1,), (1,)), ((), ())), preferred_element_type=jnp.float32
    )


def dot_tn(left, right):
    return lax.dot_general(
        left, right, (((0,), (0,)), ((), ())), preferred_element_type=jnp.float32
    )


def f32(ref):
    return ref[...].astype(jnp.float32)


def both(mine, other):
    return jnp.concatenate([f32(mine), f32(other)], 0)


def norm_stats(inputs):
    average = jnp.mean(inputs, -1, keepdims=True)
    centred = inputs - average
    inverse = lax.rsqrt(jnp.mean(centred * centred, -1, keepdims=True) + epsilon)
    return centred * inverse, inverse


def norm_back(grad_norm, normed, inverse, gain):
    scaled = grad_norm * gain
    return inverse * (
        scaled
        - jnp.mean(scaled, -1, keepdims=True)
        - normed * jnp.mean(scaled * normed, -1, keepdims=True)
    )


def gelu_and_slope(hidden):
    bell = jnp.exp(-0.5 * hidden * hidden)
    at = 1.0 / (1.0 + (0.3275911 * inv_root_two) * jnp.abs(hidden))
    tail = 1.061405429
    for term in (-1.453152027, 1.421413741, -0.284496736, 0.254829592):
        tail = tail * at + term
    tail = (0.5 * at) * tail * bell
    normal_cdf = jnp.where(hidden > 0, 1.0 - tail, tail)
    return hidden * normal_cdf, normal_cdf + hidden * (bell * inv_root_two_pi)


def pair_masks(turn, first_len, second_len, rows):
    def place(axis):
        at = lax.broadcasted_iota(jnp.int32, (rows, rows), axis) + turn
        return jnp.where(at >= rows, at - rows, at).astype(jnp.float32)

    def segment(at):
        return (at >= first_len).astype(jnp.int32) + (at >= first_len + second_len).astype(
            jnp.int32
        )

    queries, keys_all = place(0), place(1)
    return segment(queries) == segment(keys_all), jnp.abs(queries - keys_all)


def swap_sides(tile):
    return jnp.concatenate([tile[:, HD:], tile[:, :HD]], 1)


def side(tile, right):
    lane = lax.broadcasted_iota(jnp.int32, tile.shape, 1)
    return jnp.where((lane >= HD) == bool(right), tile, jnp.zeros_like(tile))


def pair_tiles(packed, pair):
    at = 6 * HD * pair
    return [packed[:, at + 2 * HD * i : at + 2 * HD * (i + 1)] for i in range(3)]


def attention_probs(queries, keys_all, slope, allowed, distance):
    scores = dot_nt(queries * HD ** (-0.5), keys_all)
    scores = jnp.where(allowed, scores - slope * distance, -1e30)
    exp_scores = jnp.exp(scores - jnp.max(scores, -1, keepdims=True))
    return (exp_scores / jnp.sum(exp_scores, -1, keepdims=True)).astype(jnp.bfloat16)


def pair_forward(tiles, slopes, pair, allowed, distance):
    left = attention_probs(
        side(tiles[0], 0), swap_sides(tiles[0]), slopes[2 * pair], allowed, distance
    )
    right = attention_probs(
        side(tiles[1], 1), swap_sides(tiles[2]), slopes[2 * pair + 1], allowed, distance
    )
    mixed = dot(left, side(tiles[1], 0)) + dot(right, side(tiles[2], 1))
    return left, right, mixed.astype(jnp.bfloat16)


def scores_back(probs, grad_mix, values):
    grad_probs = dot_nt(grad_mix, values)
    wide_probs = probs.astype(jnp.float32)
    delta = jnp.sum(wide_probs * grad_probs, -1, keepdims=True)
    return (wide_probs * (grad_probs - delta)).astype(jnp.bfloat16)


def pair_backward(tiles, left, right, grad_mix):
    scale = HD ** (-0.5)
    grad_left, grad_right = side(grad_mix, 0), side(grad_mix, 1)
    back_left = scores_back(left, grad_left, tiles[1])
    back_right = scores_back(right, grad_right, tiles[2])
    turned = [swap_sides(tile) * scale for tile in tiles]
    return [
        item.astype(jnp.bfloat16)
        for item in (
            dot(back_left, side(turned[0], 0)) + dot_tn(back_left, side(turned[0], 1)),
            dot_tn(left, grad_left) + dot(back_right, side(turned[2], 1)),
            dot_tn(back_right, side(turned[1], 0)) + dot_tn(right, grad_right),
        )
    ]


def attention_back(packed, grad_mix, probs_of, heads):
    grads = []
    for pair in range(heads // 2):
        columns = slice(2 * HD * pair, 2 * HD * (pair + 1))
        grads += pair_backward(
            pair_tiles(packed, pair), probs_of(2 * pair), probs_of(2 * pair + 1), grad_mix[:, columns]
        )
    return jnp.concatenate(grads, 1)


def store_halves(partial_sum, theirs, mine):
    half = mine.shape[0]
    mine[...] = partial_sum[:half].astype(mine.dtype)
    theirs[...] = partial_sum[half:].astype(theirs.dtype)


def flush(copies):
    for copy in copies:
        copy.wait()


def send_out(source, target, sems, at):
    copy = pltpu.make_async_copy(source, target, sems.at[at])
    copy.start()
    return copy


def attn_fwd_kernel(
    step, m, meta, lens, slopes, v_mine, v_other, gain, bias, w_qkv_in, w_out_in,
    packed_out, probs_out, v_out, a_out, theirs, mine,
    packed_here, probs_here, w_qkv, w_out, a_turned, sems,
):
    heads, rows, _ = probs_here.shape
    half = v_mine.shape[0]
    first_len, second_len = lens[m, 0, 0], lens[m, 0, 1]
    pairs = [slice(6 * HD * pair, 6 * HD * (pair + 1)) for pair in range(heads // 2)]
    parts = [
        send_out(w_qkv_in.at[:, here], w_qkv.at[:, here], sems, 4 + heads + pair)
        for pair, here in enumerate(pairs)
    ]
    last = send_out(w_out_in, w_out, sems, 3 + heads)
    copies = [send_out(v_mine, v_out.at[m], sems, 2)]
    normed, _ = norm_stats(both(v_mine, v_other))
    attn_in = (normed * gain[...] + bias[...]).astype(jnp.bfloat16)
    width = attn_in.shape[1]
    a_part = a_out.at[:, m * half : (m + 1) * half]
    chosen = meta[1] == step

    @pl.when(chosen)
    def _():
        a_turned[:width] = attn_in[:half].T
        row = lax.broadcasted_iota(jnp.int32, (LEN_ROWS, half), 0)
        own_lens = jnp.where(row == 0, first_len.astype(jnp.float32), second_len.astype(jnp.float32))
        a_turned[width:] = own_lens.astype(a_turned.dtype)
        send_out(a_turned, a_part, sems, 0)

    allowed, distance = pair_masks(
        meta[0] * half, first_len.astype(jnp.float32), second_len.astype(jnp.float32), rows
    )
    mixes = []
    for pair, here in enumerate(pairs):
        parts[pair].wait()
        packed = dot(attn_in, w_qkv[:, here]).astype(jnp.bfloat16)
        packed_here[:, here] = packed
        left, right, mixed = pair_forward(
            pair_tiles(packed, 0), slopes, pair, allowed, distance
        )
        for head, probs in ((2 * pair, left), (2 * pair + 1, right)):
            probs_here[head] = probs
            copies.append(send_out(probs_here.at[head], probs_out.at[head], sems, 3 + head))
        mixes.append(mixed)
    copies.append(send_out(packed_here, packed_out, sems, 1))
    last.wait()
    store_halves(dot(jnp.concatenate(mixes, 1), w_out[...]), theirs, mine)
    flush(copies)

    @pl.when(chosen)
    def _():
        pltpu.make_async_copy(a_turned, a_part, sems.at[0]).wait()


def ffn_fwd_kernel(
    step, m, meta, v_mine, v_other, s_mine, s_other, gain, bias, up_in, down_in,
    x1_out, normed_out, inverse_out, slope_out, c_out, theirs, mine,
    x1_mine, normed_here, inverse_here, slope_here, w_up, w_down, c_turned, sems,
):
    up, down = send_out(up_in, w_up, sems, 5), send_out(down_in, w_down, sems, 6)
    half = v_mine.shape[0]
    middle = both(v_mine, v_other) + both(s_mine, s_other)
    x1_mine[...] = middle[:half]
    normed, inverse = norm_stats(middle)
    normed_here[...] = normed.astype(jnp.bfloat16)
    inverse_here[...] = jnp.broadcast_to(inverse, inverse_here.shape)
    ffn_in = (normed * gain[...] + bias[...]).astype(jnp.bfloat16)
    c_part = c_out.at[:, m * half : (m + 1) * half]
    chosen = meta[1] == step

    @pl.when(chosen)
    def _():
        c_turned[...] = ffn_in[:half].T
        send_out(c_turned, c_part, sems, 3)

    pairs = ((x1_mine, x1_out), (normed_here, normed_out), (inverse_here, inverse_out))
    copies = [send_out(*pair, sems, at) for at, pair in enumerate(pairs)]
    up.wait()
    activated, act_slope = gelu_and_slope(dot(ffn_in, w_up[...]))
    slope_here[...] = act_slope.astype(jnp.bfloat16)
    copies.append(send_out(slope_here, slope_out, sems, 4))
    down.wait()
    store_halves(dot(activated.astype(jnp.bfloat16), w_down[...]), theirs, mine)
    flush(copies)

    @pl.when(chosen)
    def _():
        pltpu.make_async_copy(c_turned, c_part, sems.at[3]).wait()


def ffn_back_kernel(
    g_mine, g_other, down_in, slope_in, up_in, theirs, mine, w_down, slope, w_up, sems
):
    pairs = ((down_in, w_down), (slope_in, slope), (up_in, w_up))
    fetches = [send_out(*pair, sems, at) for at, pair in enumerate(pairs)]

    fetches[0].wait()
    grad_act = dot_nt(jnp.concatenate([g_mine[...], g_other[...]], 0), w_down[...])
    flush(fetches[1:])
    grad_pre = (grad_act * f32(slope)).astype(jnp.bfloat16)
    store_halves(dot_nt(grad_pre, w_up[...]), theirs, mine)


def attn_back_kernel(
    step, m, meta, g_mine, g_other, t_mine, t_other, gain,
    normed_in, inverse_in, w_out_in, packed_in, probs_in, w_qkv_in,
    x1_grad_out, ga_out, norm_grads, theirs, mine,
    normed_here, inverse_here, w_out, packed, probs, w_qkv, x1_grad_mine, ga_mine, sems,
):
    needs = (
        (inverse_in, inverse_here), (normed_in, normed_here), (w_out_in, w_out),
        (packed_in, packed), (probs_in, probs), (w_qkv_in, w_qkv),
    )
    fetches = [send_out(*pair, sems, at) for at, pair in enumerate(needs)]
    heads = probs.shape[0]
    half = ga_mine.shape[0]
    grad_norm = both(t_mine, t_other)
    grad_out = both(g_mine, g_other)
    flush(fetches[:2])
    normed = f32(normed_here)
    inverse = jnp.max(inverse_here[...], -1, keepdims=True)
    grad_mid = grad_out + norm_back(grad_norm, normed, inverse, gain[...])
    x1_grad_mine[...] = grad_mid[:half]
    grad_attn = grad_mid.astype(jnp.bfloat16)
    ga_mine[...] = grad_attn[:half]
    copies = [send_out(x1_grad_mine, x1_grad_out, sems, 6)]
    chosen = meta[1] == step

    @pl.when(chosen)
    def _():
        send_out(ga_mine, ga_out.at[m], sems, 7)

    norm_grads[0:1] = jnp.sum(grad_norm[:half] * normed[:half], 0, keepdims=True)
    norm_grads[1:2] = jnp.sum(grad_norm[:half], 0, keepdims=True)
    flush(fetches[2:5])
    grad_mix = dot_nt(grad_attn, w_out[...]).astype(jnp.bfloat16)
    grad_packed = attention_back(packed[...], grad_mix, lambda head: probs[head], heads)
    fetches[5].wait()
    store_halves(dot_nt(grad_packed, w_qkv[...]), theirs, mine)
    flush(copies)

    @pl.when(chosen)
    def _():
        pltpu.make_async_copy(ga_mine, ga_out.at[m], sems.at[7]).wait()


def input_back(near, far, gain, norm_grads, v_mine, x1_grad_mine):
    normed, inverse = norm_stats(f32(v_mine))
    grad_norm = f32(near) + f32(far)
    norm_grads[0:1] = jnp.sum(grad_norm * normed, 0, keepdims=True)
    norm_grads[1:2] = jnp.sum(grad_norm, 0, keepdims=True)
    return x1_grad_mine[...] + norm_back(grad_norm, normed, inverse, gain[...])


def fetch_skip(here, parts, w_all, sems):
    return [send_out(part, w_all.at[here ^ flip], sems, flip) for flip, part in enumerate(parts)]


def skip_back(rows, w_all, fetches):
    wide = w_all.shape[2]
    out = 0.0
    flush(fetches)
    for at in range(len(fetches)):
        out = out + dot_nt(rows[:, at * wide : (at + 1) * wide], w_all[at])
    return out


def hop_back_kernel(
    m, meta, near, far, gain, v_in, x1_grad_in, *refs
):
    *w_in, joined_out, h_grad, norm_grads, v_mine, x1_grad_mine, w_all, joined_mine, sems = refs
    parts = w_all.shape[0]
    needs = [send_out(v_in.at[m], v_mine, sems, parts), send_out(x1_grad_in, x1_grad_mine, sems, parts + 1)]
    fetches = fetch_skip(meta[3], w_in, w_all, sems)
    flush(needs)
    rounded = input_back(near, far, gain, norm_grads, v_mine, x1_grad_mine).astype(jnp.bfloat16)
    joined_mine[...] = rounded
    copy = send_out(joined_mine, joined_out.at[m], sems, parts + 2)
    h_grad[...] = skip_back(rounded, w_all, fetches).astype(h_grad.dtype)
    copy.wait()


def frames_back_kernel(
    m, meta, near, far, gain, joined_in, v_in, x1_grad_in, *refs
):
    *w_in, out, norm_grads, joined_grad, v_mine, x1_grad_mine, w_all, sems = refs
    parts = w_all.shape[0]
    pairs = ((v_in.at[m], v_mine), (x1_grad_in, x1_grad_mine), (joined_in.at[m], joined_grad))
    needs = [send_out(*pair, sems, parts + at) for at, pair in enumerate(pairs)]
    fetches = fetch_skip(meta[3], w_in, w_all, sems)
    flush(needs)
    grad_in = input_back(near, far, gain, norm_grads, v_mine, x1_grad_mine)
    out[...] = (grad_in + skip_back(joined_grad[...], w_all, fetches)).astype(out.dtype)


def skip_kernel(count, meta, *refs):
    parts, (*w_in, w_all, sems) = refs[:count], refs[count:]
    w_in, outs = w_in[:-count], w_in[-count:]
    wide = w_all.shape[2]
    flush(fetch_skip(meta[3], w_in, w_all, sems))
    for at in range(w_all.shape[0]):
        for rows, out in zip(parts, outs):
            out[:, at * wide : (at + 1) * wide] = dot(rows[...], w_all[at]).astype(out.dtype)


def join_kernel(m, meta, rows, skip_in, *refs):
    *w_in, rows_out, out, w_all, skip_part, sems = refs
    wide = w_all.shape[2]
    fetches = fetch_skip(meta[3], w_in, w_all, sems)
    fetches.append(send_out(skip_in, skip_part, sems, len(fetches) + 1))
    copy = send_out(rows, rows_out.at[m], sems, len(fetches) - 1)
    flush(fetches)
    for at in range(w_all.shape[0]):
        columns = slice(at * wide, (at + 1) * wide)
        product = dot(rows[...], w_all[at]) + skip_part[:, columns].astype(jnp.float32)
        out[:, columns] = product.astype(out.dtype)
    copy.wait()


def place_kernel(valid_of, meta, *refs):
    core, here = meta[0], meta[3]
    micro = refs[0].shape[0]
    blocks, outs = refs[: -2 * micro], refs[-2 * micro :]
    for at in range(micro):
        mine, other = outs[2 * at : 2 * at + 2]
        half, wide = mine.shape[0], blocks[0].shape[2]
        for flip, block in enumerate(blocks):
            columns = pl.ds(pl.multiple_of((here ^ flip) * wide, wide), wide)
            for start, out in ((core * half, mine), ((1 - core) * half, other)):
                start = pl.multiple_of(start, half)
                value = block[at, pl.ds(start, half)]
                if valid_of is not None:
                    row = lax.broadcasted_iota(jnp.int32, (half, wide), 0) + start
                    value = jnp.where(row < valid_of(at), value, jnp.zeros_like(value))
                out[:, columns] = value


def place_seed_kernel(meta, lens, blocks_in, *refs):
    *outs, blocks, sems = refs
    send_out(blocks_in, blocks, sems, 0).wait()
    place_kernel(
        lambda m: lens[m, 0, 0] + lens[m, 0, 1],
        meta,
        *[blocks.at[meta[3] ^ flip] for flip in range(blocks.shape[0])],
        *outs,
    )


def seed_block_kernel(meta, lens, blocks_in, out, blocks, turned, sems):
    @pl.when(meta[1] == 1)
    def _():
        send_out(blocks_in, blocks, sems, 0).wait()
        micro, wide = blocks.shape[1], blocks.shape[3]
        half = turned.shape[1] // micro
        start = pl.multiple_of(meta[0] * half, half)
        row = lax.broadcasted_iota(jnp.int32, (half, wide), 0) + start
        for m in range(micro):
            valid = row < lens[m, 0, 0] + lens[m, 0, 1]
            for at in range(blocks.shape[0]):
                value = blocks[at, m, pl.ds(start, half)]
                value = jnp.where(valid, value, jnp.zeros_like(value))
                turned[at * wide : (at + 1) * wide, m * half : (m + 1) * half] = value.T
        send_out(turned, out, sems, 1).wait()


def hop_block_kernel(meta, *refs):
    *sources, out, turned, sems = refs

    @pl.when(meta[1] == 0)
    def _():
        for m, source in enumerate(sources):
            half = source.shape[0]
            turned[:, m * half : (m + 1) * half] = source[...].T
        send_out(turned, out, sems, 0).wait()


def hand_on_kernel(*refs):
    pass


def copy_kernel(source, out, here, sems):
    send_out(source, here, sems, 0).wait()
    send_out(here, out, sems, 0).wait()


def columns_of(pair, target, sems, at, start=True):
    copies = []
    half = pair[0].shape[2] // 2
    for index in range(pair[0].shape[0]):
        for m in range(2):
            for side_at, part in enumerate(pair):
                block = (index * 2 + m) * 2 + side_at
                source = part.at[index, : target.shape[0], m * half : (m + 1) * half]
                columns = slice(block * half, (block + 1) * half)
                copies.append(
                    pltpu.make_async_copy(source, target.at[:, columns], sems.at[at + len(copies)])
                )
                if start:
                    copies[-1].start()
    return copies


def ffn_weights_kernel(meta, early, early_other, late, late_other, up_turned, w_down, *refs):
    grad_up, grad_down, ffn_in, grad_out, sems = refs[-5:]

    @pl.when(pl.program_id(0) == 0)
    def _():
        first, second = (early, early_other), (late, late_other)
        for at, (norms, grads) in enumerate(((first, second), (second, first))):

            @pl.when(meta[1] == at)
            def _(norms=norms, grads=grads):
                copies = columns_of(norms, ffn_in, sems, 0)
                copies += columns_of(grads, grad_out, sems, len(copies))
                flush(copies)

    activated, act_slope = gelu_and_slope(dot(up_turned[...], ffn_in[...]))
    grad_pre = (dot(w_down[...], grad_out[...]) * act_slope).astype(jnp.bfloat16)
    grad_down[...] = dot_nt(activated.astype(jnp.bfloat16), grad_out[...])
    grad_up[...] = dot_nt(ffn_in[...], grad_pre)


def skip_pick_kernel(meta, *refs):
    *sources, inputs, own, other, inputs_here, grad_here, sems = refs
    for at in range(2):

        @pl.when(meta[1] == at)
        def _(at=at):
            pairs = ((sources[at], inputs_here), (sources[2 + at], grad_here))
            flush([send_out(*pair, sems, i) for i, pair in enumerate(pairs)])

    inputs[...] = inputs_here[...]
    wide = own.shape[2]
    for out, owner in ((own, meta[3]), (other, meta[3] ^ 1)):
        columns = pl.ds(pl.multiple_of(owner * wide, wide), wide)
        out[...] = grad_here[:, :, columns]


def pack_kernel(first, second, out):
    out[: first.shape[0]] = first[...]
    out[first.shape[0] :] = second[...]


def unpack_kernel(source, first, *rows):
    tall, wide = first.shape
    first[...] = f32(source)[:tall]
    each = rows[0].shape[1] // wide
    for at, row in enumerate(rows):
        for part in range(each):
            here = tall + at * each + part
            row[:, part * wide : (part + 1) * wide] = source[here : here + 1].astype(jnp.float32)


def skip_weights_kernel(*refs):
    *parts, out = refs
    count = len(parts) // 2
    total = 0.0
    for rows, grads in zip(parts[:count], parts[count:]):
        for m in range(rows.shape[0]):
            total = total + dot_tn(rows[m], grads[m])
    out[...] = total.astype(out.dtype)


def attn_again_kernel(meta, slopes, mine, other, w_qkv, packed_out, probs_out, mix_out):
    heads, rows = probs_out.shape[1], probs_out.shape[2]
    width = w_qkv.shape[0]
    first_len, second_len = (
        mine[0, width + at : width + at + 1, :1].astype(jnp.float32) for at in range(2)
    )
    allowed, distance = pair_masks(meta[0] * (rows // 2), first_len, second_len, rows)
    frames = jnp.concatenate([mine[0, :width].T, other[0, :width].T], 0)
    packed = dot(frames, w_qkv[...]).astype(jnp.bfloat16)
    packed_out[...] = packed
    for pair in range(heads // 2):
        left, right, mixed = pair_forward(
            pair_tiles(packed, pair), slopes, pair, allowed, distance
        )
        probs_out[0, 2 * pair] = left
        probs_out[0, 2 * pair + 1] = right
        mix_out[2 * HD * pair : 2 * HD * (pair + 1)] = mixed.T


def attn_weights_kernel(
    mine, other, packed, probs, w_out, in_mine, in_other, grad_mine, grad_other, mix_in, *refs
):
    grad_qkv, grad_out, grad_packed, attn_in, grad_all, mix, sems = refs[-7:]
    step = pl.program_id(0)
    rows = probs.shape[2]
    half = rows // 2

    def fetches():
        made = columns_of((in_mine, in_other), attn_in, sems, 1, False)
        for index in range(grad_mine.shape[0]):
            for m in range(2):
                for side_at, part in enumerate((grad_mine, grad_other)):
                    block = (index * 2 + m) * 2 + side_at
                    target = grad_all.at[block * half : (block + 1) * half]
                    made.append(pltpu.make_async_copy(part.at[index, m], target, sems.at[1 + len(made)]))
        made.append(pltpu.make_async_copy(mix_in, mix, sems.at[0]))
        return made

    @pl.when(step == 0)
    def _():
        for copy in fetches():
            copy.start()

    heads = probs.shape[1]
    grad_attn = jnp.concatenate([mine[0, 0], other[0, 0]], 0)
    grad_mix = dot_nt(grad_attn, w_out[...]).astype(jnp.bfloat16)
    here = attention_back(packed[...], grad_mix, lambda head: probs[0, head], heads)
    grad_packed[pl.ds(pl.multiple_of(step * rows, rows), rows)] = here

    @pl.when(step == pl.num_programs(0) - 1)
    def _():
        flush(fetches())
        grad_qkv[...] = dot(attn_in[...], grad_packed[...])
        grad_out[...] = dot(mix[...], grad_all[...])


def shape(dims, kind=jnp.bfloat16):
    return jax.ShapeDtypeStruct(dims, kind)


WHOLE = pl.BlockSpec(memory_space=pltpu.VMEM)
SCALARS = pl.BlockSpec(memory_space=pltpu.SMEM)
FAR = pl.BlockSpec(memory_space=pltpu.HBM)
LATER = pl.BlockSpec(memory_space=pl.ANY)
SMALL = pl.CostEstimate(flops=1, bytes_accessed=1, transcendentals=0)
AGAIN = pl.CostEstimate(flops=8_000_000_000, bytes_accessed=24_000_000, transcendentals=0)
COSTS = [
    pl.CostEstimate(flops=int(part * 1.1e9), bytes_accessed=int(part * 3.6e6), transcendentals=0)
    for part in (11, 4, 4, 4)
]


def constant(dims):
    return pl.BlockSpec(dims, lambda step: (0,) * len(dims))


def in_hbm(value):
    return pltpu.with_memory_space_constraint(value, pltpu.HBM)


def call(
    kernel, outs, scalars, arrays, far_in=(), free_in=(), far_outs=(), scratch=(), hold=(), keep=(), cost=SMALL
):
    count = len(scalars) + len(arrays) + len(far_in) + len(free_in)
    later = count + len(hold)

    def body(*refs):
        kernel(*refs[:count], *refs[later + len(keep) :])

    return list(
        pl.pallas_call(
            body,
            name=getattr(kernel, "func", kernel).__name__,
            out_shape=[*(pltpu.HBM(item.shape, item.dtype) for item in far_outs), *outs],
            in_specs=[SCALARS] * len(scalars)
            + [WHOLE] * len(arrays)
            + [FAR] * len(far_in)
            + [LATER] * (len(free_in) + len(hold))
            + [FAR] * len(keep),
            out_specs=[FAR] * len(far_outs) + [WHOLE] * len(outs),
            scratch_shapes=list(scratch),
            input_output_aliases={later + at: at for at in range(len(keep))},
            compiler_params=pltpu.CompilerParams(vmem_limit_bytes=20 * MIB),
            cost_estimate=cost,
        )(*scalars, *arrays, *map(in_hbm, far_in), *free_in, *hold, *map(in_hbm, keep))
    )


def vmem(item):
    return pltpu.VMEM(item.shape, item.dtype)


def attn_forward(place, scalars, v, gain, bias, w_qkv, w_out, kept, hold, cost):
    half, width = v[0].shape
    rows, wide = 2 * half, w_out.shape[0]
    heads = wide // HD
    buffers = [shape((2, half, width)), shape((width + LEN_ROWS, 2 * half))]
    far = [shape((rows, 3 * wide)), shape((heads, rows, rows))]

    def kernel(*refs):
        count = len(refs) - 12
        v_out, a_out, packed_out, probs_out = refs[count : count + 4]
        attn_fwd_kernel(*place, *refs[:count], packed_out, probs_out, v_out, a_out, *refs[count + 4 :])

    kernel.__name__ = "attn_fwd_kernel"
    return call(
        kernel,
        [shape((half, width)), shape((half, width))],
        scalars,
        [*v, gain, bias],
        far_in=[w_qkv, w_out],
        far_outs=[*buffers, *far],
        scratch=[
            *map(vmem, far), vmem(w_qkv), vmem(w_out), pltpu.VMEM((width + LEN_ROWS, half), jnp.bfloat16),
            pltpu.SemaphoreType.DMA((4 + heads + heads // 2,)),
        ],
        hold=hold,
        keep=kept,
        cost=cost,
    )


def ffn_forward(place, scalars, v, s, gain, bias, w_up, w_down, kept, hold, cost):
    half, width = v[0].shape
    rows, units = 2 * half, w_up.shape[1]
    buffer = shape((width, 2 * half))
    far = [
        shape((half, width), jnp.float32),
        shape((rows, width)),
        shape((rows, LANES), jnp.float32),
        shape((rows, units)),
    ]

    def kernel(*refs):
        count = len(refs) - 15
        c_out, *others = refs[count : count + 5]
        ffn_fwd_kernel(*place, *refs[:count], *others, c_out, *refs[count + 5 :])

    kernel.__name__ = "ffn_fwd_kernel"
    return call(
        kernel,
        [shape((half, width)), shape((half, width))],
        scalars,
        [*v, *s, gain, bias],
        far_in=[w_up, w_down],
        far_outs=[buffer, *far],
        scratch=[
            *map(vmem, far), vmem(w_up), vmem(w_down), pltpu.VMEM((width, half), jnp.bfloat16),
            pltpu.SemaphoreType.DMA((7,)),
        ],
        hold=hold,
        keep=kept,
        cost=cost,
    )


def ffn_backward(g, slope, w_down, w_up, hold, cost):
    half, width = g[0].shape
    return call(
        ffn_back_kernel,
        [shape((half, width)), shape((half, width))],
        [],
        [*g],
        far_in=[w_down, slope, w_up],
        scratch=[vmem(w_down), vmem(slope), vmem(w_up), pltpu.SemaphoreType.DMA((3,))],
        hold=hold,
        cost=cost,
    )


def attn_backward(
    place, scalars, g, t, gain, w_out, w_qkv, normed, inverse, packed, probs, kept, hold, cost
):
    half, width = g[0].shape
    far = [shape((2, half, width)), shape((half, width), jnp.float32)]
    needs = [normed, inverse, w_out, packed, probs, w_qkv]

    def kernel(*refs):
        count = len(refs) - 14
        ga_out, x1_grad_out = refs[count : count + 2]
        attn_back_kernel(*place, *refs[:count], x1_grad_out, ga_out, *refs[count + 2 :])

    kernel.__name__ = "attn_back_kernel"
    return call(
        kernel,
        [shape((2, width), jnp.float32), shape((half, width)), shape((half, width))],
        scalars,
        [*g, *t, gain],
        far_in=needs,
        far_outs=far,
        scratch=[
            *map(vmem, needs), vmem(far[1]), pltpu.VMEM((half, width), jnp.bfloat16),
            pltpu.SemaphoreType.DMA((8,)),
        ],
        hold=hold,
        keep=kept,
        cost=cost,
    )


def ffn_weights(meta, early, late, up_turned, w_down, hold):
    units, width = w_down.shape
    group, _, part = early[0].shape
    rows = 2 * group * part
    wide = min(256, units)
    return pl.pallas_call(
        ffn_weights_kernel,
        name="ffn_weights_kernel",
        grid=(units // wide,),
        in_specs=[
            SCALARS, FAR, FAR, FAR, FAR,
            pl.BlockSpec((wide, width), lambda step: (step, 0)),
            pl.BlockSpec((wide, width), lambda step: (step, 0)),
            *[LATER] * len(hold),
        ],
        out_specs=[
            pl.BlockSpec((width, wide), lambda step: (0, step)),
            pl.BlockSpec((wide, width), lambda step: (step, 0)),
        ],
        out_shape=[shape((width, units), jnp.float32), shape((units, width), jnp.float32)],
        scratch_shapes=[
            pltpu.VMEM((width, rows), jnp.bfloat16),
            pltpu.VMEM((width, rows), jnp.bfloat16),
            pltpu.SemaphoreType.DMA((8 * group,)),
        ],
        compiler_params=pltpu.CompilerParams(vmem_limit_bytes=40 * MIB),
        cost_estimate=pl.CostEstimate(flops=30000000000, bytes_accessed=100000000, transcendentals=0),
    )(meta, *map(in_hbm, (*early, *late, up_turned, w_down)), *hold)


def attn_again(meta, slopes, attn_in, w_qkv, part_at, parts, kept, hold, cost):
    group, tall, part = attn_in[0].shape
    half = part // 2
    rows = 2 * half
    count = 2 * group
    per_call = count // parts
    start = part_at * per_call
    width = w_qkv.shape[0]
    wide = w_qkv.shape[1] // 3
    heads = wide // HD
    outs = [((rows * count, 3 * wide)), (count, heads, rows, rows), (wide, rows * count)]
    piece = pl.BlockSpec(
        (1, tall, half), lambda step: ((start + step) // 2, 0, (start + step) % 2)
    )

    def kernel(*refs):
        attn_again_kernel(*refs[:5], *refs[-3:])

    return pl.pallas_call(
        kernel,
        name="attn_again_kernel",
        grid=(per_call,),
        in_specs=[SCALARS, SCALARS, piece, piece, constant((width, 3 * wide))]
        + [LATER] * len(hold)
        + [FAR] * len(kept),
        out_specs=[
            pl.BlockSpec((rows, 3 * wide), lambda step: (start + step, 0)),
            pl.BlockSpec((1, heads, rows, rows), lambda step: (start + step, 0, 0, 0)),
            pl.BlockSpec((wide, rows), lambda step: (0, start + step)),
        ],
        out_shape=[pltpu.HBM(dims, jnp.bfloat16) for dims in outs],
        input_output_aliases={5 + len(hold) + at: at for at in range(len(kept))},
        compiler_params=pltpu.CompilerParams(vmem_limit_bytes=20 * MIB),
        cost_estimate=cost,
    )(meta, slopes, *map(in_hbm, (*attn_in, w_qkv)), *hold, *map(in_hbm, kept))


def attn_weights(attn_in, grad_attn, packed, probs, mix, w_out, hold):
    wide, width = w_out.shape
    count, heads, rows, _ = probs.shape
    half = rows // 2
    group = count // 2
    piece = pl.BlockSpec((1, 1, half, width), lambda step: (step // 2, step % 2, 0, 0))
    return pl.pallas_call(
        attn_weights_kernel,
        name="attn_weights_kernel",
        grid=(count,),
        in_specs=[
            piece, piece,
            pl.BlockSpec((rows, 3 * wide), lambda step: (step, 0)),
            pl.BlockSpec((1, heads, rows, rows), lambda step: (step, 0, 0, 0)),
            constant((wide, width)), FAR, FAR, FAR, FAR, FAR, *[LATER] * len(hold),
        ],
        out_specs=[constant((width, 3 * wide)), constant((wide, width))],
        out_shape=[shape((width, 3 * wide), jnp.float32), shape((wide, width), jnp.float32)],
        scratch_shapes=[
            pltpu.VMEM((rows * count, 3 * wide), jnp.bfloat16),
            pltpu.VMEM((width, rows * count), jnp.bfloat16),
            pltpu.VMEM((rows * count, width), jnp.bfloat16),
            pltpu.VMEM((wide, rows * count), jnp.bfloat16),
            pltpu.SemaphoreType.DMA((1 + 8 * group,)),
        ],
        compiler_params=pltpu.CompilerParams(vmem_limit_bytes=40 * MIB),
        cost_estimate=SMALL,
    )(*map(in_hbm, (*grad_attn, packed, probs, w_out, *attn_in, *grad_attn, mix)), *hold)


def shards(
    frames,
    cotangent,
    lengths,
    norm1_gain,
    norm1_bias,
    norm2_gain,
    norm2_bias,
    w_qkv,
    w_out,
    w_up,
    w_down,
    w_skip,
):
    first = lax.axis_index("section") == 0
    dp_at = lax.axis_index("dp")
    tensor_at = lax.axis_index("tensor")
    core, chip = tensor_at % 2, tensor_at // 2
    dp_count = lax.axis_size("dp")
    micro, rows, quarter = frames.shape
    half = rows // 2
    w_qkv, w_out, w_up, w_down = w_qkv[0], w_out[0], w_up[0], w_down[0]
    heads = w_qkv.shape[1] // (3 * HD)
    gather_dp = dp_count <= GROUP
    group = dp_count if gather_dp else 1
    section = lax.axis_index("section")
    meta = jnp.stack([core, section, chip, tensor_at, dp_at % group]).astype(jnp.int32)
    scalars = [meta, lengths]

    half_dims = shape((half, norm1_gain.shape[1]))
    pair_dims = shape((micro, *half_dims.shape))
    x1_dims = shape(half_dims.shape, jnp.float32)
    vector = shape((2, norm1_gain.shape[1]), jnp.float32)

    over = x_swap(frames)
    blocks = [frames, core_swap(frames), over, core_swap(over)]
    xs = call(functools.partial(place_kernel, None), [half_dims] * (2 * micro), [meta], blocks)
    xs = [xs[2 * m : 2 * m + 2] for m in range(micro)]
    head_ids = tensor_at * heads + jnp.arange(heads, dtype=jnp.int32)
    slopes = 2.0 ** (-8.0 * (head_ids + 1).astype(jnp.float32) / HEADS)
    up_turned = w_up.T

    w_near = call(
        copy_kernel, [], [], [], far_in=[w_skip[0]], far_outs=[shape(w_skip.shape[1:])],
        scratch=[vmem(w_skip[0]), pltpu.SemaphoreType.DMA((1,))], hold=[over],
    )[0]
    w_over = x_swap(w_near)
    w_blocks = [w_near, core_swap(w_near), w_over, core_swap(w_over)]
    w_scratch = [
        pltpu.VMEM((len(w_blocks), *w_near.shape), w_near.dtype),
        pltpu.SemaphoreType.DMA((len(w_blocks) + 3,)),
    ]
    cot_blocks = lax.all_gather(cotangent, "tensor", axis=0, tiled=False)

    def hand_on(value, after):
        return call(
            hand_on_kernel, [], [], [], far_outs=[shape(value.shape, value.dtype)], keep=[value],
            hold=after,
        )[0]

    def gather_rows(mine):
        return lax.all_gather(mine, "dp", axis=0, tiled=False) if gather_dp else mine[None]

    def all_rows(mine):
        every = gather_rows(mine)
        return every, core_swap(every)

    def forward(step, v, buffers, holds_attn, holds_ffn):
        attn, ffn, near = [], [], []
        keep_attn, keep_ffn = buffers
        for m in range(micro):
            item = attn_forward(
                (step, m), [*scalars, slopes], v[m], norm1_gain, norm1_bias, w_qkv, w_out, keep_attn,
                near[-1:] + holds_attn[m], COSTS[step],
            )
            keep_attn = item[:2]
            attn.append(item[2:])
            near.append(near_sum(*item[4:]))
        sums = [whole_sum(item) for item in near]
        near = []
        for m in range(micro):
            item = ffn_forward(
                (step, m), [meta], v[m], sums[m], norm2_gain, norm2_bias, w_up, w_down, keep_ffn,
                near[-1:] + holds_ffn[m] + attn[-1][2:3], COSTS[step],
            )
            keep_ffn = item[:1]
            ffn.append(item[1:])
            near.append(near_sum(*item[5:]))
        kept = dict(
            v=keep_attn[0],
            packed=[item[0] for item in attn],
            probs=[item[1] for item in attn],
            norm=[item[1:3] for item in ffn],
            slope=[item[3] for item in ffn],
        )
        return [(item[0], part) for item, part in zip(ffn, near)], kept, (keep_attn, keep_ffn)

    def finish(x1, near, far):
        total = x1 + near.astype(jnp.float32) + far.astype(jnp.float32)
        return total.astype(jnp.bfloat16)

    def backward(step, g, kept, buffers, holds, holds_attn=((), ())):
        near, attn = [], []
        keep_attn = buffers
        for m in range(micro):
            item = ffn_backward(g[m], kept["slope"][m], w_down, w_up, near[-1:] + holds[m], COSTS[3 - step])
            near.append(near_sum(*item))
        last = item[0]
        sums = [whole_sum(item) for item in near]
        near = []
        for m in range(micro):
            item = attn_backward(
                (step, m), [meta], g[m], sums[m], norm2_gain, w_out, w_qkv,
                *kept["norm"][m], kept["packed"][m], kept["probs"][m], keep_attn, [*near[-1:], last, *holds_attn[m]],
                COSTS[3 - step],
            )
            keep_attn = item[:1]
            attn.append(item[1:])
            near.append(near_sum(*item[3:]))
        return attn, near, keep_attn

    skip_parts = call(
        functools.partial(skip_kernel, micro), [half_dims] * micro, [meta], [v[0] for v in xs],
        far_in=w_blocks, scratch=w_scratch,
    )
    skip_recv = [section_swap(item) for item in skip_parts]
    outs_a, kept_a, (keep_attn, keep_ffn) = forward(0, xs, ([], []), [[], [w_over, in_hbm(up_turned)]], [[*skip_parts[:1], in_hbm(cot_blocks)], []])
    early = call(
        seed_block_kernel, [], scalars, [], far_in=[cot_blocks], far_outs=[shape(keep_ffn[0].shape)],
        scratch=[vmem(cot_blocks), vmem(keep_ffn[0]), pltpu.SemaphoreType.DMA((2,))], keep=keep_ffn,
    )[0]
    early = all_rows(early)
    h_recv = [section_swap(finish(*item, x_swap(item[1]))) for item in outs_a]
    joined, h_kept = [], []
    for m in range(micro):
        *h_kept, mine = call(
            functools.partial(join_kernel, m), [half_dims], [meta], [h_recv[m]],
            far_in=[skip_recv[m], *w_blocks], far_outs=[pair_dims], keep=h_kept,
            scratch=[w_scratch[0], vmem(half_dims), w_scratch[1]],
        )
        joined.append((mine, core_swap(mine)))
    outs_b, kept_b, (keep_attn, keep_ffn) = forward(1, joined, (keep_attn, []), [[], []], [[], []])
    g_c = call(
        place_seed_kernel, [half_dims] * (2 * micro), scalars, [], far_in=[cot_blocks],
        scratch=[vmem(cot_blocks), pltpu.SemaphoreType.DMA((1,))], hold=[keep_attn[0]],
    )
    g_c = [g_c[2 * m : 2 * m + 2] for m in range(micro)]
    attn_in = all_rows(keep_attn[1])

    attn_c, near_c, keep_back = backward(1, g_c, kept_b, [], [[], [in_hbm(early[0])]])
    hop, joined_own = [], []
    for m in range(micro):
        *joined_own, h_grad, norm_grads = call(
            functools.partial(hop_back_kernel, m), [half_dims, vector], [meta],
            [near_c[m], x_swap(near_c[m]), norm1_gain],
            far_in=[kept_b["v"], attn_c[m][0], *w_blocks], far_outs=[pair_dims], keep=joined_own,
            scratch=[vmem(half_dims), vmem(x1_dims), w_scratch[0], vmem(half_dims), w_scratch[1]],
        )
        hop.append((h_grad, norm_grads))
    g_d = []
    for m in range(micro):
        mine = section_swap(hop[m][0])
        g_d.append((mine, core_swap(mine)))
    def over_dp(total):
        return lax.psum(total.astype(jnp.bfloat16), "dp").astype(jnp.float32)

    late = call(
        hop_block_kernel, [], [meta], [item[0] for item in g_d], far_outs=[shape(keep_ffn[0].shape)],
        scratch=[vmem(keep_ffn[0]), pltpu.SemaphoreType.DMA((1,))], keep=keep_ffn,
    )[0]
    attn_d, near_d, keep_back = backward(
        0, g_d, kept_a, keep_back, [[in_hbm(attn_in[0])], [in_hbm(late)]]
    )

    late = gather_rows(late)
    far_d = [x_swap(item) for item in near_d]
    far_b = [x_swap(item[1]) for item in outs_b]
    joined_recv = section_swap(joined_own[0])
    again = attn_again(meta, slopes, attn_in, w_qkv, 0, 2, [], [attn_d[-1][1]], AGAIN)
    again = attn_again(meta, slopes, attn_in, w_qkv, 1, 2, again, [], AGAIN)
    late = hand_on(late, [in_hbm(again[2])])
    late = late, core_swap(late)
    grad_every = gather_rows(hand_on(keep_back[0], [in_hbm(again[2])]))
    up_total, down_total = ffn_weights(meta, early, late, up_turned, w_down, [])
    columns = shape((micro, half, quarter))
    inputs, own, other = call(
        skip_pick_kernel, [pair_dims, columns, columns], [meta], [],
        far_in=[kept_a["v"], h_kept[0], joined_recv, joined_own[0]],
        scratch=[vmem(pair_dims), vmem(pair_dims), pltpu.SemaphoreType.DMA((2,))], hold=[in_hbm(up_total)],
    )
    skip_total = call(
        skip_weights_kernel, [shape(w_skip.shape[1:])], [], [inputs, core_swap(inputs), own, core_swap(other)]
    )[0]
    last = [
        call(
            functools.partial(frames_back_kernel, m), [half_dims, vector], [meta],
            [near_d[m], far_d[m], norm1_gain],
            far_in=[joined_recv, kept_a["v"], attn_d[m][0], *w_blocks],
            scratch=[vmem(half_dims), vmem(half_dims), vmem(x1_dims), *w_scratch],
            hold=[inputs, far_b[0], far_b[1]],
        )
        for m in range(micro)
    ]
    def choose(early, late):
        return jnp.where(first, early, late)

    norm_grads = choose(
        jnp.concatenate([sum(item[1] for item in last), sum(item[1] for item in attn_d)], 0),
        jnp.concatenate([sum(item[1] for item in hop), sum(item[1] for item in attn_c)], 0),
    )
    norm_grads += core_swap(norm_grads)
    tall = skip_total.shape[0]
    flat = norm_grads.astype(jnp.bfloat16).reshape(-1, quarter)
    packed_sums = call(
        pack_kernel, [shape((tall + flat.shape[0], quarter))], [], [skip_total, flat],
    )[0]
    summed = lax.psum(packed_sums, "dp")
    grad_every = hand_on(grad_every, [item[0] for item in last])
    grad_attn = grad_every, core_swap(grad_every)
    qkv_total, out_total = attn_weights(attn_in, grad_attn, *again, w_out, [in_hbm(up_total)])
    skip_total, *norm_grads = call(
        unpack_kernel,
        [shape((tall, quarter), jnp.float32)] + [shape((1, norm_grads.shape[1]), jnp.float32)] * 4,
        [], [summed], hold=[in_hbm(out_total)],
    )
    if not gather_dp:
        up_total, down_total, qkv_total, out_total = (
            over_dp(item) for item in (up_total, down_total, qkv_total, out_total)
        )

    def own_columns(item):
        return lax.dynamic_slice_in_dim(item, tensor_at * quarter, quarter, 1)

    def other_columns(item):
        return lax.dynamic_slice_in_dim(item, (tensor_at ^ 1) * quarter, quarter, 1)

    pieces = []
    for m in range(micro):
        mine = choose(last[m][0], finish(*outs_b[m], far_b[m]))
        own, other = own_columns(mine), core_swap(other_columns(mine))
        pieces.append(
            jnp.where(core == 0, jnp.concatenate([own, other], 0), jnp.concatenate([other, own], 0))
        )
    return (
        jnp.stack(pieces, 0)[None],
        *norm_grads,
        qkv_total[None],
        out_total[None],
        up_total[None],
        down_total[None],
        skip_total.astype(jnp.float32)[None],
    )


def solution(mesh):
    in_specs = (
        P(None, "dp", "tensor"),
        P(None, "dp", "tensor"),
        P(None, "dp", None),
        P("section", None),
        P("section", None),
        P("section", None),
        P("section", None),
        P("section", None, "tensor"),
        P("section", "tensor", None),
        P("section", None, "tensor"),
        P("section", "tensor", None),
        P("section", None, "tensor"),
    )
    out_specs = (
        P("section", None, "dp", "tensor"),
        P("section", None),
        P("section", None),
        P("section", None),
        P("section", None),
        P("section", None, "tensor"),
        P("section", "tensor", None),
        P("section", None, "tensor"),
        P("section", "tensor", None),
        P("section", None, "tensor"),
    )
    return jax.shard_map(shards, mesh=mesh, in_specs=in_specs, out_specs=out_specs, check_vma=False)
```

```python
import functools

import jax
import jax.numpy as jnp
from jax import lax
from jax.experimental import pallas as pl
from jax.experimental.pallas import tpu as pltpu
from jax.sharding import PartitionSpec as P

HEADS = 16
HD = 64
UTT = 2

epsilon = 1e-05
inv_root_two = 0.7071067811865476
inv_root_two_pi = 0.3989422804014327
MIB = 1 << 20
LANES = 128
LEN_ROWS = 16
GROUP = 4


def core_swap(value):
    count = lax.axis_size("tensor")
    return lax.ppermute(value, "tensor", [(at, at ^ 1) for at in range(count)])


def x_swap(value):
    count = lax.axis_size("tensor")
    return lax.ppermute(value, "tensor", [(at, at ^ 2) for at in range(count)])


def section_swap(value):
    return lax.ppermute(value, "section", [(0, 1), (1, 0)])


def dp_swap(value, bit):
    count = lax.axis_size("dp")
    return lax.ppermute(value, "dp", [(at, at ^ bit) for at in range(count)])


def dp_shift(value, steps):
    count = lax.axis_size("dp")
    return lax.ppermute(value, "dp", [(at, (at + steps) % count) for at in range(count)])


def add_rounded(left, right):
    return (left.astype(jnp.float32) + right.astype(jnp.float32)).astype(jnp.bfloat16)


def near_sum(theirs, mine):
    return add_rounded(mine, core_swap(theirs))


def whole_sum(near):
    half = add_rounded(near, x_swap(near))
    return half, core_swap(half)


def dot(left, right):
    return jnp.dot(left, right, preferred_element_type=jnp.float32)


def dot_nt(left, right):
    return lax.dot_general(
        left, right, (((1,), (1,)), ((), ())), preferred_element_type=jnp.float32
    )


def dot_tn(left, right):
    return lax.dot_general(
        left, right, (((0,), (0,)), ((), ())), preferred_element_type=jnp.float32
    )


def f32(ref):
    return ref[...].astype(jnp.float32)


def both(mine, other):
    return jnp.concatenate([f32(mine), f32(other)], 0)


def norm_stats(inputs):
    average = jnp.mean(inputs, -1, keepdims=True)
    centred = inputs - average
    inverse = lax.rsqrt(jnp.mean(centred * centred, -1, keepdims=True) + epsilon)
    return centred * inverse, inverse


def norm_back(grad_norm, normed, inverse, gain):
    scaled = grad_norm * gain
    return inverse * (
        scaled
        - jnp.mean(scaled, -1, keepdims=True)
        - normed * jnp.mean(scaled * normed, -1, keepdims=True)
    )


def gelu_and_slope(hidden):
    bell = jnp.exp(-0.5 * hidden * hidden)
    at = 1.0 / (1.0 + (0.3275911 * inv_root_two) * jnp.abs(hidden))
    tail = 1.061405429
    for term in (-1.453152027, 1.421413741, -0.284496736, 0.254829592):
        tail = tail * at + term
    tail = (0.5 * at) * tail * bell
    normal_cdf = jnp.where(hidden > 0, 1.0 - tail, tail)
    return hidden * normal_cdf, normal_cdf + hidden * (bell * inv_root_two_pi)


def pair_masks(turn, first_len, second_len, rows):
    def place(axis):
        at = lax.broadcasted_iota(jnp.int32, (rows, rows), axis) + turn
        return jnp.where(at >= rows, at - rows, at).astype(jnp.float32)

    def segment(at):
        return (at >= first_len).astype(jnp.int32) + (at >= first_len + second_len).astype(
            jnp.int32
        )

    queries, keys_all = place(0), place(1)
    return segment(queries) == segment(keys_all), jnp.abs(queries - keys_all)


def swap_sides(tile):
    return jnp.concatenate([tile[:, HD:], tile[:, :HD]], 1)


def side(tile, right):
    lane = lax.broadcasted_iota(jnp.int32, tile.shape, 1)
    return jnp.where((lane >= HD) == bool(right), tile, jnp.zeros_like(tile))


def pair_tiles(packed, pair):
    at = 6 * HD * pair
    return [packed[:, at + 2 * HD * i : at + 2 * HD * (i + 1)] for i in range(3)]


def attention_probs(queries, keys_all, slope, allowed, distance):
    scores = dot_nt(queries * HD ** (-0.5), keys_all)
    scores = jnp.where(allowed, scores - slope * distance, -1e30)
    exp_scores = jnp.exp(scores - jnp.max(scores, -1, keepdims=True))
    return (exp_scores / jnp.sum(exp_scores, -1, keepdims=True)).astype(jnp.bfloat16)


def pair_forward(tiles, slopes, pair, allowed, distance):
    left = attention_probs(
        side(tiles[0], 0), swap_sides(tiles[0]), slopes[2 * pair], allowed, distance
    )
    right = attention_probs(
        side(tiles[1], 1), swap_sides(tiles[2]), slopes[2 * pair + 1], allowed, distance
    )
    mixed = dot(left, side(tiles[1], 0)) + dot(right, side(tiles[2], 1))
    return left, right, mixed.astype(jnp.bfloat16)


def scores_back(probs, grad_mix, values):
    grad_probs = dot_nt(grad_mix, values)
    wide_probs = probs.astype(jnp.float32)
    delta = jnp.sum(wide_probs * grad_probs, -1, keepdims=True)
    return (wide_probs * (grad_probs - delta)).astype(jnp.bfloat16)


def pair_backward(tiles, left, right, grad_mix):
    scale = HD ** (-0.5)
    grad_left, grad_right = side(grad_mix, 0), side(grad_mix, 1)
    back_left = scores_back(left, grad_left, tiles[1])
    back_right = scores_back(right, grad_right, tiles[2])
    turned = [swap_sides(tile) * scale for tile in tiles]
    return [
        item.astype(jnp.bfloat16)
        for item in (
            dot(back_left, side(turned[0], 0)) + dot_tn(back_left, side(turned[0], 1)),
            dot_tn(left, grad_left) + dot(back_right, side(turned[2], 1)),
            dot_tn(back_right, side(turned[1], 0)) + dot_tn(right, grad_right),
        )
    ]


def attention_back(packed, grad_mix, probs_of, heads):
    grads = []
    for pair in range(heads // 2):
        columns = slice(2 * HD * pair, 2 * HD * (pair + 1))
        grads += pair_backward(
            pair_tiles(packed, pair), probs_of(2 * pair), probs_of(2 * pair + 1), grad_mix[:, columns]
        )
    return jnp.concatenate(grads, 1)


def store_halves(partial_sum, theirs, mine):
    half = mine.shape[0]
    mine[...] = partial_sum[:half].astype(mine.dtype)
    theirs[...] = partial_sum[half:].astype(theirs.dtype)


def flush(copies):
    for copy in copies:
        copy.wait()


def send_out(source, target, sems, at):
    copy = pltpu.make_async_copy(source, target, sems.at[at])
    copy.start()
    return copy


def attn_fwd_kernel(
    step, m, meta, lens, slopes, v_mine, v_other, gain, bias, w_qkv_in, w_out_in,
    packed_out, probs_out, v_out, a_out, theirs, mine,
    packed_here, probs_here, w_qkv, w_out, a_turned, sems,
):
    heads, rows, _ = probs_here.shape
    half = v_mine.shape[0]
    first_len, second_len = lens[m, 0, 0], lens[m, 0, 1]
    pairs = [slice(6 * HD * pair, 6 * HD * (pair + 1)) for pair in range(heads // 2)]
    parts = [
        send_out(w_qkv_in.at[:, here], w_qkv.at[:, here], sems, 4 + heads + pair)
        for pair, here in enumerate(pairs)
    ]
    last = send_out(w_out_in, w_out, sems, 3 + heads)
    copies = [send_out(v_mine, v_out.at[m], sems, 2)]
    normed, _ = norm_stats(both(v_mine, v_other))
    attn_in = (normed * gain[...] + bias[...]).astype(jnp.bfloat16)
    width = attn_in.shape[1]
    a_part = a_out.at[:, m * half : (m + 1) * half]
    chosen = meta[1] == step

    @pl.when(chosen)
    def _():
        a_turned[:width] = attn_in[:half].T
        row = lax.broadcasted_iota(jnp.int32, (LEN_ROWS, half), 0)
        own_lens = jnp.where(row == 0, first_len.astype(jnp.float32), second_len.astype(jnp.float32))
        a_turned[width:] = own_lens.astype(a_turned.dtype)
        send_out(a_turned, a_part, sems, 0)

    allowed, distance = pair_masks(
        meta[0] * half, first_len.astype(jnp.float32), second_len.astype(jnp.float32), rows
    )
    mixes = []
    for pair, here in enumerate(pairs):
        parts[pair].wait()
        packed = dot(attn_in, w_qkv[:, here]).astype(jnp.bfloat16)
        packed_here[:, here] = packed
        left, right, mixed = pair_forward(
            pair_tiles(packed, 0), slopes, pair, allowed, distance
        )
        for head, probs in ((2 * pair, left), (2 * pair + 1, right)):
            probs_here[head] = probs
            copies.append(send_out(probs_here.at[head], probs_out.at[head], sems, 3 + head))
        mixes.append(mixed)
    copies.append(send_out(packed_here, packed_out, sems, 1))
    last.wait()
    store_halves(dot(jnp.concatenate(mixes, 1), w_out[...]), theirs, mine)
    flush(copies)

    @pl.when(chosen)
    def _():
        pltpu.make_async_copy(a_turned, a_part, sems.at[0]).wait()


def ffn_fwd_kernel(
    step, m, meta, v_mine, v_other, s_mine, s_other, gain, bias, up_in, down_in,
    x1_out, normed_out, inverse_out, slope_out, c_out, theirs, mine,
    x1_mine, normed_here, inverse_here, slope_here, w_up, w_down, c_turned, sems,
):
    up, down = send_out(up_in, w_up, sems, 5), send_out(down_in, w_down, sems, 6)
    half = v_mine.shape[0]
    middle = both(v_mine, v_other) + both(s_mine, s_other)
    x1_mine[...] = middle[:half]
    normed, inverse = norm_stats(middle)
    normed_here[...] = normed.astype(jnp.bfloat16)
    inverse_here[...] = jnp.broadcast_to(inverse, inverse_here.shape)
    ffn_in = (normed * gain[...] + bias[...]).astype(jnp.bfloat16)
    c_part = c_out.at[:, m * half : (m + 1) * half]
    chosen = meta[1] == step

    @pl.when(chosen)
    def _():
        c_turned[...] = ffn_in[:half].T
        send_out(c_turned, c_part, sems, 3)

    pairs = ((x1_mine, x1_out), (normed_here, normed_out), (inverse_here, inverse_out))
    copies = [send_out(*pair, sems, at) for at, pair in enumerate(pairs)]
    up.wait()
    activated, act_slope = gelu_and_slope(dot(ffn_in, w_up[...]))
    slope_here[...] = act_slope.astype(jnp.bfloat16)
    copies.append(send_out(slope_here, slope_out, sems, 4))
    down.wait()
    store_halves(dot(activated.astype(jnp.bfloat16), w_down[...]), theirs, mine)
    flush(copies)

    @pl.when(chosen)
    def _():
        pltpu.make_async_copy(c_turned, c_part, sems.at[3]).wait()


def ffn_back_kernel(
    g_mine, g_other, down_in, slope_in, up_in, theirs, mine, w_down, slope, w_up, sems
):
    pairs = ((down_in, w_down), (slope_in, slope), (up_in, w_up))
    fetches = [send_out(*pair, sems, at) for at, pair in enumerate(pairs)]

    fetches[0].wait()
    grad_act = dot_nt(jnp.concatenate([g_mine[...], g_other[...]], 0), w_down[...])
    flush(fetches[1:])
    grad_pre = (grad_act * f32(slope)).astype(jnp.bfloat16)
    store_halves(dot_nt(grad_pre, w_up[...]), theirs, mine)


def attn_back_kernel(
    step, m, meta, g_mine, g_other, t_mine, t_other, gain,
    normed_in, inverse_in, w_out_in, packed_in, probs_in, w_qkv_in,
    x1_grad_out, ga_out, norm_grads, theirs, mine,
    normed_here, inverse_here, w_out, packed, probs, w_qkv, x1_grad_mine, ga_mine, sems,
):
    needs = (
        (inverse_in, inverse_here), (normed_in, normed_here), (w_out_in, w_out),
        (packed_in, packed), (probs_in, probs), (w_qkv_in, w_qkv),
    )
    fetches = [send_out(*pair, sems, at) for at, pair in enumerate(needs)]
    heads = probs.shape[0]
    half = ga_mine.shape[0]
    grad_norm = both(t_mine, t_other)
    grad_out = both(g_mine, g_other)
    flush(fetches[:2])
    normed = f32(normed_here)
    inverse = jnp.max(inverse_here[...], -1, keepdims=True)
    grad_mid = grad_out + norm_back(grad_norm, normed, inverse, gain[...])
    x1_grad_mine[...] = grad_mid[:half]
    grad_attn = grad_mid.astype(jnp.bfloat16)
    ga_mine[...] = grad_attn[:half]
    copies = [send_out(x1_grad_mine, x1_grad_out, sems, 6)]
    chosen = meta[1] == step

    @pl.when(chosen)
    def _():
        send_out(ga_mine, ga_out.at[m], sems, 7)

    norm_grads[0:1] = jnp.sum(grad_norm[:half] * normed[:half], 0, keepdims=True)
    norm_grads[1:2] = jnp.sum(grad_norm[:half], 0, keepdims=True)
    flush(fetches[2:5])
    grad_mix = dot_nt(grad_attn, w_out[...]).astype(jnp.bfloat16)
    grad_packed = attention_back(packed[...], grad_mix, lambda head: probs[head], heads)
    fetches[5].wait()
    store_halves(dot_nt(grad_packed, w_qkv[...]), theirs, mine)
    flush(copies)

    @pl.when(chosen)
    def _():
        pltpu.make_async_copy(ga_mine, ga_out.at[m], sems.at[7]).wait()


def input_back(near, far, gain, norm_grads, v_mine, x1_grad_mine):
    normed, inverse = norm_stats(f32(v_mine))
    grad_norm = f32(near) + f32(far)
    norm_grads[0:1] = jnp.sum(grad_norm * normed, 0, keepdims=True)
    norm_grads[1:2] = jnp.sum(grad_norm, 0, keepdims=True)
    return x1_grad_mine[...] + norm_back(grad_norm, normed, inverse, gain[...])


def fetch_skip(here, parts, w_all, sems):
    return [send_out(part, w_all.at[here ^ flip], sems, flip) for flip, part in enumerate(parts)]


def skip_back(rows, w_all, fetches):
    wide = w_all.shape[2]
    out = 0.0
    flush(fetches)
    for at in range(len(fetches)):
        out = out + dot_nt(rows[:, at * wide : (at + 1) * wide], w_all[at])
    return out


def hop_back_kernel(
    m, meta, near, far, gain, v_in, x1_grad_in, *refs
):
    *w_in, joined_out, h_grad, norm_grads, v_mine, x1_grad_mine, w_all, joined_mine, sems = refs
    parts = w_all.shape[0]
    needs = [send_out(v_in.at[m], v_mine, sems, parts), send_out(x1_grad_in, x1_grad_mine, sems, parts + 1)]
    fetches = fetch_skip(meta[3], w_in, w_all, sems)
    flush(needs)
    rounded = input_back(near, far, gain, norm_grads, v_mine, x1_grad_mine).astype(jnp.bfloat16)
    joined_mine[...] = rounded
    copy = send_out(joined_mine, joined_out.at[m], sems, parts + 2)
    h_grad[...] = skip_back(rounded, w_all, fetches).astype(h_grad.dtype)
    copy.wait()


def frames_back_kernel(
    m, meta, near, far, gain, joined_in, v_in, x1_grad_in, *refs
):
    *w_in, out, norm_grads, joined_grad, v_mine, x1_grad_mine, w_all, sems = refs
    parts = w_all.shape[0]
    pairs = ((v_in.at[m], v_mine), (x1_grad_in, x1_grad_mine), (joined_in.at[m], joined_grad))
    needs = [send_out(*pair, sems, parts + at) for at, pair in enumerate(pairs)]
    fetches = fetch_skip(meta[3], w_in, w_all, sems)
    flush(needs)
    grad_in = input_back(near, far, gain, norm_grads, v_mine, x1_grad_mine)
    out[...] = (grad_in + skip_back(joined_grad[...], w_all, fetches)).astype(out.dtype)


def skip_kernel(count, meta, *refs):
    parts, (*w_in, w_all, sems) = refs[:count], refs[count:]
    w_in, outs = w_in[:-count], w_in[-count:]
    wide = w_all.shape[2]
    flush(fetch_skip(meta[3], w_in, w_all, sems))
    for at in range(w_all.shape[0]):
        for rows, out in zip(parts, outs):
            out[:, at * wide : (at + 1) * wide] = dot(rows[...], w_all[at]).astype(out.dtype)


def join_kernel(m, meta, rows, skip_in, *refs):
    *w_in, rows_out, out, w_all, skip_part, sems = refs
    wide = w_all.shape[2]
    fetches = fetch_skip(meta[3], w_in, w_all, sems)
    fetches.append(send_out(skip_in, skip_part, sems, len(fetches) + 1))
    copy = send_out(rows, rows_out.at[m], sems, len(fetches) - 1)
    flush(fetches)
    for at in range(w_all.shape[0]):
        columns = slice(at * wide, (at + 1) * wide)
        product = dot(rows[...], w_all[at]) + skip_part[:, columns].astype(jnp.float32)
        out[:, columns] = product.astype(out.dtype)
    copy.wait()


def place_kernel(valid_of, meta, *refs):
    core, here = meta[0], meta[3]
    micro = refs[0].shape[0]
    blocks, outs = refs[: -2 * micro], refs[-2 * micro :]
    for at in range(micro):
        mine, other = outs[2 * at : 2 * at + 2]
        half, wide = mine.shape[0], blocks[0].shape[2]
        for flip, block in enumerate(blocks):
            columns = pl.ds(pl.multiple_of((here ^ flip) * wide, wide), wide)
            for start, out in ((core * half, mine), ((1 - core) * half, other)):
                start = pl.multiple_of(start, half)
                value = block[at, pl.ds(start, half)]
                if valid_of is not None:
                    row = lax.broadcasted_iota(jnp.int32, (half, wide), 0) + start
                    value = jnp.where(row < valid_of(at), value, jnp.zeros_like(value))
                out[:, columns] = value


def place_seed_kernel(meta, lens, blocks_in, *refs):
    *outs, blocks, sems = refs
    send_out(blocks_in, blocks, sems, 0).wait()
    place_kernel(
        lambda m: lens[m, 0, 0] + lens[m, 0, 1],
        meta,
        *[blocks.at[meta[3] ^ flip] for flip in range(blocks.shape[0])],
        *outs,
    )


def seed_block_kernel(meta, lens, blocks_in, out, blocks, turned, sems):
    @pl.when(meta[1] == 1)
    def _():
        send_out(blocks_in, blocks, sems, 0).wait()
        micro, wide = blocks.shape[1], blocks.shape[3]
        half = turned.shape[1] // micro
        start = pl.multiple_of(meta[0] * half, half)
        row = lax.broadcasted_iota(jnp.int32, (half, wide), 0) + start
        for m in range(micro):
            valid = row < lens[m, 0, 0] + lens[m, 0, 1]
            for at in range(blocks.shape[0]):
                value = blocks[at, m, pl.ds(start, half)]
                value = jnp.where(valid, value, jnp.zeros_like(value))
                turned[at * wide : (at + 1) * wide, m * half : (m + 1) * half] = value.T
        send_out(turned, out, sems, 1).wait()


def hop_block_kernel(meta, *refs):
    *sources, out, turned, sems = refs

    @pl.when(meta[1] == 0)
    def _():
        for m, source in enumerate(sources):
            half = source.shape[0]
            turned[:, m * half : (m + 1) * half] = source[...].T
        send_out(turned, out, sems, 0).wait()


def hand_on_kernel(*refs):
    pass


def copy_kernel(source, out, here, sems):
    send_out(source, here, sems, 0).wait()
    send_out(here, out, sems, 0).wait()


def columns_of(pair, target, sems, at, start=True):
    copies = []
    half = pair[0].shape[2] // 2
    for index in range(pair[0].shape[0]):
        for m in range(2):
            for side_at, part in enumerate(pair):
                block = (index * 2 + m) * 2 + side_at
                source = part.at[index, : target.shape[0], m * half : (m + 1) * half]
                columns = slice(block * half, (block + 1) * half)
                copies.append(
                    pltpu.make_async_copy(source, target.at[:, columns], sems.at[at + len(copies)])
                )
                if start:
                    copies[-1].start()
    return copies


def ffn_weights_kernel(meta, early, early_other, late, late_other, up_turned, w_down, *refs):
    grad_up, grad_down, ffn_in, grad_out, sems = refs[-5:]

    @pl.when(pl.program_id(0) == 0)
    def _():
        first, second = (early, early_other), (late, late_other)
        for at, (norms, grads) in enumerate(((first, second), (second, first))):

            @pl.when(meta[1] == at)
            def _(norms=norms, grads=grads):
                copies = columns_of(norms, ffn_in, sems, 0)
                copies += columns_of(grads, grad_out, sems, len(copies))
                flush(copies)

    activated, act_slope = gelu_and_slope(dot(up_turned[...], ffn_in[...]))
    grad_pre = (dot(w_down[...], grad_out[...]) * act_slope).astype(jnp.bfloat16)
    grad_down[...] = dot_nt(activated.astype(jnp.bfloat16), grad_out[...])
    grad_up[...] = dot_nt(ffn_in[...], grad_pre)


def skip_pick_kernel(meta, *refs):
    *sources, inputs, own, other, inputs_here, grad_here, sems = refs
    for at in range(2):

        @pl.when(meta[1] == at)
        def _(at=at):
            pairs = ((sources[at], inputs_here), (sources[2 + at], grad_here))
            flush([send_out(*pair, sems, i) for i, pair in enumerate(pairs)])

    inputs[...] = inputs_here[...]
    wide = own.shape[2]
    for out, owner in ((own, meta[3]), (other, meta[3] ^ 1)):
        columns = pl.ds(pl.multiple_of(owner * wide, wide), wide)
        out[...] = grad_here[:, :, columns]


def pack_kernel(first, second, out):
    out[: first.shape[0]] = first[...]
    out[first.shape[0] :] = second[...]


def unpack_kernel(source, first, *rows):
    tall, wide = first.shape
    first[...] = f32(source)[:tall]
    each = rows[0].shape[1] // wide
    for at, row in enumerate(rows):
        for part in range(each):
            here = tall + at * each + part
            row[:, part * wide : (part + 1) * wide] = source[here : here + 1].astype(jnp.float32)


def skip_weights_kernel(*refs):
    *parts, out = refs
    count = len(parts) // 2
    total = 0.0
    for rows, grads in zip(parts[:count], parts[count:]):
        for m in range(rows.shape[0]):
            total = total + dot_tn(rows[m], grads[m])
    out[...] = total.astype(out.dtype)


def attn_again_kernel(meta, slopes, mine, other, w_qkv, packed_out, probs_out, mix_out):
    heads, rows = probs_out.shape[1], probs_out.shape[2]
    width = w_qkv.shape[0]
    first_len, second_len = (
        mine[0, width + at : width + at + 1, :1].astype(jnp.float32) for at in range(2)
    )
    allowed, distance = pair_masks(meta[0] * (rows // 2), first_len, second_len, rows)
    frames = jnp.concatenate([mine[0, :width].T, other[0, :width].T], 0)
    packed = dot(frames, w_qkv[...]).astype(jnp.bfloat16)
    packed_out[...] = packed
    for pair in range(heads // 2):
        left, right, mixed = pair_forward(
            pair_tiles(packed, pair), slopes, pair, allowed, distance
        )
        probs_out[0, 2 * pair] = left
        probs_out[0, 2 * pair + 1] = right
        mix_out[2 * HD * pair : 2 * HD * (pair + 1)] = mixed.T


def attn_weights_kernel(
    mine, other, packed, probs, w_out, in_mine, in_other, grad_mine, grad_other, mix_in, *refs
):
    grad_qkv, grad_out, grad_packed, attn_in, grad_all, mix, sems = refs[-7:]
    step = pl.program_id(0)
    rows = probs.shape[2]
    half = rows // 2

    def fetches():
        made = columns_of((in_mine, in_other), attn_in, sems, 1, False)
        for index in range(grad_mine.shape[0]):
            for m in range(2):
                for side_at, part in enumerate((grad_mine, grad_other)):
                    block = (index * 2 + m) * 2 + side_at
                    target = grad_all.at[block * half : (block + 1) * half]
                    made.append(pltpu.make_async_copy(part.at[index, m], target, sems.at[1 + len(made)]))
        made.append(pltpu.make_async_copy(mix_in, mix, sems.at[0]))
        return made

    @pl.when(step == 0)
    def _():
        for copy in fetches():
            copy.start()

    heads = probs.shape[1]
    grad_attn = jnp.concatenate([mine[0, 0], other[0, 0]], 0)
    grad_mix = dot_nt(grad_attn, w_out[...]).astype(jnp.bfloat16)
    here = attention_back(packed[...], grad_mix, lambda head: probs[0, head], heads)
    grad_packed[pl.ds(pl.multiple_of(step * rows, rows), rows)] = here

    @pl.when(step == pl.num_programs(0) - 1)
    def _():
        flush(fetches())
        grad_qkv[...] = dot(attn_in[...], grad_packed[...])
        grad_out[...] = dot(mix[...], grad_all[...])


def shape(dims, kind=jnp.bfloat16):
    return jax.ShapeDtypeStruct(dims, kind)


WHOLE = pl.BlockSpec(memory_space=pltpu.VMEM)
SCALARS = pl.BlockSpec(memory_space=pltpu.SMEM)
FAR = pl.BlockSpec(memory_space=pltpu.HBM)
LATER = pl.BlockSpec(memory_space=pl.ANY)
SMALL = pl.CostEstimate(flops=1, bytes_accessed=1, transcendentals=0)
AGAIN = pl.CostEstimate(flops=8_000_000_000, bytes_accessed=24_000_000, transcendentals=0)
COSTS = [
    pl.CostEstimate(flops=int(part * 1.1e9), bytes_accessed=int(part * 3.6e6), transcendentals=0)
    for part in (11, 4, 4, 3)
]


def constant(dims):
    return pl.BlockSpec(dims, lambda step: (0,) * len(dims))


def in_hbm(value):
    return pltpu.with_memory_space_constraint(value, pltpu.HBM)


def call(
    kernel, outs, scalars, arrays, far_in=(), free_in=(), far_outs=(), scratch=(), hold=(), keep=(), cost=SMALL
):
    count = len(scalars) + len(arrays) + len(far_in) + len(free_in)
    later = count + len(hold)

    def body(*refs):
        kernel(*refs[:count], *refs[later + len(keep) :])

    return list(
        pl.pallas_call(
            body,
            name=getattr(kernel, "func", kernel).__name__,
            out_shape=[*(pltpu.HBM(item.shape, item.dtype) for item in far_outs), *outs],
            in_specs=[SCALARS] * len(scalars)
            + [WHOLE] * len(arrays)
            + [FAR] * len(far_in)
            + [LATER] * (len(free_in) + len(hold))
            + [FAR] * len(keep),
            out_specs=[FAR] * len(far_outs) + [WHOLE] * len(outs),
            scratch_shapes=list(scratch),
            input_output_aliases={later + at: at for at in range(len(keep))},
            compiler_params=pltpu.CompilerParams(vmem_limit_bytes=20 * MIB),
            cost_estimate=cost,
        )(*scalars, *arrays, *map(in_hbm, far_in), *free_in, *hold, *map(in_hbm, keep))
    )


def vmem(item):
    return pltpu.VMEM(item.shape, item.dtype)


def attn_forward(place, scalars, v, gain, bias, w_qkv, w_out, kept, hold, cost):
    half, width = v[0].shape
    rows, wide = 2 * half, w_out.shape[0]
    heads = wide // HD
    buffers = [shape((2, half, width)), shape((width + LEN_ROWS, 2 * half))]
    far = [shape((rows, 3 * wide)), shape((heads, rows, rows))]

    def kernel(*refs):
        count = len(refs) - 12
        v_out, a_out, packed_out, probs_out = refs[count : count + 4]
        attn_fwd_kernel(*place, *refs[:count], packed_out, probs_out, v_out, a_out, *refs[count + 4 :])

    kernel.__name__ = "attn_fwd_kernel"
    return call(
        kernel,
        [shape((half, width)), shape((half, width))],
        scalars,
        [*v, gain, bias],
        far_in=[w_qkv, w_out],
        far_outs=[*buffers, *far],
        scratch=[
            *map(vmem, far), vmem(w_qkv), vmem(w_out), pltpu.VMEM((width + LEN_ROWS, half), jnp.bfloat16),
            pltpu.SemaphoreType.DMA((4 + heads + heads // 2,)),
        ],
        hold=hold,
        keep=kept,
        cost=cost,
    )


def ffn_forward(place, scalars, v, s, gain, bias, w_up, w_down, kept, hold, cost):
    half, width = v[0].shape
    rows, units = 2 * half, w_up.shape[1]
    buffer = shape((width, 2 * half))
    far = [
        shape((half, width), jnp.float32),
        shape((rows, width)),
        shape((rows, LANES), jnp.float32),
        shape((rows, units)),
    ]

    def kernel(*refs):
        count = len(refs) - 15
        c_out, *others = refs[count : count + 5]
        ffn_fwd_kernel(*place, *refs[:count], *others, c_out, *refs[count + 5 :])

    kernel.__name__ = "ffn_fwd_kernel"
    return call(
        kernel,
        [shape((half, width)), shape((half, width))],
        scalars,
        [*v, *s, gain, bias],
        far_in=[w_up, w_down],
        far_outs=[buffer, *far],
        scratch=[
            *map(vmem, far), vmem(w_up), vmem(w_down), pltpu.VMEM((width, half), jnp.bfloat16),
            pltpu.SemaphoreType.DMA((7,)),
        ],
        hold=hold,
        keep=kept,
        cost=cost,
    )


def ffn_backward(g, slope, w_down, w_up, hold, cost):
    half, width = g[0].shape
    return call(
        ffn_back_kernel,
        [shape((half, width)), shape((half, width))],
        [],
        [*g],
        far_in=[w_down, slope, w_up],
        scratch=[vmem(w_down), vmem(slope), vmem(w_up), pltpu.SemaphoreType.DMA((3,))],
        hold=hold,
        cost=cost,
    )


def attn_backward(
    place, scalars, g, t, gain, w_out, w_qkv, normed, inverse, packed, probs, kept, hold, cost
):
    half, width = g[0].shape
    far = [shape((2, half, width)), shape((half, width), jnp.float32)]
    needs = [normed, inverse, w_out, packed, probs, w_qkv]

    def kernel(*refs):
        count = len(refs) - 14
        ga_out, x1_grad_out = refs[count : count + 2]
        attn_back_kernel(*place, *refs[:count], x1_grad_out, ga_out, *refs[count + 2 :])

    kernel.__name__ = "attn_back_kernel"
    return call(
        kernel,
        [shape((2, width), jnp.float32), shape((half, width)), shape((half, width))],
        scalars,
        [*g, *t, gain],
        far_in=needs,
        far_outs=far,
        scratch=[
            *map(vmem, needs), vmem(far[1]), pltpu.VMEM((half, width), jnp.bfloat16),
            pltpu.SemaphoreType.DMA((8,)),
        ],
        hold=hold,
        keep=kept,
        cost=cost,
    )


def ffn_weights(meta, early, late, up_turned, w_down, hold):
    units, width = w_down.shape
    group, _, part = early[0].shape
    rows = 2 * group * part
    wide = min(256, units)
    return pl.pallas_call(
        ffn_weights_kernel,
        name="ffn_weights_kernel",
        grid=(units // wide,),
        in_specs=[
            SCALARS, FAR, FAR, FAR, FAR,
            pl.BlockSpec((wide, width), lambda step: (step, 0)),
            pl.BlockSpec((wide, width), lambda step: (step, 0)),
            *[LATER] * len(hold),
        ],
        out_specs=[
            pl.BlockSpec((width, wide), lambda step: (0, step)),
            pl.BlockSpec((wide, width), lambda step: (step, 0)),
        ],
        out_shape=[shape((width, units), jnp.float32), shape((units, width), jnp.float32)],
        scratch_shapes=[
            pltpu.VMEM((width, rows), jnp.bfloat16),
            pltpu.VMEM((width, rows), jnp.bfloat16),
            pltpu.SemaphoreType.DMA((8 * group,)),
        ],
        compiler_params=pltpu.CompilerParams(vmem_limit_bytes=40 * MIB),
        cost_estimate=pl.CostEstimate(flops=30000000000, bytes_accessed=100000000, transcendentals=0),
    )(meta, *map(in_hbm, (*early, *late, up_turned, w_down)), *hold)


def attn_again(meta, slopes, attn_in, w_qkv, part_at, parts, kept, hold, cost):
    group, tall, part = attn_in[0].shape
    half = part // 2
    rows = 2 * half
    count = 2 * group
    per_call = count // parts
    start = part_at * per_call
    width = w_qkv.shape[0]
    wide = w_qkv.shape[1] // 3
    heads = wide // HD
    outs = [((rows * count, 3 * wide)), (count, heads, rows, rows), (wide, rows * count)]
    piece = pl.BlockSpec(
        (1, tall, half), lambda step: ((start + step) // 2, 0, (start + step) % 2)
    )

    def kernel(*refs):
        attn_again_kernel(*refs[:5], *refs[-3:])

    return pl.pallas_call(
        kernel,
        name="attn_again_kernel",
        grid=(per_call,),
        in_specs=[SCALARS, SCALARS, piece, piece, constant((width, 3 * wide))]
        + [LATER] * len(hold)
        + [FAR] * len(kept),
        out_specs=[
            pl.BlockSpec((rows, 3 * wide), lambda step: (start + step, 0)),
            pl.BlockSpec((1, heads, rows, rows), lambda step: (start + step, 0, 0, 0)),
            pl.BlockSpec((wide, rows), lambda step: (0, start + step)),
        ],
        out_shape=[pltpu.HBM(dims, jnp.bfloat16) for dims in outs],
        input_output_aliases={5 + len(hold) + at: at for at in range(len(kept))},
        compiler_params=pltpu.CompilerParams(vmem_limit_bytes=20 * MIB),
        cost_estimate=cost,
    )(meta, slopes, *map(in_hbm, (*attn_in, w_qkv)), *hold, *map(in_hbm, kept))


def attn_weights(attn_in, grad_attn, packed, probs, mix, w_out, hold):
    wide, width = w_out.shape
    count, heads, rows, _ = probs.shape
    half = rows // 2
    group = count // 2
    piece = pl.BlockSpec((1, 1, half, width), lambda step: (step // 2, step % 2, 0, 0))
    return pl.pallas_call(
        attn_weights_kernel,
        name="attn_weights_kernel",
        grid=(count,),
        in_specs=[
            piece, piece,
            pl.BlockSpec((rows, 3 * wide), lambda step: (step, 0)),
            pl.BlockSpec((1, heads, rows, rows), lambda step: (step, 0, 0, 0)),
            constant((wide, width)), FAR, FAR, FAR, FAR, FAR, *[LATER] * len(hold),
        ],
        out_specs=[constant((width, 3 * wide)), constant((wide, width))],
        out_shape=[shape((width, 3 * wide), jnp.float32), shape((wide, width), jnp.float32)],
        scratch_shapes=[
            pltpu.VMEM((rows * count, 3 * wide), jnp.bfloat16),
            pltpu.VMEM((width, rows * count), jnp.bfloat16),
            pltpu.VMEM((rows * count, width), jnp.bfloat16),
            pltpu.VMEM((wide, rows * count), jnp.bfloat16),
            pltpu.SemaphoreType.DMA((1 + 8 * group,)),
        ],
        compiler_params=pltpu.CompilerParams(vmem_limit_bytes=40 * MIB),
        cost_estimate=SMALL,
    )(*map(in_hbm, (*grad_attn, packed, probs, w_out, *attn_in, *grad_attn, mix)), *hold)


def shards(
    frames,
    cotangent,
    lengths,
    norm1_gain,
    norm1_bias,
    norm2_gain,
    norm2_bias,
    w_qkv,
    w_out,
    w_up,
    w_down,
    w_skip,
):
    first = lax.axis_index("section") == 0
    dp_at = lax.axis_index("dp")
    tensor_at = lax.axis_index("tensor")
    core, chip = tensor_at % 2, tensor_at // 2
    dp_count = lax.axis_size("dp")
    micro, rows, quarter = frames.shape
    half = rows // 2
    w_qkv, w_out, w_up, w_down = w_qkv[0], w_out[0], w_up[0], w_down[0]
    heads = w_qkv.shape[1] // (3 * HD)
    gather_dp = dp_count <= GROUP
    group = dp_count if gather_dp else 1
    section = lax.axis_index("section")
    meta = jnp.stack([core, section, chip, tensor_at, dp_at % group]).astype(jnp.int32)
    scalars = [meta, lengths]

    half_dims = shape((half, norm1_gain.shape[1]))
    pair_dims = shape((micro, *half_dims.shape))
    x1_dims = shape(half_dims.shape, jnp.float32)
    vector = shape((2, norm1_gain.shape[1]), jnp.float32)

    over = x_swap(frames)
    blocks = [frames, core_swap(frames), over, core_swap(over)]
    xs = call(functools.partial(place_kernel, None), [half_dims] * (2 * micro), [meta], blocks)
    xs = [xs[2 * m : 2 * m + 2] for m in range(micro)]
    head_ids = tensor_at * heads + jnp.arange(heads, dtype=jnp.int32)
    slopes = 2.0 ** (-8.0 * (head_ids + 1).astype(jnp.float32) / HEADS)
    up_turned = w_up.T

    w_near = call(
        copy_kernel, [], [], [], far_in=[w_skip[0]], far_outs=[shape(w_skip.shape[1:])],
        scratch=[vmem(w_skip[0]), pltpu.SemaphoreType.DMA((1,))], hold=[over],
    )[0]
    w_over = x_swap(w_near)
    w_blocks = [w_near, core_swap(w_near), w_over, core_swap(w_over)]
    w_scratch = [
        pltpu.VMEM((len(w_blocks), *w_near.shape), w_near.dtype),
        pltpu.SemaphoreType.DMA((len(w_blocks) + 3,)),
    ]
    cot_blocks = lax.all_gather(cotangent, "tensor", axis=0, tiled=False)

    def hand_on(value, after):
        return call(
            hand_on_kernel, [], [], [], far_outs=[shape(value.shape, value.dtype)], keep=[value],
            hold=after,
        )[0]

    def gather_rows(mine):
        return lax.all_gather(mine, "dp", axis=0, tiled=False) if gather_dp else mine[None]

    def all_rows(mine):
        every = gather_rows(mine)
        return every, core_swap(every)

    def forward(step, v, buffers, holds_attn, holds_ffn):
        attn, ffn, near = [], [], []
        keep_attn, keep_ffn = buffers
        for m in range(micro):
            item = attn_forward(
                (step, m), [*scalars, slopes], v[m], norm1_gain, norm1_bias, w_qkv, w_out, keep_attn,
                near[-1:] + holds_attn[m], COSTS[step],
            )
            keep_attn = item[:2]
            attn.append(item[2:])
            near.append(near_sum(*item[4:]))
        sums = [whole_sum(item) for item in near]
        near = []
        for m in range(micro):
            item = ffn_forward(
                (step, m), [meta], v[m], sums[m], norm2_gain, norm2_bias, w_up, w_down, keep_ffn,
                near[-1:] + holds_ffn[m] + attn[-1][2:3], COSTS[step],
            )
            keep_ffn = item[:1]
            ffn.append(item[1:])
            near.append(near_sum(*item[5:]))
        kept = dict(
            v=keep_attn[0],
            packed=[item[0] for item in attn],
            probs=[item[1] for item in attn],
            norm=[item[1:3] for item in ffn],
            slope=[item[3] for item in ffn],
        )
        return [(item[0], part) for item, part in zip(ffn, near)], kept, (keep_attn, keep_ffn)

    def finish(x1, near, far):
        total = x1 + near.astype(jnp.float32) + far.astype(jnp.float32)
        return total.astype(jnp.bfloat16)

    def backward(step, g, kept, buffers, holds, holds_attn=((), ())):
        near, attn = [], []
        keep_attn = buffers
        for m in range(micro):
            item = ffn_backward(g[m], kept["slope"][m], w_down, w_up, near[-1:] + holds[m], COSTS[3 - step])
            near.append(near_sum(*item))
        last = item[0]
        sums = [whole_sum(item) for item in near]
        near = []
        for m in range(micro):
            item = attn_backward(
                (step, m), [meta], g[m], sums[m], norm2_gain, w_out, w_qkv,
                *kept["norm"][m], kept["packed"][m], kept["probs"][m], keep_attn, [*near[-1:], last, *holds_attn[m]],
                COSTS[3 - step],
            )
            keep_attn = item[:1]
            attn.append(item[1:])
            near.append(near_sum(*item[3:]))
        return attn, near, keep_attn

    skip_parts = call(
        functools.partial(skip_kernel, micro), [half_dims] * micro, [meta], [v[0] for v in xs],
        far_in=w_blocks, scratch=w_scratch,
    )
    skip_recv = [section_swap(item) for item in skip_parts]
    outs_a, kept_a, (keep_attn, keep_ffn) = forward(0, xs, ([], []), [[], [w_over, in_hbm(up_turned)]], [[*skip_parts[:1], in_hbm(cot_blocks)], []])
    early = call(
        seed_block_kernel, [], scalars, [], far_in=[cot_blocks], far_outs=[shape(keep_ffn[0].shape)],
        scratch=[vmem(cot_blocks), vmem(keep_ffn[0]), pltpu.SemaphoreType.DMA((2,))], keep=keep_ffn,
    )[0]
    early = all_rows(early)
    h_recv = [section_swap(finish(*item, x_swap(item[1]))) for item in outs_a]
    joined, h_kept = [], []
    for m in range(micro):
        *h_kept, mine = call(
            functools.partial(join_kernel, m), [half_dims], [meta], [h_recv[m]],
            far_in=[skip_recv[m], *w_blocks], far_outs=[pair_dims], keep=h_kept,
            scratch=[w_scratch[0], vmem(half_dims), w_scratch[1]],
        )
        joined.append((mine, core_swap(mine)))
    outs_b, kept_b, (keep_attn, keep_ffn) = forward(1, joined, (keep_attn, []), [[], []], [[], []])
    g_c = call(
        place_seed_kernel, [half_dims] * (2 * micro), scalars, [], far_in=[cot_blocks],
        scratch=[vmem(cot_blocks), pltpu.SemaphoreType.DMA((1,))], hold=[keep_attn[0]],
    )
    g_c = [g_c[2 * m : 2 * m + 2] for m in range(micro)]
    attn_in = all_rows(keep_attn[1])

    attn_c, near_c, keep_back = backward(1, g_c, kept_b, [], [[], [in_hbm(early[0])]])
    hop, joined_own = [], []
    for m in range(micro):
        *joined_own, h_grad, norm_grads = call(
            functools.partial(hop_back_kernel, m), [half_dims, vector], [meta],
            [near_c[m], x_swap(near_c[m]), norm1_gain],
            far_in=[kept_b["v"], attn_c[m][0], *w_blocks], far_outs=[pair_dims], keep=joined_own,
            scratch=[vmem(half_dims), vmem(x1_dims), w_scratch[0], vmem(half_dims), w_scratch[1]],
        )
        hop.append((h_grad, norm_grads))
    g_d = []
    for m in range(micro):
        mine = section_swap(hop[m][0])
        g_d.append((mine, core_swap(mine)))
    def over_dp(total):
        return lax.psum(total.astype(jnp.bfloat16), "dp").astype(jnp.float32)

    late = call(
        hop_block_kernel, [], [meta], [item[0] for item in g_d], far_outs=[shape(keep_ffn[0].shape)],
        scratch=[vmem(keep_ffn[0]), pltpu.SemaphoreType.DMA((1,))], keep=keep_ffn,
    )[0]
    attn_d, near_d, keep_back = backward(
        0, g_d, kept_a, keep_back, [[in_hbm(attn_in[0])], [in_hbm(late)]]
    )

    late = gather_rows(late)
    far_d = [x_swap(item) for item in near_d]
    far_b = [x_swap(item[1]) for item in outs_b]
    joined_recv = section_swap(joined_own[0])
    again = attn_again(meta, slopes, attn_in, w_qkv, 0, 2, [], [attn_d[-1][1]], AGAIN)
    again = attn_again(meta, slopes, attn_in, w_qkv, 1, 2, again, [], AGAIN)
    late = hand_on(late, [in_hbm(again[2])])
    late = late, core_swap(late)
    grad_every = gather_rows(hand_on(keep_back[0], [in_hbm(again[2])]))
    up_total, down_total = ffn_weights(meta, early, late, up_turned, w_down, [])
    columns = shape((micro, half, quarter))
    inputs, own, other = call(
        skip_pick_kernel, [pair_dims, columns, columns], [meta], [],
        far_in=[kept_a["v"], h_kept[0], joined_recv, joined_own[0]],
        scratch=[vmem(pair_dims), vmem(pair_dims), pltpu.SemaphoreType.DMA((2,))], hold=[in_hbm(up_total)],
    )
    skip_total = call(
        skip_weights_kernel, [shape(w_skip.shape[1:])], [], [inputs, core_swap(inputs), own, core_swap(other)]
    )[0]
    last = [
        call(
            functools.partial(frames_back_kernel, m), [half_dims, vector], [meta],
            [near_d[m], far_d[m], norm1_gain],
            far_in=[joined_recv, kept_a["v"], attn_d[m][0], *w_blocks],
            scratch=[vmem(half_dims), vmem(half_dims), vmem(x1_dims), *w_scratch],
            hold=[inputs, far_b[0], far_b[1]],
        )
        for m in range(micro)
    ]
    def choose(early, late):
        return jnp.where(first, early, late)

    norm_grads = choose(
        jnp.concatenate([sum(item[1] for item in last), sum(item[1] for item in attn_d)], 0),
        jnp.concatenate([sum(item[1] for item in hop), sum(item[1] for item in attn_c)], 0),
    )
    norm_grads += core_swap(norm_grads)
    tall = skip_total.shape[0]
    flat = norm_grads.astype(jnp.bfloat16).reshape(-1, quarter)
    packed_sums = call(
        pack_kernel, [shape((tall + flat.shape[0], quarter))], [], [skip_total, flat],
    )[0]
    summed = lax.psum(packed_sums, "dp")
    grad_every = hand_on(grad_every, [item[0] for item in last])
    grad_attn = grad_every, core_swap(grad_every)
    qkv_total, out_total = attn_weights(attn_in, grad_attn, *again, w_out, [in_hbm(up_total)])
    skip_total, *norm_grads = call(
        unpack_kernel,
        [shape((tall, quarter), jnp.float32)] + [shape((1, norm_grads.shape[1]), jnp.float32)] * 4,
        [], [summed], hold=[in_hbm(out_total)],
    )
    if not gather_dp:
        up_total, down_total, qkv_total, out_total = (
            over_dp(item) for item in (up_total, down_total, qkv_total, out_total)
        )

    def own_columns(item):
        return lax.dynamic_slice_in_dim(item, tensor_at * quarter, quarter, 1)

    def other_columns(item):
        return lax.dynamic_slice_in_dim(item, (tensor_at ^ 1) * quarter, quarter, 1)

    pieces = []
    for m in range(micro):
        mine = choose(last[m][0], finish(*outs_b[m], far_b[m]))
        own, other = own_columns(mine), core_swap(other_columns(mine))
        pieces.append(
            jnp.where(core == 0, jnp.concatenate([own, other], 0), jnp.concatenate([other, own], 0))
        )
    return (
        jnp.stack(pieces, 0)[None],
        *norm_grads,
        qkv_total[None],
        out_total[None],
        up_total[None],
        down_total[None],
        skip_total.astype(jnp.float32)[None],
    )


def solution(mesh):
    in_specs = (
        P(None, "dp", "tensor"),
        P(None, "dp", "tensor"),
        P(None, "dp", None),
        P("section", None),
        P("section", None),
        P("section", None),
        P("section", None),
        P("section", None, "tensor"),
        P("section", "tensor", None),
        P("section", None, "tensor"),
        P("section", "tensor", None),
        P("section", None, "tensor"),
    )
    out_specs = (
        P("section", None, "dp", "tensor"),
        P("section", None),
        P("section", None),
        P("section", None),
        P("section", None),
        P("section", None, "tensor"),
        P("section", "tensor", None),
        P("section", None, "tensor"),
        P("section", "tensor", None),
        P("section", None, "tensor"),
    )
    return jax.shard_map(shards, mesh=mesh, in_specs=in_specs, out_specs=out_specs, check_vma=False)
```
